128 devices in a mesh: fsdp: 16 (over z, x), ctx: 8 (over y, core).
Axes of the slice: x: 4, y: 4, z: 4, core: 2. Of those that a mesh axis runs over, the one named last changes fastest.
Arguments:
- inputs: bfloat16 [16, 1024, 1024], P('fsdp', 'ctx'), may hold values from -6 to 6
- mix_gain: bfloat16 [1024], P(('fsdp', 'ctx')), may hold values from 0.099609375 to 1.8984375
- in_proj: bfloat16 [1024, 3072], P(('fsdp', 'ctx')), may hold values from -0.1875 to 0.1875
- conv_kernel: bfloat16 [3, 1024], P(None, ('fsdp', 'ctx')), may hold values from -3 to 3
- out_proj: bfloat16 [1024, 1024], P(('fsdp', 'ctx')), may hold values from -0.1875 to 0.1875
- ffn_gain: bfloat16 [1024], P(('fsdp', 'ctx')), may hold values from 0.099609375 to 1.8984375
- gate_proj: bfloat16 [1024, 4608], P('fsdp', 'ctx'), may hold values from -0.1875 to 0.1875
- up_proj: bfloat16 [1024, 4608], P('fsdp', 'ctx'), may hold values from -0.1875 to 0.1875
- down_proj: bfloat16 [4608, 1024], P('ctx', 'fsdp'), may hold values from -0.09375 to 0.09375
- cotangent: bfloat16 [16, 1024, 1024], P('fsdp', 'ctx'), may hold values from -6 to 6
Outputs:
- block_out: bfloat16 [16, 1024, 1024], P('fsdp', 'ctx')
- grad_inputs: float32 [16, 1024, 1024], P('fsdp', 'ctx')
- grad_mix_gain: float32 [1024], P(('fsdp', 'ctx'))
- grad_in_proj: float32 [1024, 3072], P(('fsdp', 'ctx'))
- grad_conv_kernel: float32 [3, 1024], P(None, ('fsdp', 'ctx'))
- grad_out_proj: float32 [1024, 1024], P(('fsdp', 'ctx'))
- grad_ffn_gain: float32 [1024], P(('fsdp', 'ctx'))
- grad_gate_proj: float32 [1024, 4608], P('fsdp', 'ctx')
- grad_up_proj: float32 [1024, 4608], P('fsdp', 'ctx')
- grad_down_proj: float32 [4608, 1024], P('ctx', 'fsdp')
The draws below stay inside these ranges and needn't reach their ends.
All inputs are finite; a program needn't handle non-finite values.
Results may differ from the reference program's by a relative error of at most 0.018.
Values may be sent and summed in bfloat16 or wider, within the bound.
A program may use at most 192 MiB of HBM per device.

```python
import jax
import jax.numpy as jnp
from jax import lax

D = 1024
FF = 4608
LENGTH = 1024
SEQS = 16


def steps_of(stream_key, shape, shards, smallest, largest):
    level = 1.0
    for dim, parts in shards:
        steps = jax.random.uniform(jax.random.fold_in(jax.random.fold_in(stream_key, 6), dim), (parts,), jnp.float32, smallest / len(shards), largest / len(shards))
        level = level * jnp.repeat(jnp.exp(steps), shape[dim] // parts).reshape((-1,) + (1,) * (len(shape) - 1 - dim))
    return level


def gaussian(rng, extent, scale, limit, pieces=(), kind=jnp.bfloat16):
    level = steps_of(rng, extent, pieces, -0.22, 0.18) if pieces else 1.0
    entries = jax.random.normal(rng, extent, jnp.float32) * scale * level
    return jnp.minimum(jnp.maximum(entries, -limit), limit).astype(kind)


def setup_inputs(seed: int = 0) -> dict:
    seeds = jax.random.split(jax.random.key(seed), 11)
    return {
        "inputs": gaussian(seeds[0], (SEQS, LENGTH, D), 1.0, 6.0, ((0, 16), (1, 8))),
        "mix_gain": jnp.clip(1.0 + 0.18 * jax.random.normal(seeds[1], (D,), jnp.float32), 0.099609375, 1.8984375).astype(jnp.bfloat16),
        "in_proj": gaussian(seeds[2], (D, 3 * D), D ** -0.5, 0.1875, ((0, 128),)),
        "conv_kernel": gaussian(seeds[3], (3, D), 0.6, 3.0, ((1, 128),)),
        "out_proj": gaussian(seeds[4], (D, D), D ** -0.5, 0.1875, ((0, 128),)),
        "ffn_gain": jnp.clip(1.0 + 0.18 * jax.random.normal(seeds[5], (D,), jnp.float32), 0.099609375, 1.8984375).astype(jnp.bfloat16),
        "gate_proj": gaussian(seeds[6], (D, FF), D ** -0.5, 0.1875, ((0, 16), (1, 8))),
        "up_proj": gaussian(seeds[7], (D, FF), D ** -0.5, 0.1875, ((0, 16), (1, 8))),
        "down_proj": gaussian(seeds[8], (FF, D), FF ** -0.5, 0.09375, ((0, 8), (1, 16))),
        "cotangent": gaussian(seeds[9], (SEQS, LENGTH, D), 1.0, 6.0, ((0, 16), (1, 8))),
    }


@jax.custom_vjp
def low(v):
    return lax.optimization_barrier(v.astype(jnp.bfloat16)).astype(jnp.float32)

@jax.custom_vjp
def low_back(v):
    return v

def low_keep(v):
    return (low(v), None)

def low_pass(kept, grad):
    return (grad,)

def back_keep(v):
    return (v, None)

def back_low(kept, grad):
    return (low(grad),)
low.defvjp(low_keep, low_pass)
low_back.defvjp(back_keep, back_low)
epsilon = 1e-05

def product(left, right):
    return jnp.dot(left, right, precision=lax.Precision.HIGHEST, preferred_element_type=jnp.float32)

def rms_normed(values):
    return values * lax.rsqrt(lax.optimization_barrier(jnp.mean(values * values, axis=-1, keepdims=True)) + epsilon)

def forward(sequence, mix_gain, in_proj, conv_kernel, out_proj, ffn_gain, gate_proj, up_proj, down_proj):
    width = sequence.shape[-1]
    lifted = low(rms_normed(sequence) * mix_gain)
    projected = low_back(product(lifted, in_proj))
    b_part = projected[:, :width]
    c_part = projected[:, width:2 * width]
    x_part = projected[:, 2 * width:]
    carried = low(b_part * x_part)
    padded = jnp.concatenate([jnp.zeros((2, width), jnp.float32), carried], 0)
    mixed = conv_kernel[0] * padded[:-2] + conv_kernel[1] * padded[1:-1] + conv_kernel[2] * padded[2:]
    gated = low(c_part * mixed)
    middle = sequence + low_back(product(gated, out_proj))
    second_in = low(rms_normed(middle) * ffn_gain)
    gating = low_back(product(second_in, gate_proj))
    upward = low_back(product(second_in, up_proj))
    hidden = low(jax.nn.silu(gating) * upward)
    return middle + product(hidden, down_proj)

def reference(inputs, mix_gain, in_proj, conv_kernel, out_proj, ffn_gain, gate_proj, up_proj, down_proj, cotangent):
    weights = tuple((weight.astype(jnp.float32) for weight in (mix_gain, in_proj, conv_kernel, out_proj, ffn_gain, gate_proj, up_proj, down_proj)))
    initial = tuple((jnp.zeros_like(weight) for weight in weights))

    def advance(totals, element):
        sequence, gradient = element
        result, pullback = jax.vjp(forward, sequence.astype(jnp.float32), *weights)
        gradients = pullback(gradient.astype(jnp.float32))
        totals = tuple((total + part for total, part in zip(totals, gradients[1:])))
        return (totals, (result.astype(jnp.bfloat16), gradients[0]))
    totals, (outputs, grad_inputs) = lax.scan(advance, initial, (inputs, cotangent))
    return (outputs, grad_inputs, totals[0], totals[1], totals[2], totals[3], totals[4], totals[5], totals[6], totals[7])
```

```python
import jax
import jax.numpy as jnp
from jax import lax
from jax.experimental import pallas as pl
from jax.experimental.pallas import tpu as pltpu
from jax.sharding import PartitionSpec as P

epsilon = 1e-05
f32 = jnp.float32
bf16 = jnp.bfloat16
MESH = pl.DeviceIdType.MESH

GU = 1152
FFL = 1792
HID = 640
CR = 80
CL = 512


def mm(a, b):
    return lax.dot_general(a, b, (((1,), (0,)), ((), ())), preferred_element_type=f32)


def mt(a, b):
    return lax.dot_general(a, b, (((1,), (1,)), ((), ())), preferred_element_type=f32)


def tm(a, b):
    return lax.dot_general(a, b, (((0,), (0,)), ((), ())), preferred_element_type=f32)


def add_into(ref, *others):
    total = ref[...].astype(f32)
    for other in others:
        total = total + other[...].astype(f32)
    ref[...] = total.astype(ref.dtype)


class Link:
    def __init__(self, send_sems, recv_sems):
        self.send_sems, self.recv_sems = send_sems, recv_sems
        self.used = 0
        self.started = []

    def reserve(self, count):
        first = self.used
        self.used += count
        return first

    def copy(self, src, dst, device, slot):
        return pltpu.make_async_remote_copy(
            src_ref=src,
            dst_ref=dst,
            send_sem=self.send_sems.at[slot],
            recv_sem=self.recv_sems.at[slot],
            device_id=device,
            device_id_type=MESH,
        )

    def send(self, src, dst, device):
        slot = self.reserve(1)
        self.copy(src, dst, device, slot).start()
        self.started.append((src, device, slot))
        return (device, slot)

    def landed(self, handle, ref):
        device, slot = handle
        self.copy(ref, ref, device, slot).wait_recv()

    def drain(self):
        for src, device, slot in self.started:
            self.copy(src, src, device, slot).wait_send()


def ring(value, step):
    return lax.rem(value + step, 4)


class RingGather:
    def __init__(self, link, view, me, plus, minus):
        self.link, self.view, self.me, self.plus, self.minus = link, view, me, plus, minus

    def start(self):
        own = self.view(self.me, None)
        self.hp = self.link.send(own, own, self.plus)
        self.hm = self.link.send(own, own, self.minus)

    def forward(self):
        left, right = ring(self.me, 3), ring(self.me, 1)
        self.link.landed(self.hp, self.view(left, None))
        part = self.view(left, 0)
        self.fp = self.link.send(part, part, self.plus)
        self.link.landed(self.hm, self.view(right, None))
        part = self.view(right, 1)
        self.fm = self.link.send(part, part, self.minus)

    def finish(self):
        far = ring(self.me, 2)
        self.link.landed(self.fp, self.view(far, 0))
        self.link.landed(self.fm, self.view(far, 1))


class RingScatter:
    def __init__(self, link, view, me, plus, minus, r1a, r1b, r2a, r2b):
        self.link, self.view, self.me, self.plus, self.minus = link, view, me, plus, minus
        self.r1a, self.r1b, self.r2a, self.r2b = r1a, r1b, r2a, r2b

    def start(self):
        far = ring(self.me, 2)
        self.h1a = self.link.send(self.view(far, 0), self.r1a, self.plus)
        self.h1b = self.link.send(self.view(far, 1), self.r1b, self.minus)

    def middle(self):
        left, right = ring(self.me, 3), ring(self.me, 1)
        self.link.landed(self.h1a, self.r1a)
        add_into(self.view(right, 0), self.r1a)
        self.h2a = self.link.send(self.view(right, None), self.r2a, self.plus)
        self.link.landed(self.h1b, self.r1b)
        add_into(self.view(left, 1), self.r1b)
        self.h2b = self.link.send(self.view(left, None), self.r2b, self.minus)

    def finish(self):
        self.link.landed(self.h2a, self.r2a)
        self.link.landed(self.h2b, self.r2b)
        add_into(self.view(self.me, None), self.r2a, self.r2b)


class CtxGather:
    def __init__(self, link, buf, y, core, plus, minus, other):
        self.link, self.buf, self.y, self.core = link, buf, y, core
        self.plus, self.minus, self.other = plus, minus, other

    def half(self, which, part):
        return self.buf.at[which, self.core, pl.ds(64 * part, 64)]

    def start(self):
        own = self.buf.at[self.y, self.core]
        self.hp = self.link.send(own, own, self.plus)
        self.hm = self.link.send(own, own, self.minus)
        self.ho = [self.link.send(own, own, self.other)]

    def forward(self):
        left, right = ring(self.y, 3), ring(self.y, 1)
        block = self.buf.at[left, self.core]
        self.link.landed(self.hp, block)
        self.fp = self.link.send(self.half(left, 0), self.half(left, 0), self.plus)
        self.ho.append(self.link.send(block, block, self.other))
        block = self.buf.at[right, self.core]
        self.link.landed(self.hm, block)
        self.fm = self.link.send(self.half(right, 1), self.half(right, 1), self.minus)
        self.ho.append(self.link.send(block, block, self.other))

    def across(self):
        far = ring(self.y, 2)
        self.link.landed(self.fp, self.half(far, 0))
        self.link.landed(self.fm, self.half(far, 1))
        block = self.buf.at[far, self.core]
        self.ho.append(self.link.send(block, block, self.other))

    def finish(self):
        for handle, step in zip(self.ho, (0, 3, 1, 2)):
            self.link.landed(handle, self.buf.at[ring(self.y, step), 1 - self.core])


class CtxScatter:
    def __init__(self, link, part, rb, r1, r2, y, core, plus, minus, other):
        self.link, self.part, self.rb, self.r1, self.r2 = link, part, rb, r1, r2
        self.y, self.core = y, core
        self.plus, self.minus, self.other = plus, minus, other
        self.first = link.reserve(4)

    def group(self, step):
        return lax.rem(self.y + 2 + step + step // 2 + 2 * (step // 3), 4)

    def cross(self, step):
        g = self.group(step)
        self.link.copy(
            self.part.at[g, 1 - self.core], self.rb.at[g], self.other, self.first + step
        ).start()

    def crossed(self, g, step):
        ref = self.rb.at[g]
        self.link.copy(ref, ref, self.other, self.first + step).wait_recv()

    def start(self):
        far = ring(self.y, 2)
        self.crossed(far, 0)
        block = self.part.at[far, self.core]
        add_into(block, self.rb.at[far])
        self.h1a = self.link.send(block.at[pl.ds(0, 64)], self.r1.at[0], self.plus)
        self.h1b = self.link.send(block.at[pl.ds(64, 64)], self.r1.at[1], self.minus)

    def middle(self):
        left, right = ring(self.y, 3), ring(self.y, 1)
        self.crossed(left, 1)
        self.crossed(right, 2)
        block = self.part.at[right, self.core]
        self.link.landed(self.h1a, self.r1.at[0])
        add_into(block.at[pl.ds(0, 64)], self.rb.at[right, pl.ds(0, 64)], self.r1.at[0])
        add_into(block.at[pl.ds(64, 64)], self.rb.at[right, pl.ds(64, 64)])
        self.h2a = self.link.send(block, self.r2.at[0], self.plus)
        block = self.part.at[left, self.core]
        self.link.landed(self.h1b, self.r1.at[1])
        add_into(block.at[pl.ds(0, 64)], self.rb.at[left, pl.ds(0, 64)])
        add_into(block.at[pl.ds(64, 64)], self.rb.at[left, pl.ds(64, 64)], self.r1.at[1])
        self.h2b = self.link.send(block, self.r2.at[1], self.minus)

    def finish(self):
        self.crossed(self.y, 3)
        self.link.landed(self.h2a, self.r2.at[0])
        self.link.landed(self.h2b, self.r2.at[1])
        return (
            self.part[self.y, self.core].astype(f32)
            + self.rb[self.y].astype(f32)
            + self.r2[0].astype(f32)
            + self.r2[1].astype(f32)
        )

    def drain(self):
        for step in range(4):
            g = self.group(step)
            src = self.part.at[g, 1 - self.core]
            self.link.copy(src, src, self.other, self.first + step).wait_send()


def block_kernel(
    x_ref,
    cot_ref,
    wff_ref,
    win_ref,
    wout_ref,
    pack_ref,
    out_ref,
    gin_ref,
    gff_ref,
    gwin_ref,
    gwout_ref,
    gpack_ref,
    send_sems,
    recv_sems,
    xg,
    cotg,
    h2g,
    dg,
    wf,
    wc,
    pre_in,
    pre_pack,
    w_in,
    w_out,
    h1g,
    scale_g,
    proj,
    bx_pad,
    z_buf,
    y_buf,
    hid_buf,
    dgu_buf,
    dz_pad,
    dp_buf,
    mix_acc,
    rs_part,
    rs_rb,
    rs_r1,
    rs_r2,
    gf,
    gc,
    gf_a1,
    gf_a2,
    gf_b1,
    gf_b2,
    gf_a3,
    gf_a4,
    gf_b3,
    gf_b4,
    gc_a1,
    gc_a2,
    gc_b1,
    gc_b2,
    gc_a3,
    gc_a4,
    gc_b3,
    gc_b4,
    post_send,
    post_in,
    post_own,
    post_pack,
):
    f = lax.axis_index("fsdp")
    c = lax.axis_index("ctx")
    z, x = f // 4, lax.rem(f, 4)
    y, core = c // 2, lax.rem(c, 2)
    y_plus, y_minus = (f, ring(y, 1) * 2 + core), (f, ring(y, 3) * 2 + core)
    other = (f, y * 2 + 1 - core)
    x_plus, x_minus = (z * 4 + ring(x, 1), c), (z * 4 + ring(x, 3), c)
    z_plus, z_minus = (ring(z, 1) * 4 + x, c), (ring(z, 3) * 4 + x, c)
    mates = [(f, lax.rem(c + step, 8)) for step in range(1, 8)]

    barrier = pltpu.get_barrier_semaphore()
    for device in mates + [x_plus, x_minus, z_plus, z_minus]:
        pl.semaphore_signal(barrier, inc=1, device_id=device, device_id_type=MESH)
    pl.semaphore_wait(barrier, 11)

    link = Link(send_sems, recv_sems)

    def ctx_gather(buf):
        return CtxGather(link, buf, y, core, y_plus, y_minus, other)

    def ctx_scatter(n):
        return CtxScatter(
            link, rs_part.at[n], rs_rb.at[n], rs_r1.at[n], rs_r2.at[n],
            y, core, y_plus, y_minus, other,
        )

    def weight_gather(buf, half, low):
        rest = buf.shape[3] - half
        rows = buf.shape[2]
        a, b = pl.ds(0, half), pl.ds(half, rest)

        def rows_of(part):
            return pl.ds(0, rows) if part is None else (pl.ds(0, low), pl.ds(low, rows - low))[part]

        def pair(part):
            return pl.ds(0, 4) if part is None else pl.ds(2 * part, 2)

        return (
            RingGather(link, lambda i, p: buf.at[z, i, rows_of(p), a], x, x_plus, x_minus),
            RingGather(link, lambda i, p: buf.at[i, x, rows_of(p), b], z, z_plus, z_minus),
            RingGather(link, lambda i, p: buf.at[i, pair(p), :, a], z, z_plus, z_minus),
            RingGather(link, lambda i, p: buf.at[pair(p), i, :, b], x, x_plus, x_minus),
        )

    def weight_scatter(buf, half, low, a1, a2, b1, b2, a3, a4, b3, b4):
        rest = buf.shape[3] - half
        rows = buf.shape[2]
        a, b = pl.ds(0, half), pl.ds(half, rest)

        def rows_of(part):
            return pl.ds(0, rows) if part is None else (pl.ds(0, low), pl.ds(low, rows - low))[part]

        def pair(part):
            return pl.ds(0, 4) if part is None else pl.ds(2 * part, 2)

        cut = (pl.ds(0, low), pl.ds(low, rows - low))
        return (
            RingScatter(link, lambda i, p: buf.at[i, pair(p), :, a], z, z_plus, z_minus,
                        a1.at[0], a1.at[1], a2.at[0], a2.at[1]),
            RingScatter(link, lambda i, p: buf.at[pair(p), i, :, b], x, x_plus, x_minus,
                        b1.at[0], b1.at[1], b2.at[0], b2.at[1]),
            RingScatter(link, lambda i, p: buf.at[z, i, rows_of(p), a], x, x_plus, x_minus,
                        a3.at[cut[0]], a3.at[cut[1]], a4.at[0], a4.at[1]),
            RingScatter(link, lambda i, p: buf.at[i, x, rows_of(p), b], z, z_plus, z_minus,
                        b3.at[cut[0]], b3.at[cut[1]], b4.at[0], b4.at[1]),
        )

    xg[y, core] = x_ref[...]
    gather_x = ctx_gather(xg)
    pre_in[c] = win_ref[c]
    pre = []
    for step, mate in enumerate(mates):
        pre.append(
            (
                link.send(win_ref.at[mate[1]], pre_in.at[c], mate),
                link.send(pack_ref, pre_pack.at[step], mate),
            )
        )
    gather_x.start()
    wf[z, x] = wff_ref[...]
    cotg[y, core] = cot_ref[...]
    for step, (h_in, h_pack) in enumerate(pre):
        link.landed(h_in, pre_in.at[lax.rem(c + 7 - step, 8)])
        link.landed(h_pack, pre_pack.at[step])
    wc[z, x, 0:64, 0:384] = pre_in[...].reshape(64, 384).astype(bf16)
    wc[z, x, 0:64, 384:512] = wout_ref[...]
    own_pack = pack_ref[...]
    summed = own_pack
    for step in range(7):
        summed = summed + pre_pack[step]
    row = lax.broadcasted_iota(jnp.int32, (8, 128), 0)
    tile = jnp.where(row < 2, summed, own_pack)
    wc[z, x, 64:80, 0:128] = jnp.concatenate([tile, jnp.zeros_like(tile)], 0).astype(bf16)
    wc[z, x, 64:80, 128:512] = jnp.zeros((16, 384), bf16)
    conv_w = weight_gather(wc, 256, 48)
    ffn_w = weight_gather(wf, 896, 32)
    conv_w[0].start()
    conv_w[1].start()
    ffn_w[0].start()
    ffn_w[1].start()
    gather_x.forward()
    conv_w[0].forward()
    conv_w[1].forward()
    conv_w[0].finish()
    conv_w[1].finish()
    conv_w[2].start()
    conv_w[3].start()
    gather_x.across()
    ffn_w[0].forward()
    ffn_w[1].forward()
    conv_w[2].forward()
    conv_w[3].forward()
    ffn_w[0].finish()
    ffn_w[1].finish()
    ffn_w[2].start()
    ffn_w[3].start()
    gather_x.finish()
    gather_cot = ctx_gather(cotg)
    gather_cot.start()
    conv_w[2].finish()
    conv_w[3].finish()

    packs = [wc[i // 4, i % 4, 64:80, 0:128].astype(f32)[0:8] for i in range(16)]
    gain_one = jnp.concatenate([packs[2 * w][0:1] + packs[2 * w + 1][0:1] for w in range(8)], 1)
    gain_two = jnp.concatenate([packs[2 * w][1:2] + packs[2 * w + 1][1:2] for w in range(8)], 1)
    taps = packs[0]
    for i in range(1, 16):
        taps = taps + packs[i]
    tap = [taps[2 + k : 3 + k] for k in range(3)]
    w_in[...] = wc[:, :, 0:64, 0:384].reshape(1024, 384)
    slab = wc[:, :, 0:64, 384:512].astype(f32).reshape(16, 8, 8, 128)
    for w in range(8):
        w_out[:, 128 * w : 128 * w + 128] = slab[:, w].reshape(128, 128).astype(bf16)

    def project(g, carry):
        values = xg[g].reshape(256, 1024).astype(f32)
        scale = lax.rsqrt(jnp.mean(values * values, axis=-1, keepdims=True) + epsilon)
        scale_g[g] = scale
        lifted = (values * scale * gain_one).astype(bf16)
        h1g[g] = lifted
        proj[g] = mm(lifted, w_in[...])
        return carry

    lax.fori_loop(0, 4, project, 0)
    b_part = proj[:, :, 0:128].reshape(1024, 128)
    x_part = proj[:, :, 256:384].reshape(1024, 128)
    bx_pad[0:8] = jnp.zeros((8, 128), f32)
    bx_pad[8:1032] = (b_part * x_part).astype(bf16).astype(f32)
    z_all = tap[0] * bx_pad[6:1030] + tap[1] * bx_pad[7:1031] + tap[2] * bx_pad[8:1032]
    z_buf[...] = z_all
    y_buf[...] = (proj[:, :, 128:256].reshape(1024, 128) * z_all).astype(bf16).reshape(4, 256, 128)
    gather_cot.forward()
    ffn_w[2].forward()
    ffn_w[3].forward()

    scatter_r1 = ctx_scatter(0)

    def branch_out(step, carry):
        g = scatter_r1.group(step)
        rs_part[0, g] = mm(y_buf[g], w_out[...]).astype(bf16).reshape(2, 128, 1024)
        scatter_r1.cross(step)
        return carry

    lax.fori_loop(0, 4, branch_out, 0)
    scatter_r1.start()
    scatter_r1.middle()
    gather_cot.across()
    middle = x_ref[...].astype(f32) + scatter_r1.finish()
    scale_two = lax.rsqrt(jnp.mean(middle * middle, axis=-1, keepdims=True) + epsilon)
    h2g[y, core] = (middle * scale_two * gain_two).astype(bf16)
    gather_h2 = ctx_gather(h2g)
    gather_h2.start()
    gather_cot.finish()
    ffn_w[2].finish()
    ffn_w[3].finish()
    gather_h2.forward()
    gather_h2.across()
    gather_h2.finish()

    scatter_dh2 = ctx_scatter(1)
    low_half = lax.broadcasted_iota(jnp.int32, (256, 128), 1) < 64

    def feed_forward(step, carry):
        g = scatter_dh2.group(step)
        w_gu = wf[:, :, :, 0:GU].reshape(1024, GU)
        gu = mm(h2g[g].reshape(256, 1024), w_gu)
        mixed = gu[:, 1024:1152]
        gating = jnp.concatenate([gu[:, 0:512], mixed], 1)
        upward = jnp.concatenate([gu[:, 512:1024], pltpu.roll(mixed, 64, 1)], 1)
        sigma = 1.0 / (1.0 + jnp.exp(-gating))
        activated = gating * sigma
        hidden = activated * upward
        hid_buf[g, :, 0:512] = hidden[:, 0:512].astype(bf16)
        hid_buf[g, :, 512:640] = jnp.where(low_half, hidden[:, 512:640], 0.0).astype(bf16)
        w_down = wf[:, :, :, GU:FFL].reshape(1024, HID)
        d_hidden = mm(cotg[g].reshape(256, 1024), w_down)
        d_gating = d_hidden * upward * sigma * (1.0 + gating * (1.0 - sigma))
        d_upward = d_hidden * activated
        d_mixed = jnp.where(low_half, d_gating[:, 512:640], pltpu.roll(d_upward[:, 512:640], 64, 1))
        d_gu = jnp.concatenate([d_gating[:, 0:512], d_upward[:, 0:512], d_mixed], 1).astype(bf16)
        dgu_buf[g] = d_gu
        rs_part[1, g] = mt(d_gu, w_gu).astype(bf16).reshape(2, 128, 1024)
        scatter_dh2.cross(step)
        return carry

    lax.fori_loop(0, 4, feed_forward, 0)
    scatter_dh2.start()

    scatter_out = ctx_scatter(2)

    def ffn_out(step, carry):
        g = scatter_out.group(step)
        w_down = wf[:, :, :, GU:FFL].reshape(1024, HID)
        rs_part[2, g] = mt(hid_buf[g], w_down).astype(bf16).reshape(2, 128, 1024)
        scatter_out.cross(step)
        return carry

    lax.fori_loop(0, 4, ffn_out, 0)
    scatter_dh2.middle()

    def grad_gu(i, carry):
        lanes = pl.ds(pl.multiple_of(i * 256, 256), 256)
        lhs = h2g[:, :, :, lanes].reshape(1024, 256)
        gf[i, :, :, 0:GU] = tm(lhs, dgu_buf[...].reshape(1024, GU)).astype(bf16).reshape(4, 64, GU)
        return carry

    lax.fori_loop(0, 2, grad_gu, 0)

    d_second = scatter_dh2.finish()
    normed_two = middle * scale_two
    grad_gain_two = jnp.sum(d_second * normed_two, axis=0, keepdims=True)
    scaled = d_second * gain_two
    d_middle = cot_ref[...].astype(f32) + scale_two * (
        scaled - normed_two * jnp.mean(scaled * normed_two, axis=-1, keepdims=True)
    )
    dg[y, core] = d_middle.astype(bf16)
    gather_d = ctx_gather(dg)
    gather_d.start()

    lax.fori_loop(2, 4, grad_gu, 0)
    gather_d.forward()

    def grad_down(i, carry):
        lanes = pl.ds(pl.multiple_of(i * 256, 256), 256)
        lhs = cotg[:, :, :, lanes].reshape(1024, 256)
        gf[i, :, :, GU:FFL] = (
            tm(lhs, hid_buf[...].reshape(1024, HID)).astype(bf16).reshape(4, 64, HID)
        )
        return carry

    lax.fori_loop(0, 4, grad_down, 0)
    ffn_g = weight_scatter(gf, 896, 32, gf_a1, gf_a2, gf_b1, gf_b2, gf_a3, gf_a4, gf_b3, gf_b4)
    ffn_g[0].start()
    ffn_g[1].start()
    gather_d.across()
    scatter_out.start()
    gather_d.finish()

    d_z, d_c = [], []
    for g in range(4):
        d_gated = mt(dg[g].reshape(256, 1024), w_out[...])
        dz_pad[256 * g : 256 * g + 256] = d_gated * proj[g, :, 128:256]
        dp_buf[g, :, 128:256] = (d_gated * z_buf[256 * g : 256 * g + 256]).astype(bf16)
    dz_pad[1024:1032] = jnp.zeros((8, 128), f32)
    d_bx = tap[2] * dz_pad[0:1024] + tap[1] * dz_pad[1:1025] + tap[0] * dz_pad[2:1026]
    d_bx = d_bx.reshape(4, 256, 128)
    dp_buf[:, :, 0:128] = (d_bx * proj[:, :, 256:384]).astype(bf16)
    dp_buf[:, :, 256:384] = (d_bx * proj[:, :, 0:128]).astype(bf16)
    grad_tap = [
        jnp.sum(dz_pad[0:1024] * bx_pad[6 + k : 1030 + k], axis=0, keepdims=True) for k in range(3)
    ]
    ffn_g[0].middle()
    ffn_g[1].middle()

    scatter_dh1 = ctx_scatter(3)
    mix_acc[...] = jnp.zeros((8, 1024), f32)

    def branch_back(step, carry):
        g = scatter_dh1.group(step)
        d_lifted = mt(dp_buf[g], w_in[...])
        rs_part[3, g] = d_lifted.astype(bf16).reshape(2, 128, 1024)
        scatter_dh1.cross(step)
        normed = xg[g].reshape(256, 1024).astype(f32) * scale_g[g]
        mix_acc[...] += jnp.sum((d_lifted * normed).reshape(32, 8, 1024), axis=0)
        return carry

    lax.fori_loop(0, 4, branch_back, 0)
    scatter_dh1.start()

    def grad_in(i, carry):
        lanes = pl.ds(pl.multiple_of(i * 256, 256), 256)
        lhs = h1g[:, :, lanes].reshape(1024, 256)
        gc[i, :, 0:64, 0:384] = (
            tm(lhs, dp_buf[...].reshape(1024, 384)).astype(bf16).reshape(4, 64, 384)
        )
        return carry

    lax.fori_loop(0, 4, grad_in, 0)
    grad_mix = jnp.sum(mix_acc[...], axis=0, keepdims=True)
    g_out = tm(y_buf[...].reshape(1024, 128), dg[...].reshape(1024, 1024))
    pieces = [g_out[:, 128 * w : 128 * w + 128].reshape(16, 1, 8, 128) for w in range(8)]
    g_slab = jnp.concatenate(pieces, 1).reshape(4, 4, 64, 128)
    gc[:, :, 0:64, 384:512] = g_slab.astype(bf16)
    gc[:, :, 64:80, 128:512] = jnp.zeros((4, 4, 16, 384), bf16)
    for i in range(16):
        lanes = slice(128 * (i // 2), 128 * (i // 2) + 128)
        rows = [grad_mix[:, lanes], grad_gain_two[:, lanes], *grad_tap, jnp.zeros((11, 128), f32)]
        gc[i // 4, i % 4, 64:80, 0:128] = jnp.concatenate(rows, 0).astype(bf16)
    conv_g = weight_scatter(gc, 256, 48, gc_a1, gc_a2, gc_b1, gc_b2, gc_a3, gc_a4, gc_b3, gc_b4)
    conv_g[0].start()
    conv_g[1].start()
    scatter_dh1.middle()
    ffn_g[0].finish()
    ffn_g[1].finish()
    ffn_g[2].start()
    ffn_g[3].start()
    conv_g[0].middle()
    conv_g[1].middle()
    scatter_out.middle()

    d_lifted = scatter_dh1.finish()
    local = x_ref[...].astype(f32)
    scale_one = lax.rsqrt(jnp.mean(local * local, axis=-1, keepdims=True) + epsilon)
    normed_one = local * scale_one
    scaled = d_lifted * gain_one
    gin_ref[...] = d_middle + scale_one * (
        scaled - normed_one * jnp.mean(scaled * normed_one, axis=-1, keepdims=True)
    )
    conv_g[0].finish()
    conv_g[1].finish()
    conv_g[2].start()
    conv_g[3].start()
    ffn_g[2].middle()
    ffn_g[3].middle()
    conv_g[2].middle()
    conv_g[3].middle()
    out_ref[...] = (middle + scatter_out.finish()).astype(bf16)
    conv_g[2].finish()
    conv_g[3].finish()

    total = gc[z, x].astype(f32)
    gwout_ref[...] = total[0:64, 384:512]
    post_send[...] = total[0:64, 0:384].reshape(8, 8, 384)
    post_own[...] = total[64:72, 0:128]
    post = []
    for step, mate in enumerate(mates):
        post.append(
            (
                link.send(post_send.at[mate[1]], post_in.at[c], mate),
                link.send(post_own, post_pack.at[step], mate),
            )
        )
    ffn_g[2].finish()
    ffn_g[3].finish()
    gff_ref[...] = gf[z, x].astype(f32)
    post_in[c] = post_send[c]
    summed = post_own[...]
    for step, (h_in, h_pack) in enumerate(post):
        link.landed(h_in, post_in.at[lax.rem(c + 7 - step, 8)])
        link.landed(h_pack, post_pack.at[step])
        summed = summed + post_pack[step]
    gwin_ref[...] = post_in[...]
    gpack_ref[...] = jnp.where(row < 2, summed, post_own[...])

    link.drain()
    for scatter in (scatter_r1, scatter_dh2, scatter_out, scatter_dh1):
        scatter.drain()


def per_device(
    inputs,
    mix_gain,
    in_proj,
    conv_kernel,
    out_proj,
    ffn_gain,
    gate_proj,
    up_proj,
    down_proj,
    cotangent,
):
    f = lax.axis_index("fsdp")
    c = lax.axis_index("ctx")
    wff = jnp.concatenate(
        [
            gate_proj[:, :512],
            up_proj[:, :512],
            gate_proj[:, 512:],
            up_proj[:, 512:],
            down_proj.T,
            jnp.zeros((64, 64), bf16),
        ],
        1,
    )
    win = in_proj.reshape(8, 3, 16, 8, 8).transpose(3, 0, 1, 2, 4).reshape(8, 8, 384).astype(f32)
    wout = out_proj.reshape(8, 8, 128).transpose(1, 0, 2).reshape(64, 128)
    gains = jnp.stack([mix_gain, ffn_gain], 0).astype(f32)
    pack = jnp.zeros((8, 128), f32)
    pack = lax.dynamic_update_slice(pack, gains, (0, 64 * (f % 2) + 8 * c))
    pack = lax.dynamic_update_slice(pack, conv_kernel.astype(f32), (2, 8 * f))

    v = pltpu.VMEM
    in_vmem = pl.BlockSpec(memory_space=pltpu.VMEM)
    sems = 192
    out_shape = (
        jax.ShapeDtypeStruct((128, 1024), bf16),
        jax.ShapeDtypeStruct((128, 1024), f32),
        jax.ShapeDtypeStruct((64, FFL), f32),
        jax.ShapeDtypeStruct((8, 8, 384), f32),
        jax.ShapeDtypeStruct((64, 128), f32),
        jax.ShapeDtypeStruct((8, 128), f32),
    )
    scratch = [
        pltpu.SemaphoreType.DMA((sems,)),
        pltpu.SemaphoreType.DMA((sems,)),
        v((4, 2, 128, 1024), bf16),
        v((4, 2, 128, 1024), bf16),
        v((4, 2, 128, 1024), bf16),
        v((4, 2, 128, 1024), bf16),
        v((4, 4, 64, FFL), bf16),
        v((4, 4, CR, CL), bf16),
        v((8, 8, 384), f32),
        v((7, 8, 128), f32),
        v((1024, 384), bf16),
        v((128, 1024), bf16),
        v((4, 256, 1024), bf16),
        v((4, 256, 1), f32),
        v((4, 256, 384), f32),
        v((1032, 128), f32),
        v((1024, 128), f32),
        v((4, 256, 128), bf16),
        v((4, 256, HID), bf16),
        v((4, 256, GU), bf16),
        v((1032, 128), f32),
        v((4, 256, 384), bf16),
        v((8, 1024), f32),
        v((4, 4, 2, 128, 1024), bf16),
        v((4, 4, 128, 1024), bf16),
        v((4, 2, 64, 1024), bf16),
        v((4, 2, 128, 1024), bf16),
        v((4, 4, 64, FFL), bf16),
        v((4, 4, CR, CL), bf16),
        v((2, 2, 64, 896), bf16),
        v((2, 4, 64, 896), bf16),
        v((2, 2, 64, 896), bf16),
        v((2, 4, 64, 896), bf16),
        v((64, 896), bf16),
        v((2, 64, 896), bf16),
        v((64, 896), bf16),
        v((2, 64, 896), bf16),
        v((2, 2, CR, 256), bf16),
        v((2, 4, CR, 256), bf16),
        v((2, 2, CR, 256), bf16),
        v((2, 4, CR, 256), bf16),
        v((CR, 256), bf16),
        v((2, CR, 256), bf16),
        v((CR, 256), bf16),
        v((2, CR, 256), bf16),
        v((8, 8, 384), f32),
        v((8, 8, 384), f32),
        v((8, 128), f32),
        v((7, 8, 128), f32),
    ]
    block_out, grad_inputs, gff, gwin, gwout, gpack = pl.pallas_call(
        block_kernel,
        out_shape=out_shape,
        in_specs=[in_vmem] * 6,
        out_specs=(in_vmem,) * 6,
        scratch_shapes=scratch,
        compiler_params=pltpu.CompilerParams(
            collective_id=0, has_side_effects=True, vmem_limit_bytes=62 * 1024 * 1024
        ),
    )(inputs.reshape(128, 1024), cotangent.reshape(128, 1024), wff, win, wout, pack)

    grad_gains = lax.dynamic_slice(gpack, (0, 64 * (f % 2) + 8 * c), (2, 8))
    grad_taps = lax.dynamic_slice(gpack, (2, 8 * f), (3, 8))
    grad_in = gwin.reshape(8, 8, 3, 16, 8).transpose(1, 2, 3, 0, 4).reshape(8, 3072)
    grad_out = gwout.reshape(8, 8, 128).transpose(1, 0, 2).reshape(8, 1024)
    return (
        block_out.reshape(inputs.shape),
        grad_inputs.reshape(inputs.shape),
        grad_gains[0],
        grad_in,
        grad_taps,
        grad_out,
        grad_gains[1],
        jnp.concatenate([gff[:, :512], gff[:, 1024:1088]], 1),
        jnp.concatenate([gff[:, 512:1024], gff[:, 1088:1152]], 1),
        gff[:, 1152:1728].T,
    )


def solution(mesh):
    in_specs = (
        P("fsdp", "ctx", None),
        P(("fsdp", "ctx")),
        P(("fsdp", "ctx"), None),
        P(None, ("fsdp", "ctx")),
        P(("fsdp", "ctx"), None),
        P(("fsdp", "ctx")),
        P("fsdp", "ctx"),
        P("fsdp", "ctx"),
        P("ctx", "fsdp"),
        P("fsdp", "ctx", None),
    )
    out_specs = (
        P("fsdp", "ctx", None),
        P("fsdp", "ctx", None),
        P(("fsdp", "ctx")),
        P(("fsdp", "ctx"), None),
        P(None, ("fsdp", "ctx")),
        P(("fsdp", "ctx"), None),
        P(("fsdp", "ctx")),
        P("fsdp", "ctx"),
        P("fsdp", "ctx"),
        P("ctx", "fsdp"),
    )
    return jax.shard_map(
        per_device, mesh=mesh, in_specs=in_specs, out_specs=out_specs, check_vma=False
    )
```

```python
import jax
import jax.numpy as jnp
from jax import lax
from jax.experimental import pallas as pl
from jax.experimental.pallas import tpu as pltpu
from jax.sharding import PartitionSpec as P

epsilon = 1e-05
f32 = jnp.float32
bf16 = jnp.bfloat16
MESH = pl.DeviceIdType.MESH

GU = 1152
FFL = 1792
HID = 640
CR = 80
CL = 512


def mm(a, b):
    return lax.dot_general(a, b, (((1,), (0,)), ((), ())), preferred_element_type=f32)


def mt(a, b):
    return lax.dot_general(a, b, (((1,), (1,)), ((), ())), preferred_element_type=f32)


def tm(a, b):
    return lax.dot_general(a, b, (((0,), (0,)), ((), ())), preferred_element_type=f32)


def add_into(ref, *others):
    total = ref[...].astype(f32)
    for other in others:
        total = total + other[...].astype(f32)
    ref[...] = total.astype(ref.dtype)


class Link:
    def __init__(self, send_sems, recv_sems):
        self.send_sems, self.recv_sems = send_sems, recv_sems
        self.used = 0
        self.started = []

    def reserve(self, count):
        first = self.used
        self.used += count
        return first

    def copy(self, src, dst, device, slot):
        return pltpu.make_async_remote_copy(
            src_ref=src,
            dst_ref=dst,
            send_sem=self.send_sems.at[slot],
            recv_sem=self.recv_sems.at[slot],
            device_id=device,
            device_id_type=MESH,
        )

    def send(self, src, dst, device):
        slot = self.reserve(1)
        self.copy(src, dst, device, slot).start()
        self.started.append((src, device, slot))
        return (device, slot)

    def landed(self, handle, ref):
        device, slot = handle
        self.copy(ref, ref, device, slot).wait_recv()

    def drain(self):
        for src, device, slot in self.started:
            self.copy(src, src, device, slot).wait_send()


def ring(value, step):
    return lax.rem(value + step, 4)


class RingGather:
    def __init__(self, link, view, me, plus, minus):
        self.link, self.view, self.me, self.plus, self.minus = link, view, me, plus, minus

    def start(self):
        own = self.view(self.me, None)
        self.hp = self.link.send(own, own, self.plus)
        self.hm = self.link.send(own, own, self.minus)

    def forward(self):
        left, right = ring(self.me, 3), ring(self.me, 1)
        self.link.landed(self.hp, self.view(left, None))
        part = self.view(left, 0)
        self.fp = self.link.send(part, part, self.plus)
        self.link.landed(self.hm, self.view(right, None))
        part = self.view(right, 1)
        self.fm = self.link.send(part, part, self.minus)

    def finish(self):
        far = ring(self.me, 2)
        self.link.landed(self.fp, self.view(far, 0))
        self.link.landed(self.fm, self.view(far, 1))


class RingScatter:
    def __init__(self, link, view, me, plus, minus, r1a, r1b, r2a, r2b):
        self.link, self.view, self.me, self.plus, self.minus = link, view, me, plus, minus
        self.r1a, self.r1b, self.r2a, self.r2b = r1a, r1b, r2a, r2b

    def start(self):
        far = ring(self.me, 2)
        self.h1a = self.link.send(self.view(far, 0), self.r1a, self.plus)
        self.h1b = self.link.send(self.view(far, 1), self.r1b, self.minus)

    def middle(self):
        left, right = ring(self.me, 3), ring(self.me, 1)
        self.link.landed(self.h1a, self.r1a)
        add_into(self.view(right, 0), self.r1a)
        self.h2a = self.link.send(self.view(right, None), self.r2a, self.plus)
        self.link.landed(self.h1b, self.r1b)
        add_into(self.view(left, 1), self.r1b)
        self.h2b = self.link.send(self.view(left, None), self.r2b, self.minus)

    def finish(self):
        self.link.landed(self.h2a, self.r2a)
        self.link.landed(self.h2b, self.r2b)
        add_into(self.view(self.me, None), self.r2a, self.r2b)


class DirectGather:
    def __init__(self, link, view, me, device):
        self.link, self.view, self.me, self.device = link, view, me, device

    def start(self):
        own = self.view(self.me, None)
        self.sent = [(s, self.link.send(own, own, self.device(s))) for s in (1, 3, 2)]

    def finish(self):
        for step, handle in self.sent:
            self.link.landed(handle, self.view(ring(self.me, 4 - step), None))


class DirectScatter:
    def __init__(self, link, view, me, device, landing):
        self.link, self.view, self.me, self.device, self.landing = link, view, me, device, landing

    def start(self):
        self.sent = [
            (s, self.link.send(self.view(ring(self.me, s), None), self.landing.at[s - 1], self.device(s)))
            for s in (1, 3, 2)
        ]

    def finish(self):
        for step, handle in self.sent:
            self.link.landed(handle, self.landing.at[step - 1])
        add_into(self.view(self.me, None), *[self.landing.at[i] for i in range(3)])


LO, HI = pl.ds(0, 64), pl.ds(64, 64)


class CtxGather:
    def __init__(self, link, buf, y, core, plus, minus, other):
        self.link, self.buf, self.y, self.core = link, buf, y, core
        self.plus, self.minus, self.other = plus, minus, other

    def half(self, which, part):
        return self.buf.at[which, self.core, (LO, HI)[part]]

    def start(self):
        send = self.link.send
        lo, hi = self.half(self.y, 0), self.half(self.y, 1)
        own = self.buf.at[self.y, self.core]
        self.p0, self.m1 = send(lo, lo, self.plus), send(hi, hi, self.minus)
        self.p1, self.m0 = send(hi, hi, self.plus), send(lo, lo, self.minus)
        self.near = send(own, own, self.other)
        self.late = []

    def pass_on(self, handle, which, part, device):
        half = self.half(which, part)
        self.link.landed(handle, half)
        onward = None if device is None else self.link.send(half, half, device)
        theirs = self.buf.at[which, 1 - self.core, (LO, HI)[part]]
        self.late.append((self.link.send(half, half, self.other), theirs))
        return onward

    def forward(self):
        left, right = ring(self.y, 3), ring(self.y, 1)
        self.fp = self.pass_on(self.p0, left, 0, self.plus)
        self.fm = self.pass_on(self.m1, right, 1, self.minus)

    def sides(self):
        self.pass_on(self.p1, ring(self.y, 3), 1, None)
        self.pass_on(self.m0, ring(self.y, 1), 0, None)

    def across(self):
        far = ring(self.y, 2)
        self.pass_on(self.fp, far, 0, None)
        self.pass_on(self.fm, far, 1, None)

    def finish_near(self):
        self.link.landed(self.near, self.buf.at[self.y, 1 - self.core])

    def finish_far(self):
        for handle, ref in self.late:
            self.link.landed(handle, ref)


class CtxScatter:
    def __init__(self, link, part, rb, r1, r2, y, core, plus, minus, other):
        self.link, self.part, self.rb, self.r1, self.r2 = link, part, rb, r1, r2
        self.y, self.core = y, core
        self.plus, self.minus, self.other = plus, minus, other
        self.first = link.reserve(4)

    def group(self, step):
        return lax.rem(self.y + 2 + step + step // 2 + 2 * (step // 3), 4)

    def cross(self, step):
        g = self.group(step)
        self.link.copy(
            self.part.at[g, 1 - self.core], self.rb.at[g], self.other, self.first + step
        ).start()

    def crossed(self, g, step):
        ref = self.rb.at[g]
        self.link.copy(ref, ref, self.other, self.first + step).wait_recv()

    def block(self, which, rows):
        return self.part.at[which, self.core, rows]

    def start(self):
        far = ring(self.y, 2)
        self.crossed(far, 0)
        add_into(self.block(far, LO), self.rb.at[far, LO])
        self.h1a = self.link.send(self.block(far, LO), self.r1.at[0], self.plus)
        add_into(self.block(far, HI), self.rb.at[far, HI])
        self.h1b = self.link.send(self.block(far, HI), self.r1.at[1], self.minus)

    def sides(self):
        left, right = ring(self.y, 3), ring(self.y, 1)
        self.crossed(left, 1)
        add_into(self.block(left, LO), self.rb.at[left, LO])
        self.h2b0 = self.link.send(self.block(left, LO), self.r2.at[1, LO], self.minus)
        self.crossed(right, 2)
        add_into(self.block(right, HI), self.rb.at[right, HI])
        self.h2a1 = self.link.send(self.block(right, HI), self.r2.at[0, HI], self.plus)

    def middle(self):
        left, right = ring(self.y, 3), ring(self.y, 1)
        self.link.landed(self.h1a, self.r1.at[0])
        add_into(self.block(right, LO), self.rb.at[right, LO], self.r1.at[0])
        self.h2a0 = self.link.send(self.block(right, LO), self.r2.at[0, LO], self.plus)
        self.link.landed(self.h1b, self.r1.at[1])
        add_into(self.block(left, HI), self.rb.at[left, HI], self.r1.at[1])
        self.h2b1 = self.link.send(self.block(left, HI), self.r2.at[1, HI], self.minus)

    def finish(self):
        self.crossed(self.y, 3)
        self.link.landed(self.h2b0, self.r2.at[1, LO])
        self.link.landed(self.h2a1, self.r2.at[0, HI])
        self.link.landed(self.h2a0, self.r2.at[0, LO])
        self.link.landed(self.h2b1, self.r2.at[1, HI])
        return (
            self.part[self.y, self.core].astype(f32)
            + self.rb[self.y].astype(f32)
            + self.r2[0].astype(f32)
            + self.r2[1].astype(f32)
        )

    def drain(self):
        for step in range(4):
            g = self.group(step)
            src = self.part.at[g, 1 - self.core]
            self.link.copy(src, src, self.other, self.first + step).wait_send()


def by_channel(blocks, lane, inverse):
    made = []
    for target in range(8):
        total = jnp.zeros((8, 128), f32)
        for source in range(8):
            for h in range(2):
                if inverse:
                    start, lands = 16 * target + 8 * h, 64 * h + 8 * source
                else:
                    start, lands = 64 * h + 8 * target, 16 * source + 8 * h
                moved = pltpu.roll(blocks[source], (lands - start) % 128, 1)
                total = jnp.where((lane >= lands) & (lane < lands + 8), moved, total)
        made.append(total)
    return made


def block_kernel(
    x_ref,
    cot_ref,
    mix_ref,
    in_ref,
    tap_ref,
    proj_ref,
    ffn_ref,
    gate_ref,
    up_ref,
    down_ref,
    out_ref,
    gin_ref,
    gff_ref,
    gwin_ref,
    gwout_ref,
    gpack_ref,
    send_sems,
    recv_sems,
    win_ref,
    pack_ref,
    xg,
    cotg,
    h2g,
    dg,
    wf,
    wc,
    pre_in,
    pre_pack,
    w_in,
    w_out,
    h1g,
    scale_g,
    proj,
    bx_pad,
    z_buf,
    y_buf,
    hid_buf,
    dgu_buf,
    dz_pad,
    dp_buf,
    mix_acc,
    rs_part,
    rs_rb,
    rs_r1,
    rs_r2,
    gf,
    gc,
    gf_a1,
    gf_a2,
    gf_b1,
    gf_b2,
    gf_a3,
    gf_a4,
    gf_b3,
    gf_b4,
    gc_r1,
    gc_r2,
    post_send,
    post_in,
    post_own,
    post_pack,
):
    f = lax.axis_index("fsdp")
    c = lax.axis_index("ctx")
    z, x = f // 4, lax.rem(f, 4)
    y, core = c // 2, lax.rem(c, 2)
    y_plus, y_minus = (f, ring(y, 1) * 2 + core), (f, ring(y, 3) * 2 + core)
    other = (f, y * 2 + 1 - core)
    x_plus, x_minus = (z * 4 + ring(x, 1), c), (z * 4 + ring(x, 3), c)
    z_plus, z_minus = (ring(z, 1) * 4 + x, c), (ring(z, 3) * 4 + x, c)

    def along_x(step):
        return (z * 4 + ring(x, step), c)

    def along_z(step):
        return (ring(z, step) * 4 + x, c)

    mates = [(f, lax.rem(c + step, 8)) for step in range(1, 8)]

    barrier = pltpu.get_barrier_semaphore()
    rings = [along_x(step) for step in (1, 2, 3)] + [along_z(step) for step in (1, 2, 3)]
    for device in mates + rings:
        pl.semaphore_signal(barrier, inc=1, device_id=device, device_id_type=MESH)

    lane = lax.broadcasted_iota(jnp.int32, (8, 128), 1)
    row = lax.broadcasted_iota(jnp.int32, (8, 128), 0)
    xg[y, core] = x_ref[0]
    in_rows = in_ref[...].astype(f32)
    for b in range(3):
        blocks = [in_rows[:, 1024 * b + 128 * v : 1024 * b + 128 * v + 128] for v in range(8)]
        for channel, block in enumerate(by_channel(blocks, lane, False)):
            win_ref[channel, :, 128 * b : 128 * b + 128] = block
    pack_ref[...] = jnp.zeros((8, 128), f32)
    pack_ref[0:1, 0:8] = mix_ref[...].astype(f32)
    pack_ref[1:2, 0:8] = ffn_ref[...].astype(f32)
    pack_ref[2:5, 0:8] = tap_ref[...].astype(f32)
    small = pack_ref[...]
    gains = pltpu.roll(small, 64 * lax.rem(f, 2) + 8 * c, 1)
    own_pack = jnp.where(row < 2, gains, pltpu.roll(small, 8 * f, 1))
    pack_ref[...] = own_pack
    pre_in[c] = win_ref[c]
    pl.semaphore_wait(barrier, 13)

    link = Link(send_sems, recv_sems)

    def ctx_gather(buf):
        return CtxGather(link, buf, y, core, y_plus, y_minus, other)

    def ctx_scatter(n):
        return CtxScatter(
            link, rs_part.at[n], rs_rb.at[n], rs_r1.at[n], rs_r2.at[n],
            y, core, y_plus, y_minus, other,
        )

    def weight_gather(buf, half, low):
        rest = buf.shape[3] - half
        rows = buf.shape[2]
        a, b = pl.ds(0, half), pl.ds(half, rest)

        def rows_of(part):
            return pl.ds(0, rows) if part is None else (pl.ds(0, low), pl.ds(low, rows - low))[part]

        def pair(part):
            return pl.ds(0, 4) if part is None else pl.ds(2 * part, 2)

        return (
            RingGather(link, lambda i, p: buf.at[z, i, rows_of(p), a], x, x_plus, x_minus),
            RingGather(link, lambda i, p: buf.at[i, x, rows_of(p), b], z, z_plus, z_minus),
            RingGather(link, lambda i, p: buf.at[i, pair(p), :, a], z, z_plus, z_minus),
            RingGather(link, lambda i, p: buf.at[pair(p), i, :, b], x, x_plus, x_minus),
        )

    def conv_gather(buf):
        a, b = pl.ds(0, 256), pl.ds(256, 256)
        return (
            DirectGather(link, lambda i, p: buf.at[z, i, :, a], x, along_x),
            DirectGather(link, lambda i, p: buf.at[i, x, :, b], z, along_z),
            DirectGather(link, lambda i, p: buf.at[i, :, :, a], z, along_z),
            DirectGather(link, lambda i, p: buf.at[:, i, :, b], x, along_x),
        )

    def conv_scatter(buf, r1, r2):
        a, b = pl.ds(0, 256), pl.ds(256, 256)
        return (
            DirectScatter(link, lambda i, p: buf.at[i, :, :, a], z, along_z, r1.at[0]),
            DirectScatter(link, lambda i, p: buf.at[:, i, :, b], x, along_x, r1.at[1]),
            DirectScatter(link, lambda i, p: buf.at[z, i, :, a], x, along_x, r2.at[0]),
            DirectScatter(link, lambda i, p: buf.at[i, x, :, b], z, along_z, r2.at[1]),
        )

    def weight_scatter(buf, half, low, a1, a2, b1, b2, a3, a4, b3, b4):
        rest = buf.shape[3] - half
        rows = buf.shape[2]
        a, b = pl.ds(0, half), pl.ds(half, rest)

        def rows_of(part):
            return pl.ds(0, rows) if part is None else (pl.ds(0, low), pl.ds(low, rows - low))[part]

        def pair(part):
            return pl.ds(0, 4) if part is None else pl.ds(2 * part, 2)

        cut = (pl.ds(0, low), pl.ds(low, rows - low))
        return (
            RingScatter(link, lambda i, p: buf.at[i, pair(p), :, a], z, z_plus, z_minus,
                        a1.at[0], a1.at[1], a2.at[0], a2.at[1]),
            RingScatter(link, lambda i, p: buf.at[pair(p), i, :, b], x, x_plus, x_minus,
                        b1.at[0], b1.at[1], b2.at[0], b2.at[1]),
            RingScatter(link, lambda i, p: buf.at[z, i, rows_of(p), a], x, x_plus, x_minus,
                        a3.at[cut[0]], a3.at[cut[1]], a4.at[0], a4.at[1]),
            RingScatter(link, lambda i, p: buf.at[i, x, rows_of(p), b], z, z_plus, z_minus,
                        b3.at[cut[0]], b3.at[cut[1]], b4.at[0], b4.at[1]),
        )

    pre = []
    for step, mate in enumerate(mates):
        pre.append(
            (
                link.send(win_ref.at[mate[1]], pre_in.at[c], mate),
                link.send(pack_ref, pre_pack.at[step], mate),
            )
        )
    gather_x = ctx_gather(xg)
    gather_x.start()
    own = wf.at[z, x]
    own[:, 0:512] = gate_ref[:, 0:512]
    own[:, 512:1024] = up_ref[:, 0:512]
    own[:, 1024:1152] = jnp.concatenate([gate_ref[:, 512:576], up_ref[:, 512:576]], 1)
    own[:, 1152:1792] = jnp.concatenate(
        [down_ref[...].astype(f32).T, jnp.zeros((64, 64), f32)], 1
    ).astype(bf16)
    cotg[y, core] = cot_ref[0]
    out_rows = proj_ref[...].astype(f32)
    wc[z, x, 0:64, 384:512] = jnp.concatenate(
        [out_rows[:, 128 * w : 128 * w + 128] for w in range(8)], 0
    ).astype(bf16)
    wc[z, x, 64:80, 128:512] = jnp.zeros((16, 384), bf16)
    conv_w = conv_gather(wc)
    ffn_w = weight_gather(wf, 896, 32)
    for step, (h_in, h_pack) in enumerate(pre):
        link.landed(h_in, pre_in.at[lax.rem(c + 7 - step, 8)])
        link.landed(h_pack, pre_pack.at[step])
    wc[z, x, 0:64, 0:384] = pre_in[...].reshape(64, 384).astype(bf16)
    summed = own_pack
    for step in range(7):
        summed = summed + pre_pack[step]
    tile = jnp.where(row < 2, summed, own_pack)
    wc[z, x, 64:80, 0:128] = jnp.concatenate([tile, jnp.zeros_like(tile)], 0).astype(bf16)
    conv_w[0].start()
    conv_w[1].start()
    gather_x.forward()
    ffn_w[0].start()
    ffn_w[1].start()
    gather_x.sides()
    conv_w[0].finish()
    conv_w[1].finish()
    conv_w[2].start()
    conv_w[3].start()
    gather_x.across()
    ffn_w[0].forward()
    ffn_w[1].forward()
    gather_x.finish_near()
    gather_x.finish_far()
    gather_cot = ctx_gather(cotg)
    gather_cot.start()
    conv_w[2].finish()
    conv_w[3].finish()
    ffn_w[0].finish()
    ffn_w[1].finish()
    ffn_w[2].start()
    ffn_w[3].start()

    packs = [wc[i // 4, i % 4, 64:80, 0:128].astype(f32)[0:8] for i in range(16)]
    gain_one = jnp.concatenate([packs[2 * w][0:1] + packs[2 * w + 1][0:1] for w in range(8)], 1)
    gain_two = jnp.concatenate([packs[2 * w][1:2] + packs[2 * w + 1][1:2] for w in range(8)], 1)
    taps = packs[0]
    for i in range(1, 16):
        taps = taps + packs[i]
    tap = [taps[2 + k : 3 + k] for k in range(3)]
    w_in[...] = wc[:, :, 0:64, 0:384].reshape(1024, 384)
    slab = wc[:, :, 0:64, 384:512].astype(f32).reshape(16, 8, 8, 128)
    for w in range(8):
        w_out[:, 128 * w : 128 * w + 128] = slab[:, w].reshape(128, 128).astype(bf16)

    def project(g, carry):
        values = xg[g].reshape(256, 1024).astype(f32)
        scale = lax.rsqrt(jnp.mean(values * values, axis=-1, keepdims=True) + epsilon)
        scale_g[g] = scale
        lifted = (values * scale * gain_one).astype(bf16)
        h1g[g] = lifted
        proj[g] = mm(lifted, w_in[...])
        return carry

    lax.fori_loop(0, 4, project, 0)
    b_part = proj[:, :, 0:128].reshape(1024, 128)
    x_part = proj[:, :, 256:384].reshape(1024, 128)
    bx_pad[0:8] = jnp.zeros((8, 128), f32)
    bx_pad[8:1032] = (b_part * x_part).astype(bf16).astype(f32)
    z_all = tap[0] * bx_pad[6:1030] + tap[1] * bx_pad[7:1031] + tap[2] * bx_pad[8:1032]
    z_buf[...] = z_all
    y_buf[...] = (proj[:, :, 128:256].reshape(1024, 128) * z_all).astype(bf16).reshape(4, 256, 128)
    gather_cot.forward()
    gather_cot.sides()
    ffn_w[2].forward()
    ffn_w[3].forward()

    scatter_r1 = ctx_scatter(0)

    def branch_out(step, carry):
        g = scatter_r1.group(step)
        rs_part[0, g] = mm(y_buf[g], w_out[...]).astype(bf16).reshape(2, 128, 1024)
        scatter_r1.cross(step)
        return carry

    lax.fori_loop(0, 4, branch_out, 0)
    scatter_r1.start()
    scatter_r1.sides()
    scatter_r1.middle()
    gather_cot.across()
    middle = x_ref[0].astype(f32) + scatter_r1.finish()
    scale_two = lax.rsqrt(jnp.mean(middle * middle, axis=-1, keepdims=True) + epsilon)
    h2g[y, core] = (middle * scale_two * gain_two).astype(bf16)
    gather_h2 = ctx_gather(h2g)
    gather_h2.start()
    gather_cot.finish_near()
    gather_cot.finish_far()
    ffn_w[2].finish()
    ffn_w[3].finish()
    gather_h2.forward()
    gather_h2.sides()
    gather_h2.across()
    gather_h2.finish_near()
    gather_h2.finish_far()

    scatter_dh2 = ctx_scatter(1)
    low_half = lax.broadcasted_iota(jnp.int32, (256, 128), 1) < 64

    def feed_forward(step, carry):
        g = scatter_dh2.group(step)
        w_gu = wf[:, :, :, 0:GU].reshape(1024, GU)
        gu = mm(h2g[g].reshape(256, 1024), w_gu)
        mixed = gu[:, 1024:1152]
        gating = jnp.concatenate([gu[:, 0:512], mixed], 1)
        upward = jnp.concatenate([gu[:, 512:1024], pltpu.roll(mixed, 64, 1)], 1)
        sigma = 1.0 / (1.0 + jnp.exp(-gating))
        activated = gating * sigma
        hidden = activated * upward
        hid_buf[g, :, 0:512] = hidden[:, 0:512].astype(bf16)
        hid_buf[g, :, 512:640] = jnp.where(low_half, hidden[:, 512:640], 0.0).astype(bf16)
        w_down = wf[:, :, :, GU:FFL].reshape(1024, HID)
        d_hidden = mm(cotg[g].reshape(256, 1024), w_down)
        d_gating = d_hidden * upward * sigma * (1.0 + gating * (1.0 - sigma))
        d_upward = d_hidden * activated
        d_mixed = jnp.where(low_half, d_gating[:, 512:640], pltpu.roll(d_upward[:, 512:640], 64, 1))
        d_gu = jnp.concatenate([d_gating[:, 0:512], d_upward[:, 0:512], d_mixed], 1).astype(bf16)
        dgu_buf[g] = d_gu
        rs_part[1, g] = mt(d_gu, w_gu).astype(bf16).reshape(2, 128, 1024)
        scatter_dh2.cross(step)
        return carry

    lax.fori_loop(0, 4, feed_forward, 0)
    scatter_dh2.start()
    scatter_dh2.sides()

    scatter_out = ctx_scatter(2)

    def ffn_out(step, carry):
        g = scatter_out.group(step)
        w_down = wf[:, :, :, GU:FFL].reshape(1024, HID)
        rs_part[2, g] = mt(hid_buf[g], w_down).astype(bf16).reshape(2, 128, 1024)
        scatter_out.cross(step)
        return carry

    lax.fori_loop(0, 4, ffn_out, 0)
    scatter_dh2.middle()

    def grad_gu(i, carry):
        lanes = pl.ds(pl.multiple_of(i * 256, 256), 256)
        lhs = h2g[:, :, :, lanes].reshape(1024, 256)
        gf[i, :, :, 0:GU] = tm(lhs, dgu_buf[...].reshape(1024, GU)).astype(bf16).reshape(4, 64, GU)
        return carry

    lax.fori_loop(0, 2, grad_gu, 0)

    d_second = scatter_dh2.finish()
    normed_two = middle * scale_two
    grad_gain_two = jnp.sum(d_second * normed_two, axis=0, keepdims=True)
    scaled = d_second * gain_two
    d_middle = cot_ref[0].astype(f32) + scale_two * (
        scaled - normed_two * jnp.mean(scaled * normed_two, axis=-1, keepdims=True)
    )
    dg[y, core] = d_middle.astype(bf16)
    gather_d = ctx_gather(dg)
    gather_d.start()

    lax.fori_loop(2, 4, grad_gu, 0)
    gather_d.forward()
    gather_d.sides()

    def grad_down(i, carry):
        lanes = pl.ds(pl.multiple_of(i * 256, 256), 256)
        lhs = cotg[:, :, :, lanes].reshape(1024, 256)
        gf[i, :, :, GU:FFL] = (
            tm(lhs, hid_buf[...].reshape(1024, HID)).astype(bf16).reshape(4, 64, HID)
        )
        return carry

    lax.fori_loop(0, 4, grad_down, 0)
    ffn_g = weight_scatter(gf, 896, 32, gf_a1, gf_a2, gf_b1, gf_b2, gf_a3, gf_a4, gf_b3, gf_b4)
    ffn_g[0].start()
    ffn_g[1].start()
    gather_d.across()
    scatter_out.start()
    scatter_out.sides()
    gather_d.finish_near()
    gather_d.finish_far()

    for g in range(4):
        d_gated = mt(dg[g].reshape(256, 1024), w_out[...])
        dz_pad[256 * g : 256 * g + 256] = d_gated * proj[g, :, 128:256]
        dp_buf[g, :, 128:256] = (d_gated * z_buf[256 * g : 256 * g + 256]).astype(bf16)
    dz_pad[1024:1032] = jnp.zeros((8, 128), f32)
    d_bx = tap[2] * dz_pad[0:1024] + tap[1] * dz_pad[1:1025] + tap[0] * dz_pad[2:1026]
    d_bx = d_bx.reshape(4, 256, 128)
    dp_buf[:, :, 0:128] = (d_bx * proj[:, :, 256:384]).astype(bf16)
    dp_buf[:, :, 256:384] = (d_bx * proj[:, :, 0:128]).astype(bf16)
    grad_tap = [
        jnp.sum(dz_pad[0:1024] * bx_pad[6 + k : 1030 + k], axis=0, keepdims=True) for k in range(3)
    ]
    ffn_g[0].middle()
    ffn_g[1].middle()

    scatter_dh1 = ctx_scatter(3)
    mix_acc[...] = jnp.zeros((8, 1024), f32)

    def branch_back(step, carry):
        g = scatter_dh1.group(step)
        d_lifted = mt(dp_buf[g], w_in[...])
        rs_part[3, g] = d_lifted.astype(bf16).reshape(2, 128, 1024)
        scatter_dh1.cross(step)
        normed = xg[g].reshape(256, 1024).astype(f32) * scale_g[g]
        mix_acc[...] += jnp.sum((d_lifted * normed).reshape(32, 8, 1024), axis=0)
        return carry

    lax.fori_loop(0, 4, branch_back, 0)
    scatter_dh1.start()
    scatter_dh1.sides()

    def grad_in(i, carry):
        lanes = pl.ds(pl.multiple_of(i * 256, 256), 256)
        lhs = h1g[:, :, lanes].reshape(1024, 256)
        gc[i, :, 0:64, 0:384] = (
            tm(lhs, dp_buf[...].reshape(1024, 384)).astype(bf16).reshape(4, 64, 384)
        )
        return carry

    lax.fori_loop(0, 4, grad_in, 0)
    grad_mix = jnp.sum(mix_acc[...], axis=0, keepdims=True)
    g_out = tm(y_buf[...].reshape(1024, 128), dg[...].reshape(1024, 1024))
    pieces = [g_out[:, 128 * w : 128 * w + 128].reshape(16, 1, 8, 128) for w in range(8)]
    g_slab = jnp.concatenate(pieces, 1).reshape(4, 4, 64, 128)
    gc[:, :, 0:64, 384:512] = g_slab.astype(bf16)
    gc[:, :, 64:80, 128:512] = jnp.zeros((4, 4, 16, 384), bf16)
    for i in range(16):
        lanes = slice(128 * (i // 2), 128 * (i // 2) + 128)
        rows = [grad_mix[:, lanes], grad_gain_two[:, lanes], *grad_tap, jnp.zeros((11, 128), f32)]
        gc[i // 4, i % 4, 64:80, 0:128] = jnp.concatenate(rows, 0).astype(bf16)
    conv_g = conv_scatter(gc, gc_r1, gc_r2)
    conv_g[0].start()
    conv_g[1].start()
    scatter_dh1.middle()
    ffn_g[0].finish()
    ffn_g[1].finish()
    ffn_g[2].start()
    ffn_g[3].start()
    scatter_out.middle()

    d_lifted = scatter_dh1.finish()
    local = x_ref[0].astype(f32)
    scale_one = lax.rsqrt(jnp.mean(local * local, axis=-1, keepdims=True) + epsilon)
    normed_one = local * scale_one
    scaled = d_lifted * gain_one
    gin_ref[...] = d_middle + scale_one * (
        scaled - normed_one * jnp.mean(scaled * normed_one, axis=-1, keepdims=True)
    )
    conv_g[0].finish()
    conv_g[1].finish()
    conv_g[2].start()
    conv_g[3].start()
    ffn_g[2].middle()
    ffn_g[3].middle()
    out_ref[...] = (middle + scatter_out.finish()).astype(bf16)
    conv_g[2].finish()
    conv_g[3].finish()

    total = gc[z, x].astype(f32)
    gwout_ref[...] = total[0:64, 384:512]
    post_send[...] = total[0:64, 0:384].reshape(8, 8, 384)
    post_own[...] = total[64:72, 0:128]
    post = []
    for step, mate in enumerate(mates):
        post.append(
            (
                link.send(post_send.at[mate[1]], post_in.at[c], mate),
                link.send(post_own, post_pack.at[step], mate),
            )
        )
    ffn_g[2].finish()
    ffn_g[3].finish()
    gff_ref[...] = gf[z, x].astype(f32)
    post_in[c] = post_send[c]
    summed = post_own[...]
    for step, (h_in, h_pack) in enumerate(post):
        link.landed(h_in, post_in.at[lax.rem(c + 7 - step, 8)])
        link.landed(h_pack, post_pack.at[step])
        summed = summed + post_pack[step]
    gwin_ref[...] = post_in[...]
    gpack_ref[...] = jnp.where(row < 2, summed, post_own[...])

    link.drain()
    for scatter in (scatter_r1, scatter_dh2, scatter_out, scatter_dh1):
        scatter.drain()


def spread_kernel(
    block_ref,
    gin_ref,
    gff_ref,
    gwin_ref,
    gwout_ref,
    gpack_ref,
    o_block,
    o_gin,
    o_mix,
    o_in,
    o_tap,
    o_proj,
    o_ffn,
    o_gate,
    o_up,
    o_down,
):
    f = lax.axis_index("fsdp")
    c = lax.axis_index("ctx")
    lane = lax.broadcasted_iota(jnp.int32, (8, 128), 1)
    o_block[0] = block_ref[...]
    o_gin[0] = gin_ref[...]
    for b in range(3):
        blocks = [gwin_ref[i, :, 128 * b : 128 * b + 128] for i in range(8)]
        for v, block in enumerate(by_channel(blocks, lane, True)):
            o_in[:, 1024 * b + 128 * v : 1024 * b + 128 * v + 128] = block
    for w in range(8):
        o_proj[:, 128 * w : 128 * w + 128] = gwout_ref[8 * w : 8 * w + 8]
    small = gpack_ref[...]
    gains = pltpu.roll(small, lax.rem(256 - 64 * lax.rem(f, 2) - 8 * c, 128), 1)
    o_mix[...] = gains[0:1, 0:8]
    o_ffn[...] = gains[1:2, 0:8]
    o_tap[...] = pltpu.roll(small, lax.rem(128 - 8 * f, 128), 1)[2:5, 0:8]
    mixed = gff_ref[:, 1024:1152]
    o_gate[:, 0:512] = gff_ref[:, 0:512]
    o_gate[:, 512:576] = mixed[:, 0:64]
    o_up[:, 0:512] = gff_ref[:, 512:1024]
    o_up[:, 512:576] = pltpu.roll(mixed, 64, 1)[:, 0:64]
    o_down[...] = gff_ref[:, 1152:1792].T[0:576]


def per_device(
    inputs,
    mix_gain,
    in_proj,
    conv_kernel,
    out_proj,
    ffn_gain,
    gate_proj,
    up_proj,
    down_proj,
    cotangent,
):
    v = pltpu.VMEM
    in_vmem = pl.BlockSpec(memory_space=pltpu.VMEM)
    sems = 256
    out_shape = (
        jax.ShapeDtypeStruct((128, 1024), bf16),
        jax.ShapeDtypeStruct((128, 1024), f32),
        jax.ShapeDtypeStruct((64, FFL), f32),
        jax.ShapeDtypeStruct((8, 8, 384), f32),
        jax.ShapeDtypeStruct((64, 128), f32),
        jax.ShapeDtypeStruct((8, 128), f32),
    )
    scratch = [
        pltpu.SemaphoreType.DMA((sems,)),
        pltpu.SemaphoreType.DMA((sems,)),
        v((8, 8, 384), f32),
        v((8, 128), f32),
        v((4, 2, 128, 1024), bf16),
        v((4, 2, 128, 1024), bf16),
        v((4, 2, 128, 1024), bf16),
        v((4, 2, 128, 1024), bf16),
        v((4, 4, 64, FFL), bf16),
        v((4, 4, CR, CL), bf16),
        v((8, 8, 384), f32),
        v((7, 8, 128), f32),
        v((1024, 384), bf16),
        v((128, 1024), bf16),
        v((4, 256, 1024), bf16),
        v((4, 256, 1), f32),
        v((4, 256, 384), f32),
        v((1032, 128), f32),
        v((1024, 128), f32),
        v((4, 256, 128), bf16),
        v((4, 256, HID), bf16),
        v((4, 256, GU), bf16),
        v((1032, 128), f32),
        v((4, 256, 384), bf16),
        v((8, 1024), f32),
        v((4, 4, 2, 128, 1024), bf16),
        v((4, 4, 128, 1024), bf16),
        v((4, 2, 64, 1024), bf16),
        v((4, 2, 128, 1024), bf16),
        v((4, 4, 64, FFL), bf16),
        v((4, 4, CR, CL), bf16),
        v((2, 2, 64, 896), bf16),
        v((2, 4, 64, 896), bf16),
        v((2, 2, 64, 896), bf16),
        v((2, 4, 64, 896), bf16),
        v((64, 896), bf16),
        v((2, 64, 896), bf16),
        v((64, 896), bf16),
        v((2, 64, 896), bf16),
        v((2, 3, 4, CR, 256), bf16),
        v((2, 3, CR, 256), bf16),
        v((8, 8, 384), f32),
        v((8, 8, 384), f32),
        v((8, 128), f32),
        v((7, 8, 128), f32),
    ]
    raw = pl.pallas_call(
        block_kernel,
        out_shape=out_shape,
        in_specs=[in_vmem] * 10,
        out_specs=(in_vmem,) * 6,
        scratch_shapes=scratch,
        compiler_params=pltpu.CompilerParams(
            collective_id=0, has_side_effects=True, vmem_limit_bytes=62 * 1024 * 1024
        ),
    )(
        inputs,
        cotangent,
        mix_gain.reshape(1, 8),
        in_proj,
        conv_kernel,
        out_proj,
        ffn_gain.reshape(1, 8),
        gate_proj,
        up_proj,
        down_proj,
    )
    made = pl.pallas_call(
        spread_kernel,
        out_shape=(
            jax.ShapeDtypeStruct(inputs.shape, bf16),
            jax.ShapeDtypeStruct(inputs.shape, f32),
            jax.ShapeDtypeStruct((1, 8), f32),
            jax.ShapeDtypeStruct(in_proj.shape, f32),
            jax.ShapeDtypeStruct(conv_kernel.shape, f32),
            jax.ShapeDtypeStruct(out_proj.shape, f32),
            jax.ShapeDtypeStruct((1, 8), f32),
            jax.ShapeDtypeStruct(gate_proj.shape, f32),
            jax.ShapeDtypeStruct(up_proj.shape, f32),
            jax.ShapeDtypeStruct(down_proj.shape, f32),
        ),
        in_specs=[in_vmem] * 6,
        out_specs=(in_vmem,) * 10,
        compiler_params=pltpu.CompilerParams(vmem_limit_bytes=16 * 1024 * 1024),
    )(*raw)
    return (*made[:2], made[2].reshape(8), *made[3:6], made[6].reshape(8), *made[7:])


def solution(mesh):
    in_specs = (
        P("fsdp", "ctx", None),
        P(("fsdp", "ctx")),
        P(("fsdp", "ctx"), None),
        P(None, ("fsdp", "ctx")),
        P(("fsdp", "ctx"), None),
        P(("fsdp", "ctx")),
        P("fsdp", "ctx"),
        P("fsdp", "ctx"),
        P("ctx", "fsdp"),
        P("fsdp", "ctx", None),
    )
    out_specs = (
        P("fsdp", "ctx", None),
        P("fsdp", "ctx", None),
        P(("fsdp", "ctx")),
        P(("fsdp", "ctx"), None),
        P(None, ("fsdp", "ctx")),
        P(("fsdp", "ctx"), None),
        P(("fsdp", "ctx")),
        P("fsdp", "ctx"),
        P("fsdp", "ctx"),
        P("ctx", "fsdp"),
    )
    return jax.shard_map(
        per_device, mesh=mesh, in_specs=in_specs, out_specs=out_specs, check_vma=False
    )
```

```python
import jax
import jax.numpy as jnp
from jax import lax
from jax.experimental import pallas as pl
from jax.experimental.pallas import tpu as pltpu
from jax.sharding import PartitionSpec as P

epsilon = 1e-05
f32 = jnp.float32
bf16 = jnp.bfloat16
MESH = pl.DeviceIdType.MESH

GU = 1152
FFL = 1792
HID = 640
CR = 80
CL = 512


def mm(a, b):
    return lax.dot_general(a, b, (((1,), (0,)), ((), ())), preferred_element_type=f32)


def mt(a, b):
    return lax.dot_general(a, b, (((1,), (1,)), ((), ())), preferred_element_type=f32)


def tm(a, b):
    return lax.dot_general(a, b, (((0,), (0,)), ((), ())), preferred_element_type=f32)


def add_into(ref, *others):
    total = ref[...].astype(f32)
    for other in others:
        total = total + other[...].astype(f32)
    ref[...] = total.astype(ref.dtype)


class Link:
    def __init__(self, send_sems, recv_sems):
        self.send_sems, self.recv_sems = send_sems, recv_sems
        self.used = 0
        self.started = []

    def reserve(self, count):
        first = self.used
        self.used += count
        return first

    def copy(self, src, dst, device, slot):
        return pltpu.make_async_remote_copy(
            src_ref=src,
            dst_ref=dst,
            send_sem=self.send_sems.at[slot],
            recv_sem=self.recv_sems.at[slot],
            device_id=device,
            device_id_type=MESH,
        )

    def send(self, src, dst, device):
        slot = self.reserve(1)
        self.copy(src, dst, device, slot).start()
        self.started.append((src, device, slot))
        return (device, slot)

    def landed(self, handle, ref):
        device, slot = handle
        self.copy(ref, ref, device, slot).wait_recv()

    def drain(self):
        for src, device, slot in self.started:
            self.copy(src, src, device, slot).wait_send()


def ring(value, step):
    return lax.rem(value + step, 4)


class RingGather:
    def __init__(self, link, view, me, plus, minus):
        self.link, self.view, self.me, self.plus, self.minus = link, view, me, plus, minus

    def start(self):
        own = self.view(self.me, None)
        self.hp = self.link.send(own, own, self.plus)
        self.hm = self.link.send(own, own, self.minus)

    def forward(self):
        left, right = ring(self.me, 3), ring(self.me, 1)
        self.link.landed(self.hp, self.view(left, None))
        part = self.view(left, 0)
        self.fp = self.link.send(part, part, self.plus)
        self.link.landed(self.hm, self.view(right, None))
        part = self.view(right, 1)
        self.fm = self.link.send(part, part, self.minus)

    def finish(self):
        far = ring(self.me, 2)
        self.link.landed(self.fp, self.view(far, 0))
        self.link.landed(self.fm, self.view(far, 1))


class RingScatter:
    def __init__(self, link, view, me, plus, minus, r1a, r1b, r2a, r2b):
        self.link, self.view, self.me, self.plus, self.minus = link, view, me, plus, minus
        self.r1a, self.r1b, self.r2a, self.r2b = r1a, r1b, r2a, r2b

    def start(self):
        far = ring(self.me, 2)
        self.h1a = self.link.send(self.view(far, 0), self.r1a, self.plus)
        self.h1b = self.link.send(self.view(far, 1), self.r1b, self.minus)

    def middle(self):
        left, right = ring(self.me, 3), ring(self.me, 1)
        self.link.landed(self.h1a, self.r1a)
        add_into(self.view(right, 0), self.r1a)
        self.h2a = self.link.send(self.view(right, None), self.r2a, self.plus)
        self.link.landed(self.h1b, self.r1b)
        add_into(self.view(left, 1), self.r1b)
        self.h2b = self.link.send(self.view(left, None), self.r2b, self.minus)

    def finish(self):
        self.link.landed(self.h2a, self.r2a)
        self.link.landed(self.h2b, self.r2b)
        add_into(self.view(self.me, None), self.r2a, self.r2b)


class DirectGather:
    def __init__(self, link, view, me, device):
        self.link, self.view, self.me, self.device = link, view, me, device

    def start(self):
        own = self.view(self.me, None)
        self.sent = [(s, self.link.send(own, own, self.device(s))) for s in (1, 3, 2)]

    def finish(self):
        for step, handle in self.sent:
            self.link.landed(handle, self.view(ring(self.me, 4 - step), None))


class DirectScatter:
    def __init__(self, link, view, me, device, landing):
        self.link, self.view, self.me, self.device, self.landing = link, view, me, device, landing

    def start(self):
        self.sent = [
            (s, self.link.send(self.view(ring(self.me, s), None), self.landing.at[s - 1], self.device(s)))
            for s in (1, 3, 2)
        ]

    def finish(self):
        for step, handle in self.sent:
            self.link.landed(handle, self.landing.at[step - 1])
        add_into(self.view(self.me, None), *[self.landing.at[i] for i in range(3)])


LO, HI = pl.ds(0, 64), pl.ds(64, 64)


class CtxGather:
    def __init__(self, link, buf, y, core, plus, minus, other):
        self.link, self.buf, self.y, self.core = link, buf, y, core
        self.plus, self.minus, self.other = plus, minus, other
        self.left, self.far, self.right = ring(y, 3), ring(y, 2), ring(y, 1)
        self.mate = 1 - core

    def half(self, which, part):
        return self.buf.at[which, self.core, (LO, HI)[part]]

    def start(self):
        send = self.link.send
        lo, hi = self.half(self.y, 0), self.half(self.y, 1)
        own = self.buf.at[self.y, self.core]
        self.p0, self.m1 = send(lo, lo, self.plus), send(hi, hi, self.minus)
        self.p1, self.m0 = send(hi, hi, self.plus), send(lo, lo, self.minus)
        self.near = send(own, own, self.other)
        self.late = []

    def pass_on(self, handle, which, part, device):
        half = self.half(which, part)
        self.link.landed(handle, half)
        onward = None if device is None else self.link.send(half, half, device)
        theirs = self.buf.at[which, self.mate, (LO, HI)[part]]
        self.late.append((self.link.send(half, half, self.other), theirs))
        return onward

    def forward(self):
        left, right = self.left, self.right
        self.fp = self.pass_on(self.p0, left, 0, self.plus)
        self.fm = self.pass_on(self.m1, right, 1, self.minus)

    def sides(self):
        self.pass_on(self.p1, self.left, 1, None)
        self.pass_on(self.m0, self.right, 0, None)

    def across(self):
        far = self.far
        self.pass_on(self.fp, far, 0, None)
        self.pass_on(self.fm, far, 1, None)

    def finish_near(self):
        self.link.landed(self.near, self.buf.at[self.y, self.mate])

    def finish_far(self):
        for handle, ref in self.late:
            self.link.landed(handle, ref)


class CtxScatter:
    def __init__(self, link, part, rb, r1, r2, y, core, plus, minus, other, own_first):
        self.link, self.part, self.rb, self.r1, self.r2 = link, part, rb, r1, r2
        self.y, self.core, self.own_first = y, core, own_first
        self.plus, self.minus, self.other = plus, minus, other
        self.left, self.far, self.right = ring(y, 3), ring(y, 2), ring(y, 1)
        self.mate = 1 - core
        self.first = link.reserve(4)
        self.at_far, self.at_left, self.at_right, self.at_own = (1, 2, 3, 0) if own_first else (0, 1, 2, 3)

    def group(self, step):
        if self.own_first:
            return lax.rem(self.y + 2 * step - step // 2, 4)
        return lax.rem(self.y + 2 + step + step // 2 + 2 * (step // 3), 4)

    def cross(self, step):
        g = self.group(step)
        self.link.copy(
            self.part.at[g, self.mate], self.rb.at[g], self.other, self.first + step
        ).start()

    def crossed(self, g, step):
        ref = self.rb.at[g]
        self.link.copy(ref, ref, self.other, self.first + step).wait_recv()

    def block(self, which, rows):
        return self.part.at[which, self.core, rows]

    def start(self):
        far = self.far
        self.crossed(far, self.at_far)
        add_into(self.block(far, LO), self.rb.at[far, LO])
        self.h1a = self.link.send(self.block(far, LO), self.r1.at[0], self.plus)
        add_into(self.block(far, HI), self.rb.at[far, HI])
        self.h1b = self.link.send(self.block(far, HI), self.r1.at[1], self.minus)

    def sides(self):
        left, right = self.left, self.right
        self.crossed(left, self.at_left)
        add_into(self.block(left, LO), self.rb.at[left, LO])
        self.h2b0 = self.link.send(self.block(left, LO), self.r2.at[1, LO], self.minus)
        self.crossed(right, self.at_right)
        add_into(self.block(right, HI), self.rb.at[right, HI])
        self.h2a1 = self.link.send(self.block(right, HI), self.r2.at[0, HI], self.plus)

    def middle(self):
        left, right = self.left, self.right
        self.link.landed(self.h1a, self.r1.at[0])
        add_into(self.block(right, LO), self.rb.at[right, LO], self.r1.at[0])
        self.h2a0 = self.link.send(self.block(right, LO), self.r2.at[0, LO], self.plus)
        self.link.landed(self.h1b, self.r1.at[1])
        add_into(self.block(left, HI), self.rb.at[left, HI], self.r1.at[1])
        self.h2b1 = self.link.send(self.block(left, HI), self.r2.at[1, HI], self.minus)

    def finish(self):
        self.crossed(self.y, self.at_own)
        self.link.landed(self.h2b0, self.r2.at[1, LO])
        self.link.landed(self.h2a1, self.r2.at[0, HI])
        self.link.landed(self.h2a0, self.r2.at[0, LO])
        self.link.landed(self.h2b1, self.r2.at[1, HI])
        return (
            self.part[self.y, self.core].astype(f32)
            + self.rb[self.y].astype(f32)
            + self.r2[0].astype(f32)
            + self.r2[1].astype(f32)
        )

    def drain(self):
        for step in range(4):
            g = self.group(step)
            src = self.part.at[g, self.mate]
            self.link.copy(src, src, self.other, self.first + step).wait_send()


def by_channel(blocks, lane, inverse):
    made = []
    for target in range(8):
        total = jnp.zeros((8, 128), f32)
        for source in range(8):
            for h in range(2):
                if inverse:
                    start, lands = 16 * target + 8 * h, 64 * h + 8 * source
                else:
                    start, lands = 64 * h + 8 * target, 16 * source + 8 * h
                moved = pltpu.roll(blocks[source], (lands - start) % 128, 1)
                total = jnp.where((lane >= lands) & (lane < lands + 8), moved, total)
        made.append(total)
    return made


def block_kernel(
    x_hbm,
    cot_hbm,
    mix_hbm,
    in_hbm,
    tap_hbm,
    proj_hbm,
    ffn_hbm,
    gate_hbm,
    up_hbm,
    down_hbm,
    out_hbm,
    gin_hbm,
    gff_hbm,
    gwin_hbm,
    gwout_hbm,
    gpack_hbm,
    x_ref,
    cot_ref,
    mix_ref,
    in_ref,
    tap_ref,
    proj_ref,
    ffn_ref,
    gate_ref,
    up_ref,
    down_ref,
    out_ref,
    gin_ref,
    gff_ref,
    gwin_ref,
    gwout_ref,
    gpack_ref,
    local_sems,
    send_sems,
    recv_sems,
    win_ref,
    pack_ref,
    xg,
    cotg,
    h2g,
    dg,
    wf,
    wc,
    pre_in,
    pre_pack,
    w_in,
    wog,
    h1g,
    scale_g,
    proj,
    bx_pad,
    z_buf,
    y_buf,
    y_own,
    dy_buf,
    dy_own,
    hid_buf,
    dgu_buf,
    dz_pad,
    dp_buf,
    mix_acc,
    rs_part,
    rs_rb,
    rs_r1,
    rs_r2,
    gf,
    gc,
    gf_a1,
    gf_a2,
    gf_b1,
    gf_b2,
    gf_a3,
    gf_a4,
    gf_b3,
    gf_b4,
    gc_r1,
    gc_r2,
    gc_r3,
    gc_r4,
    post_send,
    post_in,
    post_own,
    post_pack,
):
    loads = [
        pltpu.make_async_copy(src, dst, local_sems.at[i])
        for i, (src, dst) in enumerate(
            (
                (x_hbm, x_ref),
                (in_hbm, in_ref),
                (mix_hbm, mix_ref),
                (ffn_hbm, ffn_ref),
                (tap_hbm, tap_ref),
                (proj_hbm, proj_ref),
                (gate_hbm, gate_ref),
                (up_hbm, up_ref),
                (down_hbm, down_ref),
                (cot_hbm, cot_ref),
            )
        )
    ]
    for load in loads:
        load.start()
    f = lax.axis_index("fsdp")
    c = lax.axis_index("ctx")
    z, x = f // 4, lax.rem(f, 4)
    y, core = c // 2, lax.rem(c, 2)
    y_plus, y_minus = (f, ring(y, 1) * 2 + core), (f, ring(y, 3) * 2 + core)
    other = (f, y * 2 + 1 - core)
    x_plus, x_minus = (z * 4 + ring(x, 1), c), (z * 4 + ring(x, 3), c)
    z_plus, z_minus = (ring(z, 1) * 4 + x, c), (ring(z, 3) * 4 + x, c)

    def along_x(step):
        return (z * 4 + ring(x, step), c)

    def along_z(step):
        return (ring(z, step) * 4 + x, c)

    mates = [(f, lax.rem(c + step, 8)) for step in range(1, 8)]

    barrier = pltpu.get_barrier_semaphore()
    rings = [along_x(step) for step in (1, 2, 3)] + [along_z(step) for step in (1, 2, 3)]
    for device in mates + rings:
        pl.semaphore_signal(barrier, inc=1, device_id=device, device_id_type=MESH)

    lane = lax.broadcasted_iota(jnp.int32, (8, 128), 1)
    row = lax.broadcasted_iota(jnp.int32, (8, 128), 0)
    for load in loads[:5]:
        load.wait()
    xg[y, core] = x_ref[0]
    in_rows = in_ref[...].astype(f32)
    for b in range(3):
        blocks = [in_rows[:, 1024 * b + 128 * v : 1024 * b + 128 * v + 128] for v in range(8)]
        for channel, block in enumerate(by_channel(blocks, lane, False)):
            win_ref[channel, :, 128 * b : 128 * b + 128] = block
    pack_ref[...] = jnp.zeros((8, 128), f32)
    pack_ref[0:1, 0:8] = mix_ref[...].astype(f32)
    pack_ref[1:2, 0:8] = ffn_ref[...].astype(f32)
    pack_ref[2:5, 0:8] = tap_ref[...].astype(f32)
    small = pack_ref[...]
    gains = pltpu.roll(small, 64 * lax.rem(f, 2) + 8 * c, 1)
    own_pack = jnp.where(row < 2, gains, pltpu.roll(small, 8 * f, 1))
    pack_ref[...] = own_pack
    pre_in[c] = win_ref[c]
    pl.semaphore_wait(barrier, 13)

    link = Link(send_sems, recv_sems)

    def ctx_gather(buf):
        return CtxGather(link, buf, y, core, y_plus, y_minus, other)

    def ctx_scatter(n, own_first=False):
        return CtxScatter(
            link, rs_part.at[n], rs_rb.at[n], rs_r1.at[n], rs_r2.at[n],
            y, core, y_plus, y_minus, other, own_first,
        )

    def exchange(blocks, landing):
        return [link.send(blocks.at[mate[1]], landing.at[c], mate) for mate in mates]

    def exchanged(handles, landing):
        for step, handle in enumerate(handles):
            link.landed(handle, landing.at[lax.rem(c + 7 - step, 8)])

    def weight_gather(buf, half, low):
        rest = buf.shape[3] - half
        rows = buf.shape[2]
        a, b = pl.ds(0, half), pl.ds(half, rest)

        def rows_of(part):
            return pl.ds(0, rows) if part is None else (pl.ds(0, low), pl.ds(low, rows - low))[part]

        def pair(part):
            return pl.ds(0, 4) if part is None else pl.ds(2 * part, 2)

        return (
            RingGather(link, lambda i, p: buf.at[z, i, rows_of(p), a], x, x_plus, x_minus),
            RingGather(link, lambda i, p: buf.at[i, x, rows_of(p), b], z, z_plus, z_minus),
            RingGather(link, lambda i, p: buf.at[i, pair(p), :, a], z, z_plus, z_minus),
            RingGather(link, lambda i, p: buf.at[pair(p), i, :, b], x, x_plus, x_minus),
        )

    def conv_gather(buf):
        a, b = pl.ds(0, 256), pl.ds(256, 256)
        return (
            DirectGather(link, lambda i, p: buf.at[z, i, :, a], x, along_x),
            DirectGather(link, lambda i, p: buf.at[i, x, :, b], z, along_z),
            DirectGather(link, lambda i, p: buf.at[i, :, :, a], z, along_z),
            DirectGather(link, lambda i, p: buf.at[:, i, :, b], x, along_x),
        )

    def conv_scatter(buf, r1, r2, r3, r4):
        a, b, o = pl.ds(0, 256), pl.ds(256, 128), pl.ds(384, 128)
        rows = pl.ds(0, 64)
        return (
            DirectScatter(link, lambda i, p: buf.at[i, :, :, a], z, along_z, r1),
            DirectScatter(link, lambda i, p: buf.at[:, i, rows, b], x, along_x, r2.at[0]),
            DirectScatter(link, lambda i, p: buf.at[z, i, :, a], x, along_x, r3),
            DirectScatter(link, lambda i, p: buf.at[i, x, rows, b], z, along_z, r4.at[0]),
            DirectScatter(link, lambda i, p: buf.at[:, i, rows, o], x, along_x, r2.at[1]),
            DirectScatter(link, lambda i, p: buf.at[i, x, rows, o], z, along_z, r4.at[1]),
        )

    def weight_scatter(buf, half, low, a1, a2, b1, b2, a3, a4, b3, b4):
        rest = buf.shape[3] - half
        rows = buf.shape[2]
        a, b = pl.ds(0, half), pl.ds(half, rest)

        def rows_of(part):
            return pl.ds(0, rows) if part is None else (pl.ds(0, low), pl.ds(low, rows - low))[part]

        def pair(part):
            return pl.ds(0, 4) if part is None else pl.ds(2 * part, 2)

        cut = (pl.ds(0, low), pl.ds(low, rows - low))
        return (
            RingScatter(link, lambda i, p: buf.at[i, pair(p), :, a], z, z_plus, z_minus,
                        a1.at[0], a1.at[1], a2.at[0], a2.at[1]),
            RingScatter(link, lambda i, p: buf.at[pair(p), i, :, b], x, x_plus, x_minus,
                        b1.at[0], b1.at[1], b2.at[0], b2.at[1]),
            RingScatter(link, lambda i, p: buf.at[z, i, rows_of(p), a], x, x_plus, x_minus,
                        a3.at[cut[0]], a3.at[cut[1]], a4.at[0], a4.at[1]),
            RingScatter(link, lambda i, p: buf.at[i, x, rows_of(p), b], z, z_plus, z_minus,
                        b3.at[cut[0]], b3.at[cut[1]], b4.at[0], b4.at[1]),
        )

    pre = []
    for step, mate in enumerate(mates):
        pre.append(
            (
                link.send(win_ref.at[mate[1]], pre_in.at[c], mate),
                link.send(pack_ref, pre_pack.at[step], mate),
            )
        )
    gather_x = ctx_gather(xg)
    gather_x.start()
    for load in loads[5:]:
        load.wait()
    own = wf.at[z, x]
    own[:, 0:512] = gate_ref[:, 0:512]
    own[:, 512:1024] = up_ref[:, 0:512]
    own[:, 1024:1152] = jnp.concatenate([gate_ref[:, 512:576], up_ref[:, 512:576]], 1)
    own[:, 1152:1792] = jnp.concatenate(
        [down_ref[...], jnp.zeros((64, 64), bf16)], 1
    )
    cotg[y, core] = cot_ref[0]
    out_rows = proj_ref[...].astype(f32)
    wc[z, x, 0:64, 384:512] = jnp.concatenate(
        [out_rows[:, 128 * w : 128 * w + 128] for w in range(8)], 0
    ).astype(bf16)
    wc[z, x, 64:80, 128:512] = jnp.zeros((16, 384), bf16)
    conv_w = conv_gather(wc)
    ffn_w = weight_gather(wf, 896, 32)
    for step, (h_in, h_pack) in enumerate(pre):
        link.landed(h_in, pre_in.at[lax.rem(c + 7 - step, 8)])
        link.landed(h_pack, pre_pack.at[step])
    wc[z, x, 0:64, 0:384] = pre_in[...].reshape(64, 384).astype(bf16)
    summed = own_pack
    for step in range(7):
        summed = summed + pre_pack[step]
    tile = jnp.where(row < 2, summed, own_pack)
    wc[z, x, 64:80, 0:128] = jnp.concatenate([tile, jnp.zeros_like(tile)], 0).astype(bf16)
    conv_w[0].start()
    conv_w[1].start()
    gather_x.forward()
    ffn_w[0].start()
    ffn_w[1].start()
    gather_x.sides()
    conv_w[0].finish()
    conv_w[1].finish()
    conv_w[2].start()
    conv_w[3].start()
    gather_x.across()
    ffn_w[0].forward()
    ffn_w[1].forward()
    gather_x.finish_near()
    gather_x.finish_far()
    gather_cot = ctx_gather(cotg)
    gather_cot.start()
    ffn_w[0].finish()
    ffn_w[1].finish()
    ffn_w[2].start()
    ffn_w[3].start()

    def first_scale(g, carry):
        values = xg[g].reshape(256, 1024).astype(f32)
        scale_g[g] = lax.rsqrt(jnp.mean(values * values, axis=-1, keepdims=True) + epsilon)
        return carry

    lax.fori_loop(0, 4, first_scale, 0)
    conv_w[2].finish()
    conv_w[3].finish()

    packs = [wc[i // 4, i % 4, 64:80, 0:128].astype(f32)[0:8] for i in range(16)]
    gain_one = jnp.concatenate([packs[2 * w][0:1] + packs[2 * w + 1][0:1] for w in range(8)], 1)
    gain_two = jnp.concatenate([packs[2 * w][1:2] + packs[2 * w + 1][1:2] for w in range(8)], 1)
    taps = packs[0]
    for i in range(1, 16):
        taps = taps + packs[i]
    tap = [taps[2 + k : 3 + k] for k in range(3)]
    w_in[...] = wc[:, :, 0:64, 0:384].reshape(1024, 384)
    slab = wc[:, :, 0:64, 384:512].astype(f32).reshape(16, 8, 8, 128)
    for w in range(8):
        wog[y, core, :, 128 * w : 128 * w + 128] = slab[:, w].reshape(128, 128).astype(bf16)
    gather_out = ctx_gather(wog)
    gather_out.start()

    def project(g, carry):
        values = xg[g].reshape(256, 1024).astype(f32)
        lifted = (values * scale_g[g] * gain_one).astype(bf16)
        h1g[g] = lifted
        proj[g] = mm(lifted, w_in[...])
        return carry

    lax.fori_loop(0, 4, project, 0)
    b_part = proj[:, :, 0:128].reshape(1024, 128)
    x_part = proj[:, :, 256:384].reshape(1024, 128)
    bx_pad[0:8] = jnp.zeros((8, 128), f32)
    bx_pad[8:1032] = (b_part * x_part).astype(bf16).astype(f32)
    z_all = tap[0] * bx_pad[6:1030] + tap[1] * bx_pad[7:1031] + tap[2] * bx_pad[8:1032]
    z_buf[...] = z_all
    y_buf[...] = (proj[:, :, 128:256].reshape(1024, 128) * z_all).astype(bf16).reshape(8, 128, 128)
    swap_y = exchange(y_buf, y_own)
    y_own[c] = y_buf[c]
    gather_cot.forward()
    gather_out.forward()
    gather_cot.sides()
    gather_out.sides()
    gather_cot.across()
    gather_out.across()
    ffn_w[2].forward()
    ffn_w[3].forward()
    exchanged(swap_y, y_own)
    gather_out.finish_near()
    gather_out.finish_far()
    gated = jnp.concatenate([y_own[i] for i in range(8)], 1)
    middle = x_ref[0].astype(f32) + mm(gated, wog[...].reshape(1024, 1024))
    scale_two = lax.rsqrt(jnp.mean(middle * middle, axis=-1, keepdims=True) + epsilon)
    h2g[y, core] = (middle * scale_two * gain_two).astype(bf16)
    gather_h2 = ctx_gather(h2g)
    gather_h2.start()
    gather_cot.finish_near()
    gather_cot.finish_far()
    ffn_w[2].finish()
    ffn_w[3].finish()
    gather_h2.finish_near()

    scatter_dh2 = ctx_scatter(0, own_first=True)
    low_half = lax.broadcasted_iota(jnp.int32, (256, 128), 1) < 64

    def feed_forward(step, carry):
        g = scatter_dh2.group(step)

        @pl.when(step == 1)
        def _():
            gather_h2.forward()
            gather_h2.sides()
            gather_h2.across()
            gather_h2.finish_far()

        @pl.when(step == 2)
        def _():
            scatter_dh2.start()

        w_gu = wf[:, :, :, 0:GU].reshape(1024, GU)
        gu = mm(h2g[g].reshape(256, 1024), w_gu)
        mixed = gu[:, 1024:1152]
        gating = jnp.concatenate([gu[:, 0:512], mixed], 1)
        upward = jnp.concatenate([gu[:, 512:1024], pltpu.roll(mixed, 64, 1)], 1)
        sigma = 1.0 / (1.0 + jnp.exp(-gating))
        activated = gating * sigma
        hidden = activated * upward
        hid_buf[g, :, 0:512] = hidden[:, 0:512].astype(bf16)
        hid_buf[g, :, 512:640] = jnp.where(low_half, hidden[:, 512:640], 0.0).astype(bf16)
        w_down = wf[:, :, :, GU:FFL].reshape(1024, HID)
        d_hidden = mm(cotg[g].reshape(256, 1024), w_down)
        d_gating = d_hidden * upward * sigma * (1.0 + gating * (1.0 - sigma))
        d_upward = d_hidden * activated
        d_mixed = jnp.where(low_half, d_gating[:, 512:640], pltpu.roll(d_upward[:, 512:640], 64, 1))
        d_gu = jnp.concatenate([d_gating[:, 0:512], d_upward[:, 0:512], d_mixed], 1).astype(bf16)
        dgu_buf[g] = d_gu
        rs_part[0, g] = mt(d_gu, w_gu).astype(bf16).reshape(2, 128, 1024)
        scatter_dh2.cross(step)
        return carry

    lax.fori_loop(0, 4, feed_forward, 0)
    scatter_dh2.sides()
    scatter_out = ctx_scatter(1)

    def ffn_out(step, carry):
        g = scatter_out.group(step)
        w_down = wf[:, :, :, GU:FFL].reshape(1024, HID)
        rs_part[1, g] = mt(hid_buf[g], w_down).astype(bf16).reshape(2, 128, 1024)
        scatter_out.cross(step)
        return carry

    lax.fori_loop(0, 4, ffn_out, 0)
    scatter_dh2.middle()
    scatter_out.start()
    scatter_out.sides()

    def grad_ffn(i, carry):
        lanes = pl.ds(pl.multiple_of(i * 256, 256), 256)
        lhs = h2g[:, :, :, lanes].reshape(1024, 256)
        gf[i, :, :, 0:GU] = tm(lhs, dgu_buf[...].reshape(1024, GU)).astype(bf16).reshape(4, 64, GU)
        lhs = cotg[:, :, :, lanes].reshape(1024, 256)
        gf[i, :, :, GU:FFL] = (
            tm(lhs, hid_buf[...].reshape(1024, HID)).astype(bf16).reshape(4, 64, HID)
        )
        return carry

    lax.fori_loop(0, 4, grad_ffn, 0)
    ffn_g = weight_scatter(gf, 896, 32, gf_a1, gf_a2, gf_b1, gf_b2, gf_a3, gf_a4, gf_b3, gf_b4)
    ffn_g[0].start()
    ffn_g[1].start()

    d_second = scatter_dh2.finish()
    normed_two = middle * scale_two
    grad_gain_two = jnp.sum(d_second * normed_two, axis=0, keepdims=True)
    scaled = d_second * gain_two
    d_middle = cot_ref[0].astype(f32) + scale_two * (
        scaled - normed_two * jnp.mean(scaled * normed_two, axis=-1, keepdims=True)
    )
    d_branch = d_middle.astype(bf16)
    dg[y, core] = d_branch
    d_gated = mt(d_branch, wog[...].reshape(1024, 1024)).astype(bf16)
    for i in range(8):
        dy_buf[i] = d_gated[:, 128 * i : 128 * i + 128]
    swap_dy = exchange(dy_buf, dy_own)
    gather_d = ctx_gather(dg)
    gather_d.start()
    dy_own[c] = dy_buf[c]
    ffn_g[0].middle()
    ffn_g[1].middle()
    exchanged(swap_dy, dy_own)

    d_gated = dy_own[...].reshape(1024, 128).astype(f32)
    dz_pad[0:1024] = d_gated * proj[:, :, 128:256].reshape(1024, 128)
    dp_buf[:, :, 128:256] = (d_gated * z_buf[...]).astype(bf16).reshape(4, 256, 128)
    dz_pad[1024:1032] = jnp.zeros((8, 128), f32)
    d_bx = tap[2] * dz_pad[0:1024] + tap[1] * dz_pad[1:1025] + tap[0] * dz_pad[2:1026]
    d_bx = d_bx.reshape(4, 256, 128)
    dp_buf[:, :, 0:128] = (d_bx * proj[:, :, 256:384]).astype(bf16)
    dp_buf[:, :, 256:384] = (d_bx * proj[:, :, 0:128]).astype(bf16)
    grad_tap = [
        jnp.sum(dz_pad[0:1024] * bx_pad[6 + k : 1030 + k], axis=0, keepdims=True) for k in range(3)
    ]
    gather_d.forward()
    gather_d.sides()

    scatter_dh1 = ctx_scatter(2)
    mix_acc[...] = jnp.zeros((8, 1024), f32)

    def branch_back(step, carry):
        g = scatter_dh1.group(step)
        d_lifted = mt(dp_buf[g], w_in[...])
        rs_part[2, g] = d_lifted.astype(bf16).reshape(2, 128, 1024)
        scatter_dh1.cross(step)
        normed = xg[g].reshape(256, 1024).astype(f32) * scale_g[g]
        mix_acc[...] += jnp.sum((d_lifted * normed).reshape(32, 8, 1024), axis=0)
        return carry

    lax.fori_loop(0, 4, branch_back, 0)
    scatter_dh1.start()
    scatter_dh1.sides()

    def grad_in(i, carry):
        lanes = pl.ds(pl.multiple_of(i * 256, 256), 256)
        lhs = h1g[:, :, lanes].reshape(1024, 256)
        gc[i, :, 0:64, 0:384] = (
            tm(lhs, dp_buf[...].reshape(1024, 384)).astype(bf16).reshape(4, 64, 384)
        )
        return carry

    lax.fori_loop(0, 4, grad_in, 0)
    grad_mix = jnp.sum(mix_acc[...], axis=0, keepdims=True)
    gc[:, :, 64:80, 128:512] = jnp.zeros((4, 4, 16, 384), bf16)
    for i in range(16):
        lanes = slice(128 * (i // 2), 128 * (i // 2) + 128)
        rows = [grad_mix[:, lanes], grad_gain_two[:, lanes], *grad_tap, jnp.zeros((11, 128), f32)]
        gc[i // 4, i % 4, 64:80, 0:128] = jnp.concatenate(rows, 0).astype(bf16)
    conv_g = conv_scatter(gc, gc_r1, gc_r2, gc_r3, gc_r4)
    for part in conv_g[0:2]:
        part.start()
    scatter_dh1.middle()
    gather_d.across()
    gather_d.finish_near()
    gather_d.finish_far()
    g_out = tm(y_buf[...].reshape(1024, 128), dg[...].reshape(1024, 1024))
    pieces = [g_out[:, 128 * w : 128 * w + 128].reshape(16, 1, 8, 128) for w in range(8)]
    g_slab = jnp.concatenate(pieces, 1).reshape(4, 4, 64, 128)
    gc[:, :, 0:64, 384:512] = g_slab.astype(bf16)
    conv_g[4].start()
    ffn_g[0].finish()
    ffn_g[1].finish()
    ffn_g[2].start()
    ffn_g[3].start()
    for part in conv_g[0:2]:
        part.finish()
    for part in conv_g[2:4]:
        part.start()
    scatter_out.middle()
    conv_g[4].finish()
    conv_g[5].start()

    d_lifted = scatter_dh1.finish()
    local = x_ref[0].astype(f32)
    scale_one = lax.rsqrt(jnp.mean(local * local, axis=-1, keepdims=True) + epsilon)
    normed_one = local * scale_one
    scaled = d_lifted * gain_one
    gin_ref[...] = d_middle + scale_one * (
        scaled - normed_one * jnp.mean(scaled * normed_one, axis=-1, keepdims=True)
    )
    stores = [
        pltpu.make_async_copy(src, dst, local_sems.at[10 + i])
        for i, (src, dst) in enumerate(
            (
                (gin_ref, gin_hbm),
                (gff_ref, gff_hbm),
                (out_ref, out_hbm),
                (gwout_ref, gwout_hbm),
                (gwin_ref, gwin_hbm),
                (gpack_ref, gpack_hbm),
            )
        )
    ]
    stores[0].start()
    ffn_g[2].middle()
    ffn_g[3].middle()
    for part in conv_g[2:4]:
        part.finish()

    total = gc[z, x, :, 0:384].astype(f32)
    post_send[...] = total[0:64].reshape(8, 8, 384)
    post_own[...] = total[64:72, 0:128]
    post = []
    for step, mate in enumerate(mates):
        post.append(
            (
                link.send(post_send.at[mate[1]], post_in.at[c], mate),
                link.send(post_own, post_pack.at[step], mate),
            )
        )
    ffn_g[2].finish()
    ffn_g[3].finish()
    gff_ref[...] = gf[z, x].astype(f32)
    stores[1].start()
    out_ref[...] = (middle + scatter_out.finish()).astype(bf16)
    stores[2].start()
    conv_g[5].finish()
    gwout_ref[...] = gc[z, x, 0:64, 384:512].astype(f32)
    stores[3].start()
    post_in[c] = post_send[c]
    summed = post_own[...]
    for step, (h_in, h_pack) in enumerate(post):
        link.landed(h_in, post_in.at[lax.rem(c + 7 - step, 8)])
        link.landed(h_pack, post_pack.at[step])
        summed = summed + post_pack[step]
    gwin_ref[...] = post_in[...]
    gpack_ref[...] = jnp.where(row < 2, summed, post_own[...])
    stores[4].start()
    stores[5].start()
    for store in stores:
        store.wait()

    link.drain()
    for scatter in (scatter_dh2, scatter_out, scatter_dh1):
        scatter.drain()


def spread_kernel(
    block_ref,
    gin_ref,
    gff_ref,
    gwin_ref,
    gwout_ref,
    gpack_ref,
    o_block,
    o_gin,
    o_mix,
    o_in,
    o_tap,
    o_proj,
    o_ffn,
    o_gate,
    o_up,
    o_down,
):
    f = lax.axis_index("fsdp")
    c = lax.axis_index("ctx")
    lane = lax.broadcasted_iota(jnp.int32, (8, 128), 1)
    o_block[0] = block_ref[...]
    o_gin[0] = gin_ref[...]
    for b in range(3):
        blocks = [gwin_ref[i, :, 128 * b : 128 * b + 128] for i in range(8)]
        for v, block in enumerate(by_channel(blocks, lane, True)):
            o_in[:, 1024 * b + 128 * v : 1024 * b + 128 * v + 128] = block
    for w in range(8):
        o_proj[:, 128 * w : 128 * w + 128] = gwout_ref[8 * w : 8 * w + 8]
    small = gpack_ref[...]
    gains = pltpu.roll(small, lax.rem(256 - 64 * lax.rem(f, 2) - 8 * c, 128), 1)
    o_mix[...] = gains[0:1, 0:8]
    o_ffn[...] = gains[1:2, 0:8]
    o_tap[...] = pltpu.roll(small, lax.rem(128 - 8 * f, 128), 1)[2:5, 0:8]
    mixed = gff_ref[:, 1024:1152]
    o_gate[:, 0:512] = gff_ref[:, 0:512]
    o_gate[:, 512:576] = mixed[:, 0:64]
    o_up[:, 0:512] = gff_ref[:, 512:1024]
    o_up[:, 512:576] = pltpu.roll(mixed, 64, 1)[:, 0:64]
    o_down[...] = gff_ref[:, 1152:1728]


def per_device(
    inputs,
    mix_gain,
    in_proj,
    conv_kernel,
    out_proj,
    ffn_gain,
    gate_proj,
    up_proj,
    down_proj,
    cotangent,
):
    v = pltpu.VMEM
    anywhere = pl.BlockSpec(memory_space=pl.ANY)
    sems = 256
    out_shape = (
        jax.ShapeDtypeStruct((128, 1024), bf16),
        jax.ShapeDtypeStruct((128, 1024), f32),
        jax.ShapeDtypeStruct((64, FFL), f32),
        jax.ShapeDtypeStruct((8, 8, 384), f32),
        jax.ShapeDtypeStruct((64, 128), f32),
        jax.ShapeDtypeStruct((8, 128), f32),
    )
    scratch = [
        v(inputs.shape, bf16),
        v(cotangent.shape, bf16),
        v((1, 8), bf16),
        v(in_proj.shape, bf16),
        v(conv_kernel.shape, bf16),
        v(out_proj.shape, bf16),
        v((1, 8), bf16),
        v(gate_proj.shape, bf16),
        v(up_proj.shape, bf16),
        v(down_proj.shape[::-1], bf16),
        *[v(shape.shape, shape.dtype) for shape in out_shape],
        pltpu.SemaphoreType.DMA((16,)),
        pltpu.SemaphoreType.DMA((sems,)),
        pltpu.SemaphoreType.DMA((sems,)),
        v((8, 8, 384), f32),
        v((8, 128), f32),
        v((4, 2, 128, 1024), bf16),
        v((4, 2, 128, 1024), bf16),
        v((4, 2, 128, 1024), bf16),
        v((4, 2, 128, 1024), bf16),
        v((4, 4, 64, FFL), bf16),
        v((4, 4, CR, CL), bf16),
        v((8, 8, 384), f32),
        v((7, 8, 128), f32),
        v((1024, 384), bf16),
        v((4, 2, 128, 1024), bf16),
        v((4, 256, 1024), bf16),
        v((4, 256, 1), f32),
        v((4, 256, 384), f32),
        v((1032, 128), f32),
        v((1024, 128), f32),
        v((8, 128, 128), bf16),
        v((8, 128, 128), bf16),
        v((8, 128, 128), bf16),
        v((8, 128, 128), bf16),
        v((4, 256, HID), bf16),
        v((4, 256, GU), bf16),
        v((1032, 128), f32),
        v((4, 256, 384), bf16),
        v((8, 1024), f32),
        v((3, 4, 2, 128, 1024), bf16),
        v((3, 4, 128, 1024), bf16),
        v((3, 2, 64, 1024), bf16),
        v((3, 2, 128, 1024), bf16),
        v((4, 4, 64, FFL), bf16),
        v((4, 4, CR, CL), bf16),
        v((2, 2, 64, 896), bf16),
        v((2, 4, 64, 896), bf16),
        v((2, 2, 64, 896), bf16),
        v((2, 4, 64, 896), bf16),
        v((64, 896), bf16),
        v((2, 64, 896), bf16),
        v((64, 896), bf16),
        v((2, 64, 896), bf16),
        v((3, 4, CR, 256), bf16),
        v((2, 3, 4, 64, 128), bf16),
        v((3, CR, 256), bf16),
        v((2, 3, 64, 128), bf16),
        v((8, 8, 384), f32),
        v((8, 8, 384), f32),
        v((8, 128), f32),
        v((7, 8, 128), f32),
    ]
    raw = pl.pallas_call(
        block_kernel,
        out_shape=out_shape,
        in_specs=[anywhere] * 10,
        out_specs=(anywhere,) * 6,
        scratch_shapes=scratch,
        compiler_params=pltpu.CompilerParams(
            collective_id=0, has_side_effects=True, vmem_limit_bytes=62 * 1024 * 1024
        ),
    )(
        inputs,
        cotangent,
        mix_gain.reshape(1, 8),
        in_proj,
        conv_kernel,
        out_proj,
        ffn_gain.reshape(1, 8),
        gate_proj,
        up_proj,
        down_proj.T,
    )
    made = pl.pallas_call(
        spread_kernel,
        out_shape=(
            jax.ShapeDtypeStruct(inputs.shape, bf16),
            jax.ShapeDtypeStruct(inputs.shape, f32),
            jax.ShapeDtypeStruct((1, 8), f32),
            jax.ShapeDtypeStruct(in_proj.shape, f32),
            jax.ShapeDtypeStruct(conv_kernel.shape, f32),
            jax.ShapeDtypeStruct(out_proj.shape, f32),
            jax.ShapeDtypeStruct((1, 8), f32),
            jax.ShapeDtypeStruct(gate_proj.shape, f32),
            jax.ShapeDtypeStruct(up_proj.shape, f32),
            jax.ShapeDtypeStruct(down_proj.shape[::-1], f32),
        ),
        grid=(1,),
        compiler_params=pltpu.CompilerParams(vmem_limit_bytes=16 * 1024 * 1024),
    )(*raw)
    return (*made[:2], made[2].reshape(8), *made[3:6], made[6].reshape(8), *made[7:9], made[9].T)


def solution(mesh):
    in_specs = (
        P("fsdp", "ctx", None),
        P(("fsdp", "ctx")),
        P(("fsdp", "ctx"), None),
        P(None, ("fsdp", "ctx")),
        P(("fsdp", "ctx"), None),
        P(("fsdp", "ctx")),
        P("fsdp", "ctx"),
        P("fsdp", "ctx"),
        P("ctx", "fsdp"),
        P("fsdp", "ctx", None),
    )
    out_specs = (
        P("fsdp", "ctx", None),
        P("fsdp", "ctx", None),
        P(("fsdp", "ctx")),
        P(("fsdp", "ctx"), None),
        P(None, ("fsdp", "ctx")),
        P(("fsdp", "ctx"), None),
        P(("fsdp", "ctx")),
        P("fsdp", "ctx"),
        P("fsdp", "ctx"),
        P("ctx", "fsdp"),
    )
    return jax.shard_map(
        per_device, mesh=mesh, in_specs=in_specs, out_specs=out_specs, check_vma=False
    )
```

```python
import jax
import jax.numpy as jnp
from jax import lax
from jax.experimental import pallas as pl
from jax.experimental.pallas import tpu as pltpu
from jax.sharding import PartitionSpec as P

epsilon = 1e-05
f32 = jnp.float32
bf16 = jnp.bfloat16
MESH = pl.DeviceIdType.MESH

GU = 1152
FFL = 1792
HID = 640


def mm(a, b):
    return lax.dot_general(a, b, (((1,), (0,)), ((), ())), preferred_element_type=f32)


def mt(a, b):
    return lax.dot_general(a, b, (((1,), (1,)), ((), ())), preferred_element_type=f32)


def tm(a, b):
    return lax.dot_general(a, b, (((0,), (0,)), ((), ())), preferred_element_type=f32)


def add_into(ref, *others):
    total = ref[...].astype(f32)
    for other in others:
        total = total + other[...].astype(f32)
    ref[...] = total.astype(ref.dtype)


class Link:
    def __init__(self, send_sems, recv_sems):
        self.send_sems, self.recv_sems = send_sems, recv_sems
        self.used = 0
        self.started = []

    def reserve(self, count):
        first = self.used
        self.used += count
        return first

    def copy(self, src, dst, device, slot):
        return pltpu.make_async_remote_copy(
            src_ref=src,
            dst_ref=dst,
            send_sem=self.send_sems.at[slot],
            recv_sem=self.recv_sems.at[slot],
            device_id=device,
            device_id_type=MESH,
        )

    def send(self, src, dst, device):
        slot = self.reserve(1)
        self.copy(src, dst, device, slot).start()
        self.started.append((src, device, slot))
        return (device, slot)

    def landed(self, handle, ref):
        device, slot = handle
        self.copy(ref, ref, device, slot).wait_recv()

    def drain(self):
        for src, device, slot in self.started:
            self.copy(src, src, device, slot).wait_send()


def ring(value, step):
    return lax.rem(value + step, 4)


class RingGather:
    def __init__(self, link, view, me, plus, minus):
        self.link, self.view, self.me, self.plus, self.minus = link, view, me, plus, minus
        self.left, self.far, self.right = ring(me, 3), ring(me, 2), ring(me, 1)

    def start(self):
        send = self.link.send
        lo, hi = self.view(self.me, 0), self.view(self.me, 1)
        self.p0, self.m1 = send(lo, lo, self.plus), send(hi, hi, self.minus)
        self.p1, self.m0 = send(hi, hi, self.plus), send(lo, lo, self.minus)

    def forward(self):
        part = self.view(self.left, 0)
        self.link.landed(self.p0, part)
        self.fp = self.link.send(part, part, self.plus)
        part = self.view(self.right, 1)
        self.link.landed(self.m1, part)
        self.fm = self.link.send(part, part, self.minus)

    def finish(self):
        self.link.landed(self.p1, self.view(self.left, 1))
        self.link.landed(self.m0, self.view(self.right, 0))
        self.link.landed(self.fp, self.view(self.far, 0))
        self.link.landed(self.fm, self.view(self.far, 1))


class RingScatter:
    def __init__(self, link, view, me, plus, minus, r1a, r1b, r2a, r2b):
        self.link, self.view, self.me, self.plus, self.minus = link, view, me, plus, minus
        self.r1a, self.r1b, self.r2a, self.r2b = r1a, r1b, r2a, r2b
        self.left, self.far, self.right = ring(me, 3), ring(me, 2), ring(me, 1)

    def start(self):
        send = self.link.send
        self.h1a = send(self.view(self.far, 0), self.r1a, self.plus)
        self.h1b = send(self.view(self.far, 1), self.r1b, self.minus)
        self.h2a1 = send(self.view(self.right, 1), self.r2a[1], self.plus)
        self.h2b0 = send(self.view(self.left, 0), self.r2b[0], self.minus)

    def middle(self):
        self.link.landed(self.h1a, self.r1a)
        add_into(self.view(self.right, 0), self.r1a)
        self.h2a0 = self.link.send(self.view(self.right, 0), self.r2a[0], self.plus)
        self.link.landed(self.h1b, self.r1b)
        add_into(self.view(self.left, 1), self.r1b)
        self.h2b1 = self.link.send(self.view(self.left, 1), self.r2b[1], self.minus)

    def finish(self):
        self.link.landed(self.h2a1, self.r2a[1])
        self.link.landed(self.h2b0, self.r2b[0])
        self.link.landed(self.h2a0, self.r2a[0])
        self.link.landed(self.h2b1, self.r2b[1])
        for part in (0, 1):
            add_into(self.view(self.me, part), self.r2a[part], self.r2b[part])


class DirectGather:
    def __init__(self, link, view, me, device):
        self.link, self.view, self.me, self.device = link, view, me, device

    def start(self):
        own = self.view(self.me, None)
        self.sent = [(s, self.link.send(own, own, self.device(s))) for s in (1, 3, 2)]

    def finish(self):
        for step, handle in self.sent:
            self.link.landed(handle, self.view(ring(self.me, 4 - step), None))


class DirectScatter:
    def __init__(self, link, view, me, device, landing):
        self.link, self.view, self.me, self.device, self.landing = link, view, me, device, landing

    def start(self):
        self.sent = [
            (s, self.link.send(self.view(ring(self.me, s), None), self.landing.at[s - 1], self.device(s)))
            for s in (1, 3, 2)
        ]

    def finish(self):
        for step, handle in self.sent:
            self.link.landed(handle, self.landing.at[step - 1])
        add_into(self.view(self.me, None), *[self.landing.at[i] for i in range(3)])


LO, HI = pl.ds(0, 64), pl.ds(64, 64)


class CtxGather:
    def __init__(self, link, buf, y, core, plus, minus, other):
        self.link, self.buf, self.y, self.core = link, buf, y, core
        self.plus, self.minus, self.other = plus, minus, other
        self.left, self.far, self.right = ring(y, 3), ring(y, 2), ring(y, 1)
        self.mate = 1 - core

    def half(self, which, part):
        return self.buf.at[which, self.core, (LO, HI)[part]]

    def start(self):
        send = self.link.send
        lo, hi = self.half(self.y, 0), self.half(self.y, 1)
        own = self.buf.at[self.y, self.core]
        self.p0, self.m1 = send(lo, lo, self.plus), send(hi, hi, self.minus)
        self.p1, self.m0 = send(hi, hi, self.plus), send(lo, lo, self.minus)
        self.near = send(own, own, self.other)
        self.late = []

    def pass_on(self, handle, which, part, device):
        half = self.half(which, part)
        self.link.landed(handle, half)
        onward = None if device is None else self.link.send(half, half, device)
        theirs = self.buf.at[which, self.mate, (LO, HI)[part]]
        self.late.append((self.link.send(half, half, self.other), theirs))
        return onward

    def forward(self):
        left, right = self.left, self.right
        self.fp = self.pass_on(self.p0, left, 0, self.plus)
        self.fm = self.pass_on(self.m1, right, 1, self.minus)

    def sides(self):
        self.pass_on(self.p1, self.left, 1, None)
        self.pass_on(self.m0, self.right, 0, None)

    def across(self):
        far = self.far
        self.pass_on(self.fp, far, 0, None)
        self.pass_on(self.fm, far, 1, None)

    def finish_near(self):
        self.link.landed(self.near, self.buf.at[self.y, self.mate])

    def finish_sides(self):
        for handle, ref in self.late[:4]:
            self.link.landed(handle, ref)

    def finish_far(self):
        for handle, ref in self.late[4:]:
            self.link.landed(handle, ref)


class CtxScatter:
    def __init__(self, link, part, rb, r1, r2, y, core, plus, minus, other, own_first):
        self.link, self.part, self.rb, self.r1, self.r2 = link, part, rb, r1, r2
        self.y, self.core, self.own_first = y, core, own_first
        self.plus, self.minus, self.other = plus, minus, other
        self.left, self.far, self.right = ring(y, 3), ring(y, 2), ring(y, 1)
        self.mate = 1 - core
        self.first = link.reserve(4)
        self.at_far, self.at_left, self.at_right, self.at_own = (2, 1, 3, 0) if own_first else (0, 1, 2, 3)

    def group(self, step):
        if self.own_first:
            return lax.rem(self.y + 3 * step, 4)
        return lax.rem(self.y + 2 + step + step // 2 + 2 * (step // 3), 4)

    def cross(self, step):
        g = self.group(step)
        self.link.copy(
            self.part.at[g, self.mate], self.rb.at[g], self.other, self.first + step
        ).start()

    def crossed(self, g, step):
        ref = self.rb.at[g]
        self.link.copy(ref, ref, self.other, self.first + step).wait_recv()

    def block(self, which, rows):
        return self.part.at[which, self.core, rows]

    def start(self):
        far = self.far
        self.crossed(far, self.at_far)
        add_into(self.block(far, LO), self.rb.at[far, LO])
        self.h1a = self.link.send(self.block(far, LO), self.r1.at[0], self.plus)
        add_into(self.block(far, HI), self.rb.at[far, HI])
        self.h1b = self.link.send(self.block(far, HI), self.r1.at[1], self.minus)

    def side_left(self):
        left = self.left
        self.crossed(left, self.at_left)
        add_into(self.block(left, LO), self.rb.at[left, LO])
        self.h2b0 = self.link.send(self.block(left, LO), self.r2.at[1, LO], self.minus)

    def side_right(self):
        right = self.right
        self.crossed(right, self.at_right)
        add_into(self.block(right, HI), self.rb.at[right, HI])
        self.h2a1 = self.link.send(self.block(right, HI), self.r2.at[0, HI], self.plus)

    def middle(self):
        left, right = self.left, self.right
        self.link.landed(self.h1a, self.r1.at[0])
        add_into(self.block(right, LO), self.rb.at[right, LO], self.r1.at[0])
        self.h2a0 = self.link.send(self.block(right, LO), self.r2.at[0, LO], self.plus)
        self.link.landed(self.h1b, self.r1.at[1])
        add_into(self.block(left, HI), self.rb.at[left, HI], self.r1.at[1])
        self.h2b1 = self.link.send(self.block(left, HI), self.r2.at[1, HI], self.minus)

    def finish(self):
        self.crossed(self.y, self.at_own)
        self.link.landed(self.h2b0, self.r2.at[1, LO])
        self.link.landed(self.h2a1, self.r2.at[0, HI])
        self.link.landed(self.h2a0, self.r2.at[0, LO])
        self.link.landed(self.h2b1, self.r2.at[1, HI])
        return (
            self.part[self.y, self.core].astype(f32)
            + self.rb[self.y].astype(f32)
            + self.r2[0].astype(f32)
            + self.r2[1].astype(f32)
        )

    def drain(self):
        for step in range(4):
            g = self.group(step)
            src = self.part.at[g, self.mate]
            self.link.copy(src, src, self.other, self.first + step).wait_send()


def by_channel(blocks, lane, inverse):
    made = []
    for target in range(8):
        total = jnp.zeros((8, 128), f32)
        for source in range(8):
            for h in range(2):
                if inverse:
                    start, lands = 16 * target + 8 * h, 64 * h + 8 * source
                else:
                    start, lands = 64 * h + 8 * target, 16 * source + 8 * h
                moved = pltpu.roll(blocks[source], (lands - start) % 128, 1)
                total = jnp.where((lane >= lands) & (lane < lands + 8), moved, total)
        made.append(total)
    return made


def block_kernel(
    x_hbm,
    cot_hbm,
    mix_hbm,
    in_hbm,
    tap_hbm,
    proj_hbm,
    ffn_hbm,
    gate_hbm,
    up_hbm,
    down_hbm,
    out_hbm,
    gin_hbm,
    gff_hbm,
    gwin_hbm,
    gwout_hbm,
    gpack_hbm,
    x_ref,
    cot_ref,
    mix_ref,
    in_ref,
    tap_ref,
    proj_ref,
    ffn_ref,
    gate_ref,
    up_ref,
    down_ref,
    out_ref,
    gin_ref,
    gff_ref,
    gwin_ref,
    gwout_ref,
    gpack_ref,
    local_sems,
    send_sems,
    recv_sems,
    win_ref,
    pack_ref,
    xg,
    cotg,
    h2g,
    dg,
    wf,
    wi,
    wp,
    wo,
    pre_in,
    pre_pack,
    wog,
    h1g,
    scale_g,
    proj,
    bx_pad,
    z_buf,
    y_buf,
    y_own,
    dy_buf,
    dy_own,
    hid_buf,
    dgu_buf,
    dz_pad,
    dp_buf,
    mix_acc,
    rs_part,
    rs_rb,
    rs_r1,
    rs_r2,
    gf,
    gi,
    gp,
    go,
    gf_a1,
    gf_a2,
    gf_b1,
    gf_b2,
    gf_a3,
    gf_a4,
    gf_b3,
    gf_b4,
    gi_r1,
    gi_r2,
    gp_r1,
    gp_r2,
    go_r1,
    go_r2,
    post_send,
    post_in,
    post_own,
    post_pack,
):
    loads = [
        pltpu.make_async_copy(src, dst, local_sems.at[i])
        for i, (src, dst) in enumerate(
            (
                (x_hbm, x_ref),
                (in_hbm, in_ref),
                (mix_hbm, mix_ref),
                (ffn_hbm, ffn_ref),
                (tap_hbm, tap_ref),
                (proj_hbm, proj_ref),
                (gate_hbm, gate_ref),
                (up_hbm, up_ref),
                (down_hbm, down_ref),
                (cot_hbm, cot_ref),
            )
        )
    ]
    for load in loads:
        load.start()
    f = lax.axis_index("fsdp")
    c = lax.axis_index("ctx")
    z, x = f // 4, lax.rem(f, 4)
    y, core = c // 2, lax.rem(c, 2)
    y_plus, y_minus = (f, ring(y, 1) * 2 + core), (f, ring(y, 3) * 2 + core)
    other = (f, y * 2 + 1 - core)
    x_plus, x_minus = (z * 4 + ring(x, 1), c), (z * 4 + ring(x, 3), c)
    z_plus, z_minus = (ring(z, 1) * 4 + x, c), (ring(z, 3) * 4 + x, c)

    def along_x(step):
        return (z * 4 + ring(x, step), c)

    def along_z(step):
        return (ring(z, step) * 4 + x, c)

    mates = [(f, lax.rem(c + step, 8)) for step in range(1, 8)]

    barrier = pltpu.get_barrier_semaphore()
    rings = [along_x(step) for step in (1, 2, 3)] + [along_z(step) for step in (1, 2, 3)]
    for device in mates + rings:
        pl.semaphore_signal(barrier, inc=1, device_id=device, device_id_type=MESH)

    lane = lax.broadcasted_iota(jnp.int32, (8, 128), 1)
    row = lax.broadcasted_iota(jnp.int32, (8, 128), 0)
    for load in loads[:5]:
        load.wait()
    xg[y, core] = x_ref[0]
    in_rows = in_ref[...].astype(f32)
    for b in range(3):
        blocks = [in_rows[:, 1024 * b + 128 * v : 1024 * b + 128 * v + 128] for v in range(8)]
        for channel, block in enumerate(by_channel(blocks, lane, False)):
            win_ref[channel, :, 128 * b : 128 * b + 128] = block
    pack_ref[...] = jnp.zeros((8, 128), f32)
    pack_ref[0:1, 0:8] = mix_ref[...].astype(f32)
    pack_ref[1:2, 0:8] = ffn_ref[...].astype(f32)
    pack_ref[2:5, 0:8] = tap_ref[...].astype(f32)
    small = pack_ref[...]
    gains = pltpu.roll(small, 64 * lax.rem(f, 2) + 8 * c, 1)
    own_pack = jnp.where(row < 2, gains, pltpu.roll(small, 8 * f, 1))
    pack_ref[...] = own_pack
    pre_in[c] = win_ref[c]
    pl.semaphore_wait(barrier, 13)

    link = Link(send_sems, recv_sems)

    def ctx_gather(buf):
        return CtxGather(link, buf, y, core, y_plus, y_minus, other)

    def ctx_scatter(n, own_first=False):
        return CtxScatter(
            link, rs_part.at[n], rs_rb.at[n], rs_r1.at[n], rs_r2.at[n],
            y, core, y_plus, y_minus, other, own_first,
        )

    def exchange(blocks, landing):
        return [link.send(blocks.at[mate[1]], landing.at[c], mate) for mate in mates]

    def exchanged(handles, landing):
        for step, handle in enumerate(handles):
            link.landed(handle, landing.at[lax.rem(c + 7 - step, 8)])

    def weight_gather(buf, half, low):
        rest = buf.shape[3] - half
        rows = buf.shape[2]
        a, b = pl.ds(0, half), pl.ds(half, rest)

        def rows_of(part):
            return pl.ds(0, rows) if part is None else (pl.ds(0, low), pl.ds(low, rows - low))[part]

        def pair(part):
            return pl.ds(0, 4) if part is None else pl.ds(2 * part, 2)

        return (
            RingGather(link, lambda i, p: buf.at[z, i, rows_of(p), a], x, x_plus, x_minus),
            RingGather(link, lambda i, p: buf.at[i, x, rows_of(p), b], z, z_plus, z_minus),
            RingGather(link, lambda i, p: buf.at[i, pair(p), :, a], z, z_plus, z_minus),
            RingGather(link, lambda i, p: buf.at[pair(p), i, :, b], x, x_plus, x_minus),
        )

    low, high = pl.ds(0, 32), pl.ds(32, 32)

    def in_gather():
        return (
            DirectGather(link, lambda i, p: wi.at[z, i, low], x, along_x),
            DirectGather(link, lambda i, p: wi.at[i, x, high], z, along_z),
            DirectGather(link, lambda i, p: wp.at[z, i], x, along_x),
            DirectGather(link, lambda i, p: wi.at[i, :, low], z, along_z),
            DirectGather(link, lambda i, p: wi.at[:, i, high], x, along_x),
            DirectGather(link, lambda i, p: wp.at[i], z, along_z),
        )

    def out_gather():
        return (
            DirectGather(link, lambda i, p: wo.at[i, x], z, along_z),
            DirectGather(link, lambda i, p: wo.at[:, i], x, along_x),
        )

    def in_scatter():
        return (
            DirectScatter(link, lambda i, p: gi.at[i, :, low], z, along_z, gi_r1.at[0]),
            DirectScatter(link, lambda i, p: gi.at[:, i, high], x, along_x, gi_r1.at[1]),
            DirectScatter(link, lambda i, p: gp.at[i], z, along_z, gp_r1),
            DirectScatter(link, lambda i, p: gi.at[z, i, low], x, along_x, gi_r2.at[0]),
            DirectScatter(link, lambda i, p: gi.at[i, x, high], z, along_z, gi_r2.at[1]),
            DirectScatter(link, lambda i, p: gp.at[z, i], x, along_x, gp_r2),
        )

    def out_scatter():
        return (
            DirectScatter(link, lambda i, p: go.at[:, i], x, along_x, go_r1),
            DirectScatter(link, lambda i, p: go.at[i, x], z, along_z, go_r2),
        )

    def weight_scatter(buf, half, low, a1, a2, b1, b2, a3, a4, b3, b4):
        rest = buf.shape[3] - half
        rows = buf.shape[2]
        a, b = pl.ds(0, half), pl.ds(half, rest)

        def rows_of(part):
            return pl.ds(0, rows) if part is None else (pl.ds(0, low), pl.ds(low, rows - low))[part]

        def pair(part):
            return pl.ds(0, 4) if part is None else pl.ds(2 * part, 2)

        return (
            RingScatter(link, lambda i, p: buf.at[i, pair(p), :, a], z, z_plus, z_minus,
                        a1.at[0], a1.at[1], (a2.at[0], a2.at[1]), (a2.at[2], a2.at[3])),
            RingScatter(link, lambda i, p: buf.at[pair(p), i, :, b], x, x_plus, x_minus,
                        b1.at[0], b1.at[1], (b2.at[0], b2.at[1]), (b2.at[2], b2.at[3])),
            RingScatter(link, lambda i, p: buf.at[z, i, rows_of(p), a], x, x_plus, x_minus,
                        a3.at[0], a3.at[1], (a4.at[0], a4.at[1]), (a4.at[2], a4.at[3])),
            RingScatter(link, lambda i, p: buf.at[i, x, rows_of(p), b], z, z_plus, z_minus,
                        b3.at[0], b3.at[1], (b4.at[0], b4.at[1]), (b4.at[2], b4.at[3])),
        )

    pre = []
    for step, mate in enumerate(mates):
        pre.append(
            (
                link.send(win_ref.at[mate[1]], pre_in.at[c], mate),
                link.send(pack_ref, pre_pack.at[step], mate),
            )
        )
    gather_x = ctx_gather(xg)
    gather_x.start()
    for load in loads[5:6]:
        load.wait()
    out_rows = proj_ref[...].astype(f32)
    wo[z, x] = jnp.concatenate(
        [out_rows[:, 128 * w : 128 * w + 128] for w in range(8)], 0
    ).astype(bf16)
    out_w = out_gather()
    out_w[0].start()
    for load in loads[6:]:
        load.wait()
    own = wf.at[z, x]
    own[:, 0:512] = gate_ref[:, 0:512]
    own[:, 512:1024] = up_ref[:, 0:512]
    own[:, 1024:1152] = jnp.concatenate([gate_ref[:, 512:576], up_ref[:, 512:576]], 1)
    own[:, 1152:1792] = jnp.concatenate([down_ref[...], jnp.zeros((64, 64), bf16)], 1)
    ffn_w = weight_gather(wf, 896, 32)
    for step, (h_in, h_pack) in enumerate(pre):
        link.landed(h_in, pre_in.at[lax.rem(c + 7 - step, 8)])
        link.landed(h_pack, pre_pack.at[step])
    wi[z, x] = pre_in[...].reshape(64, 384).astype(bf16)
    summed = own_pack
    for step in range(7):
        summed = summed + pre_pack[step]
    tile = jnp.where(row < 2, summed, own_pack)
    wp[z, x] = jnp.concatenate([tile, jnp.zeros_like(tile)], 0).astype(bf16)
    in_w = in_gather()
    for part in in_w[0:3]:
        part.start()
    ffn_w[0].start()
    ffn_w[1].start()
    out_w[0].finish()
    out_w[1].start()
    gather_x.forward()
    for part in in_w[0:3]:
        part.finish()
    for part in in_w[3:6]:
        part.start()
    gather_x.sides()
    cotg[y, core] = cot_ref[0]
    out_w[1].finish()
    slab = wo[...].astype(f32).reshape(16, 8, 8, 128)
    for w in range(8):
        wog[y, core, :, 128 * w : 128 * w + 128] = slab[:, w].reshape(128, 128).astype(bf16)
    gather_out = ctx_gather(wog)
    gather_out.start()
    ffn_w[0].forward()
    ffn_w[1].forward()
    gather_x.across()
    ffn_w[0].finish()
    ffn_w[1].finish()
    ffn_w[2].start()
    ffn_w[3].start()
    gather_x.finish_near()
    gather_x.finish_sides()
    gather_x.finish_far()

    def first_scale(g, carry):
        values = xg[g].reshape(256, 1024).astype(f32)
        scale_g[g] = lax.rsqrt(jnp.mean(values * values, axis=-1, keepdims=True) + epsilon)
        return carry

    lax.fori_loop(0, 4, first_scale, 0)
    for part in in_w[3:6]:
        part.finish()
    gather_out.forward()
    gather_cot = ctx_gather(cotg)
    gather_cot.start()

    packs = [wp[i // 4, i % 4].astype(f32)[0:8] for i in range(16)]
    gain_one = jnp.concatenate([packs[2 * w][0:1] + packs[2 * w + 1][0:1] for w in range(8)], 1)
    gain_two = jnp.concatenate([packs[2 * w][1:2] + packs[2 * w + 1][1:2] for w in range(8)], 1)
    taps = packs[0]
    for i in range(1, 16):
        taps = taps + packs[i]
    tap = [taps[2 + k : 3 + k] for k in range(3)]

    def project(g, carry):
        values = xg[g].reshape(256, 1024).astype(f32)
        lifted = (values * scale_g[g] * gain_one).astype(bf16)
        h1g[g] = lifted
        proj[g] = mm(lifted, wi[...].reshape(1024, 384))
        return carry

    lax.fori_loop(0, 4, project, 0)
    b_part = proj[:, :, 0:128].reshape(1024, 128)
    x_part = proj[:, :, 256:384].reshape(1024, 128)
    bx_pad[0:8] = jnp.zeros((8, 128), f32)
    bx_pad[8:1032] = (b_part * x_part).astype(bf16).astype(f32)
    z_all = tap[0] * bx_pad[6:1030] + tap[1] * bx_pad[7:1031] + tap[2] * bx_pad[8:1032]
    z_buf[...] = z_all
    y_buf[...] = (proj[:, :, 128:256].reshape(1024, 128) * z_all).astype(bf16).reshape(8, 128, 128)
    swap_y = exchange(y_buf, y_own)
    y_own[c] = y_buf[c]
    ffn_w[2].forward()
    ffn_w[3].forward()
    gather_out.sides()
    gather_out.across()
    gather_cot.forward()
    exchanged(swap_y, y_own)
    gather_out.finish_near()
    gather_out.finish_sides()
    gather_out.finish_far()
    gated = jnp.concatenate([y_own[i] for i in range(8)], 1)
    middle = x_ref[0].astype(f32) + mm(gated, wog[...].reshape(1024, 1024))
    scale_two = lax.rsqrt(jnp.mean(middle * middle, axis=-1, keepdims=True) + epsilon)
    h2g[y, core] = (middle * scale_two * gain_two).astype(bf16)
    gather_h2 = ctx_gather(h2g)
    gather_h2.start()
    gather_cot.sides()
    gather_cot.across()
    gather_cot.finish_near()
    gather_cot.finish_sides()
    gather_cot.finish_far()
    ffn_w[2].finish()
    ffn_w[3].finish()
    gather_h2.finish_near()

    scatter_dh2 = ctx_scatter(0, own_first=True)
    low_half = lax.broadcasted_iota(jnp.int32, (256, 128), 1) < 64

    def feed_forward(step, carry):
        g = scatter_dh2.group(step)

        @pl.when(step == 1)
        def _():
            gather_h2.forward()
            gather_h2.sides()
            gather_h2.finish_sides()

        @pl.when(step == 2)
        def _():
            scatter_dh2.side_left()
            gather_h2.across()
            gather_h2.finish_far()

        @pl.when(step == 3)
        def _():
            scatter_dh2.start()

        w_gu = wf[:, :, :, 0:GU].reshape(1024, GU)
        gu = mm(h2g[g].reshape(256, 1024), w_gu)
        mixed = gu[:, 1024:1152]
        gating = jnp.concatenate([gu[:, 0:512], mixed], 1)
        upward = jnp.concatenate([gu[:, 512:1024], pltpu.roll(mixed, 64, 1)], 1)
        sigma = 1.0 / (1.0 + jnp.exp(-gating))
        activated = gating * sigma
        hidden = activated * upward
        hid_buf[g, :, 0:512] = hidden[:, 0:512].astype(bf16)
        hid_buf[g, :, 512:640] = jnp.where(low_half, hidden[:, 512:640], 0.0).astype(bf16)
        w_down = wf[:, :, :, GU:FFL].reshape(1024, HID)
        d_hidden = mm(cotg[g].reshape(256, 1024), w_down)
        d_gating = d_hidden * upward * sigma * (1.0 + gating * (1.0 - sigma))
        d_upward = d_hidden * activated
        d_mixed = jnp.where(low_half, d_gating[:, 512:640], pltpu.roll(d_upward[:, 512:640], 64, 1))
        d_gu = jnp.concatenate([d_gating[:, 0:512], d_upward[:, 0:512], d_mixed], 1).astype(bf16)
        dgu_buf[g] = d_gu
        rs_part[0, g] = mt(d_gu, w_gu).astype(bf16).reshape(2, 128, 1024)
        scatter_dh2.cross(step)
        return carry

    lax.fori_loop(0, 4, feed_forward, 0)
    scatter_dh2.side_right()
    scatter_out = ctx_scatter(1)

    def ffn_out(step, carry):
        g = scatter_out.group(step)
        w_down = wf[:, :, :, GU:FFL].reshape(1024, HID)
        rs_part[1, g] = mt(hid_buf[g], w_down).astype(bf16).reshape(2, 128, 1024)
        scatter_out.cross(step)
        return carry

    lax.fori_loop(0, 4, ffn_out, 0)
    scatter_dh2.middle()
    scatter_out.start()
    scatter_out.side_left()
    scatter_out.side_right()

    def grad_ffn(i, carry):
        lanes = pl.ds(pl.multiple_of(i * 256, 256), 256)
        lhs = h2g[:, :, :, lanes].reshape(1024, 256)
        gf[i, :, :, 0:GU] = tm(lhs, dgu_buf[...].reshape(1024, GU)).astype(bf16).reshape(4, 64, GU)
        lhs = cotg[:, :, :, lanes].reshape(1024, 256)
        gf[i, :, :, GU:FFL] = (
            tm(lhs, hid_buf[...].reshape(1024, HID)).astype(bf16).reshape(4, 64, HID)
        )
        return carry

    lax.fori_loop(0, 4, grad_ffn, 0)
    ffn_g = weight_scatter(gf, 896, 32, gf_a1, gf_a2, gf_b1, gf_b2, gf_a3, gf_a4, gf_b3, gf_b4)
    ffn_g[0].start()
    ffn_g[1].start()

    d_second = scatter_dh2.finish()
    normed_two = middle * scale_two
    grad_gain_two = jnp.sum(d_second * normed_two, axis=0, keepdims=True)
    scaled = d_second * gain_two
    d_middle = cot_ref[0].astype(f32) + scale_two * (
        scaled - normed_two * jnp.mean(scaled * normed_two, axis=-1, keepdims=True)
    )
    d_branch = d_middle.astype(bf16)
    dg[y, core] = d_branch
    d_gated = mt(d_branch, wog[...].reshape(1024, 1024)).astype(bf16)
    for i in range(8):
        dy_buf[i] = d_gated[:, 128 * i : 128 * i + 128]
    swap_dy = exchange(dy_buf, dy_own)
    gather_d = ctx_gather(dg)
    gather_d.start()
    dy_own[c] = dy_buf[c]
    ffn_g[0].middle()
    ffn_g[1].middle()
    exchanged(swap_dy, dy_own)

    d_gated = dy_own[...].reshape(1024, 128).astype(f32)
    dz_pad[0:1024] = d_gated * proj[:, :, 128:256].reshape(1024, 128)
    dp_buf[:, :, 128:256] = (d_gated * z_buf[...]).astype(bf16).reshape(4, 256, 128)
    dz_pad[1024:1032] = jnp.zeros((8, 128), f32)
    d_bx = tap[2] * dz_pad[0:1024] + tap[1] * dz_pad[1:1025] + tap[0] * dz_pad[2:1026]
    d_bx = d_bx.reshape(4, 256, 128)
    dp_buf[:, :, 0:128] = (d_bx * proj[:, :, 256:384]).astype(bf16)
    dp_buf[:, :, 256:384] = (d_bx * proj[:, :, 0:128]).astype(bf16)
    grad_tap = [
        jnp.sum(dz_pad[0:1024] * bx_pad[6 + k : 1030 + k], axis=0, keepdims=True) for k in range(3)
    ]
    gather_d.forward()
    gather_d.sides()

    scatter_dh1 = ctx_scatter(2)
    mix_acc[...] = jnp.zeros((8, 1024), f32)

    def branch_back(step, carry):
        g = scatter_dh1.group(step)
        d_lifted = mt(dp_buf[g], wi[...].reshape(1024, 384))
        rs_part[2, g] = d_lifted.astype(bf16).reshape(2, 128, 1024)
        scatter_dh1.cross(step)
        normed = xg[g].reshape(256, 1024).astype(f32) * scale_g[g]
        mix_acc[...] += jnp.sum((d_lifted * normed).reshape(32, 8, 1024), axis=0)
        return carry

    lax.fori_loop(0, 4, branch_back, 0)
    scatter_dh1.start()
    scatter_dh1.side_left()
    scatter_dh1.side_right()

    def grad_in(i, carry):
        lanes = pl.ds(pl.multiple_of(i * 256, 256), 256)
        lhs = h1g[:, :, lanes].reshape(1024, 256)
        gi[i] = tm(lhs, dp_buf[...].reshape(1024, 384)).astype(bf16).reshape(4, 64, 384)
        return carry

    lax.fori_loop(0, 4, grad_in, 0)
    grad_mix = jnp.sum(mix_acc[...], axis=0, keepdims=True)
    for i in range(16):
        lanes = slice(128 * (i // 2), 128 * (i // 2) + 128)
        rows = [grad_mix[:, lanes], grad_gain_two[:, lanes], *grad_tap, jnp.zeros((11, 128), f32)]
        gp[i // 4, i % 4] = jnp.concatenate(rows, 0).astype(bf16)
    in_g = in_scatter()
    for part in in_g[0:3]:
        part.start()
    scatter_dh1.middle()
    gather_d.across()
    gather_d.finish_near()
    gather_d.finish_sides()
    gather_d.finish_far()
    g_out = tm(y_buf[...].reshape(1024, 128), dg[...].reshape(1024, 1024))
    pieces = [g_out[:, 128 * w : 128 * w + 128].reshape(16, 1, 8, 128) for w in range(8)]
    go[...] = jnp.concatenate(pieces, 1).reshape(4, 4, 64, 128).astype(bf16)
    out_g = out_scatter()
    out_g[0].start()
    for part in in_g[0:3]:
        part.finish()
    for part in in_g[3:6]:
        part.start()
    ffn_g[0].finish()
    ffn_g[1].finish()
    ffn_g[2].start()
    ffn_g[3].start()
    scatter_out.middle()
    out_g[0].finish()
    out_g[1].start()

    d_lifted = scatter_dh1.finish()
    local = x_ref[0].astype(f32)
    scale_one = lax.rsqrt(jnp.mean(local * local, axis=-1, keepdims=True) + epsilon)
    normed_one = local * scale_one
    scaled = d_lifted * gain_one
    gin_ref[...] = d_middle + scale_one * (
        scaled - normed_one * jnp.mean(scaled * normed_one, axis=-1, keepdims=True)
    )
    stores = [
        pltpu.make_async_copy(src, dst, local_sems.at[10 + i])
        for i, (src, dst) in enumerate(
            (
                (gin_ref, gin_hbm),
                (gff_ref, gff_hbm),
                (out_ref, out_hbm),
                (gwout_ref, gwout_hbm),
                (gwin_ref, gwin_hbm),
                (gpack_ref, gpack_hbm),
            )
        )
    ]
    stores[0].start()
    ffn_g[2].middle()
    ffn_g[3].middle()
    for part in in_g[3:6]:
        part.finish()

    post_send[...] = gi[z, x].astype(f32).reshape(8, 8, 384)
    post_own[...] = gp[z, x].astype(f32)[0:8]
    post = []
    for step, mate in enumerate(mates):
        post.append(
            (
                link.send(post_send.at[mate[1]], post_in.at[c], mate),
                link.send(post_own, post_pack.at[step], mate),
            )
        )
    ffn_g[2].finish()
    ffn_g[3].finish()
    gff_ref[...] = gf[z, x].astype(f32)
    stores[1].start()
    out_ref[...] = (middle + scatter_out.finish()).astype(bf16)
    stores[2].start()
    out_g[1].finish()
    gwout_ref[...] = go[z, x].astype(f32)
    stores[3].start()
    post_in[c] = post_send[c]
    summed = post_own[...]
    for step, (h_in, h_pack) in enumerate(post):
        link.landed(h_in, post_in.at[lax.rem(c + 7 - step, 8)])
        link.landed(h_pack, post_pack.at[step])
        summed = summed + post_pack[step]
    gwin_ref[...] = post_in[...]
    gpack_ref[...] = jnp.where(row < 2, summed, post_own[...])
    stores[4].start()
    stores[5].start()
    for store in stores:
        store.wait()

    link.drain()
    for scatter in (scatter_dh2, scatter_out, scatter_dh1):
        scatter.drain()


def spread_kernel(
    block_ref,
    gin_ref,
    gff_ref,
    gwin_ref,
    gwout_ref,
    gpack_ref,
    o_block,
    o_gin,
    o_mix,
    o_in,
    o_tap,
    o_proj,
    o_ffn,
    o_gate,
    o_up,
    o_down,
):
    f = lax.axis_index("fsdp")
    c = lax.axis_index("ctx")
    lane = lax.broadcasted_iota(jnp.int32, (8, 128), 1)
    o_block[0] = block_ref[...]
    o_gin[0] = gin_ref[...]
    for b in range(3):
        blocks = [gwin_ref[i, :, 128 * b : 128 * b + 128] for i in range(8)]
        for v, block in enumerate(by_channel(blocks, lane, True)):
            o_in[:, 1024 * b + 128 * v : 1024 * b + 128 * v + 128] = block
    for w in range(8):
        o_proj[:, 128 * w : 128 * w + 128] = gwout_ref[8 * w : 8 * w + 8]
    small = gpack_ref[...]
    gains = pltpu.roll(small, lax.rem(256 - 64 * lax.rem(f, 2) - 8 * c, 128), 1)
    o_mix[...] = gains[0:1, 0:8]
    o_ffn[...] = gains[1:2, 0:8]
    o_tap[...] = pltpu.roll(small, lax.rem(128 - 8 * f, 128), 1)[2:5, 0:8]
    mixed = gff_ref[:, 1024:1152]
    o_gate[:, 0:512] = gff_ref[:, 0:512]
    o_gate[:, 512:576] = mixed[:, 0:64]
    o_up[:, 0:512] = gff_ref[:, 512:1024]
    o_up[:, 512:576] = pltpu.roll(mixed, 64, 1)[:, 0:64]
    o_down[...] = gff_ref[:, 1152:1728]


def per_device(
    inputs,
    mix_gain,
    in_proj,
    conv_kernel,
    out_proj,
    ffn_gain,
    gate_proj,
    up_proj,
    down_proj,
    cotangent,
):
    v = pltpu.VMEM
    anywhere = pl.BlockSpec(memory_space=pl.ANY)
    sems = 256
    out_shape = (
        jax.ShapeDtypeStruct((128, 1024), bf16),
        jax.ShapeDtypeStruct((128, 1024), f32),
        jax.ShapeDtypeStruct((64, FFL), f32),
        jax.ShapeDtypeStruct((8, 8, 384), f32),
        jax.ShapeDtypeStruct((64, 128), f32),
        jax.ShapeDtypeStruct((8, 128), f32),
    )
    scratch = [
        v(inputs.shape, bf16),
        v(cotangent.shape, bf16),
        v((1, 8), bf16),
        v(in_proj.shape, bf16),
        v(conv_kernel.shape, bf16),
        v(out_proj.shape, bf16),
        v((1, 8), bf16),
        v(gate_proj.shape, bf16),
        v(up_proj.shape, bf16),
        v(down_proj.shape[::-1], bf16),
        *[v(shape.shape, shape.dtype) for shape in out_shape],
        pltpu.SemaphoreType.DMA((16,)),
        pltpu.SemaphoreType.DMA((sems,)),
        pltpu.SemaphoreType.DMA((sems,)),
        v((8, 8, 384), f32),
        v((8, 128), f32),
        v((4, 2, 128, 1024), bf16),
        v((4, 2, 128, 1024), bf16),
        v((4, 2, 128, 1024), bf16),
        v((4, 2, 128, 1024), bf16),
        v((4, 4, 64, FFL), bf16),
        v((4, 4, 64, 384), bf16),
        v((4, 4, 16, 128), bf16),
        v((4, 4, 64, 128), bf16),
        v((8, 8, 384), f32),
        v((7, 8, 128), f32),
        v((4, 2, 128, 1024), bf16),
        v((4, 256, 1024), bf16),
        v((4, 256, 1), f32),
        v((4, 256, 384), f32),
        v((1032, 128), f32),
        v((1024, 128), f32),
        v((8, 128, 128), bf16),
        v((8, 128, 128), bf16),
        v((8, 128, 128), bf16),
        v((8, 128, 128), bf16),
        v((4, 256, HID), bf16),
        v((4, 256, GU), bf16),
        v((1032, 128), f32),
        v((4, 256, 384), bf16),
        v((8, 1024), f32),
        v((3, 4, 2, 128, 1024), bf16),
        v((3, 4, 128, 1024), bf16),
        v((3, 2, 64, 1024), bf16),
        v((3, 2, 128, 1024), bf16),
        v((4, 4, 64, FFL), bf16),
        v((4, 4, 64, 384), bf16),
        v((4, 4, 16, 128), bf16),
        v((4, 4, 64, 128), bf16),
        v((2, 2, 64, 896), bf16),
        v((4, 2, 64, 896), bf16),
        v((2, 2, 64, 896), bf16),
        v((4, 2, 64, 896), bf16),
        v((2, 32, 896), bf16),
        v((4, 32, 896), bf16),
        v((2, 32, 896), bf16),
        v((4, 32, 896), bf16),
        v((2, 3, 4, 32, 384), bf16),
        v((2, 3, 32, 384), bf16),
        v((3, 4, 16, 128), bf16),
        v((3, 16, 128), bf16),
        v((3, 4, 64, 128), bf16),
        v((3, 64, 128), bf16),
        v((8, 8, 384), f32),
        v((8, 8, 384), f32),
        v((8, 128), f32),
        v((7, 8, 128), f32),
    ]
    raw = pl.pallas_call(
        block_kernel,
        out_shape=out_shape,
        in_specs=[anywhere] * 10,
        out_specs=(anywhere,) * 6,
        scratch_shapes=scratch,
        compiler_params=pltpu.CompilerParams(
            collective_id=0, has_side_effects=True, vmem_limit_bytes=62 * 1024 * 1024
        ),
    )(
        inputs,
        cotangent,
        mix_gain.reshape(1, 8),
        in_proj,
        conv_kernel,
        out_proj,
        ffn_gain.reshape(1, 8),
        gate_proj,
        up_proj,
        down_proj.T,
    )
    made = pl.pallas_call(
        spread_kernel,
        out_shape=(
            jax.ShapeDtypeStruct(inputs.shape, bf16),
            jax.ShapeDtypeStruct(inputs.shape, f32),
            jax.ShapeDtypeStruct((1, 8), f32),
            jax.ShapeDtypeStruct(in_proj.shape, f32),
            jax.ShapeDtypeStruct(conv_kernel.shape, f32),
            jax.ShapeDtypeStruct(out_proj.shape, f32),
            jax.ShapeDtypeStruct((1, 8), f32),
            jax.ShapeDtypeStruct(gate_proj.shape, f32),
            jax.ShapeDtypeStruct(up_proj.shape, f32),
            jax.ShapeDtypeStruct(down_proj.shape[::-1], f32),
        ),
        grid=(1,),
        compiler_params=pltpu.CompilerParams(vmem_limit_bytes=62 * 1024 * 1024),
    )(*raw)
    return (*made[:2], made[2].reshape(8), *made[3:6], made[6].reshape(8), *made[7:9], made[9].T)


def solution(mesh):
    in_specs = (
        P("fsdp", "ctx", None),
        P(("fsdp", "ctx")),
        P(("fsdp", "ctx"), None),
        P(None, ("fsdp", "ctx")),
        P(("fsdp", "ctx"), None),
        P(("fsdp", "ctx")),
        P("fsdp", "ctx"),
        P("fsdp", "ctx"),
        P("ctx", "fsdp"),
        P("fsdp", "ctx", None),
    )
    out_specs = (
        P("fsdp", "ctx", None),
        P("fsdp", "ctx", None),
        P(("fsdp", "ctx")),
        P(("fsdp", "ctx"), None),
        P(None, ("fsdp", "ctx")),
        P(("fsdp", "ctx"), None),
        P(("fsdp", "ctx")),
        P("fsdp", "ctx"),
        P("fsdp", "ctx"),
        P("ctx", "fsdp"),
    )
    return jax.shard_map(
        per_device, mesh=mesh, in_specs=in_specs, out_specs=out_specs, check_vma=False
    )
```

```python
import jax
import jax.numpy as jnp
from jax import lax
from jax.experimental import pallas as pl
from jax.experimental.pallas import tpu as pltpu
from jax.sharding import PartitionSpec as P

epsilon = 1e-05
f32 = jnp.float32
bf16 = jnp.bfloat16
MESH = pl.DeviceIdType.MESH

GU = 1152
FFL = 1792
HID = 640


def mm(a, b):
    return lax.dot_general(a, b, (((1,), (0,)), ((), ())), preferred_element_type=f32)


def mt(a, b):
    return lax.dot_general(a, b, (((1,), (1,)), ((), ())), preferred_element_type=f32)


def tm(a, b):
    return lax.dot_general(a, b, (((0,), (0,)), ((), ())), preferred_element_type=f32)


def add_into(ref, *others):
    total = ref[...].astype(f32)
    for other in others:
        total = total + other[...].astype(f32)
    ref[...] = total.astype(ref.dtype)


class Link:
    def __init__(self, send_sems, recv_sems):
        self.send_sems, self.recv_sems = send_sems, recv_sems
        self.used = 0
        self.started = []

    def reserve(self, count):
        first = self.used
        self.used += count
        return first

    def copy(self, src, dst, device, slot):
        return pltpu.make_async_remote_copy(
            src_ref=src,
            dst_ref=dst,
            send_sem=self.send_sems.at[slot],
            recv_sem=self.recv_sems.at[slot],
            device_id=device,
            device_id_type=MESH,
        )

    def send(self, src, dst, device):
        slot = self.reserve(1)
        self.copy(src, dst, device, slot).start()
        self.started.append((src, device, slot))
        return (device, slot)

    def landed(self, handle, ref):
        device, slot = handle
        self.copy(ref, ref, device, slot).wait_recv()

    def drain(self):
        for src, device, slot in self.started:
            self.copy(src, src, device, slot).wait_send()


def ring(value, step):
    return lax.rem(value + step, 4)


class RingGather:
    def __init__(self, link, view, me, plus, minus):
        self.link, self.view, self.me, self.plus, self.minus = link, view, me, plus, minus
        self.left, self.far, self.right = ring(me, 3), ring(me, 2), ring(me, 1)

    def start(self):
        send = self.link.send
        lo, hi = self.view(self.me, 0), self.view(self.me, 1)
        self.p0, self.m1 = send(lo, lo, self.plus), send(hi, hi, self.minus)
        self.p1, self.m0 = send(hi, hi, self.plus), send(lo, lo, self.minus)

    def forward(self):
        part = self.view(self.left, 0)
        self.link.landed(self.p0, part)
        self.fp = self.link.send(part, part, self.plus)
        part = self.view(self.right, 1)
        self.link.landed(self.m1, part)
        self.fm = self.link.send(part, part, self.minus)

    def finish(self):
        self.link.landed(self.p1, self.view(self.left, 1))
        self.link.landed(self.m0, self.view(self.right, 0))
        self.link.landed(self.fp, self.view(self.far, 0))
        self.link.landed(self.fm, self.view(self.far, 1))


class RingScatter:
    def __init__(self, link, view, me, plus, minus, r1a, r1b, r2a, r2b):
        self.link, self.view, self.me, self.plus, self.minus = link, view, me, plus, minus
        self.r1a, self.r1b, self.r2a, self.r2b = r1a, r1b, r2a, r2b
        self.left, self.far, self.right = ring(me, 3), ring(me, 2), ring(me, 1)

    def start(self):
        send = self.link.send
        self.h1a = send(self.view(self.far, 0), self.r1a, self.plus)
        self.h1b = send(self.view(self.far, 1), self.r1b, self.minus)
        self.h2a1 = send(self.view(self.right, 1), self.r2a[1], self.plus)
        self.h2b0 = send(self.view(self.left, 0), self.r2b[0], self.minus)

    def middle(self):
        self.link.landed(self.h1a, self.r1a)
        add_into(self.view(self.right, 0), self.r1a)
        self.h2a0 = self.link.send(self.view(self.right, 0), self.r2a[0], self.plus)
        self.link.landed(self.h1b, self.r1b)
        add_into(self.view(self.left, 1), self.r1b)
        self.h2b1 = self.link.send(self.view(self.left, 1), self.r2b[1], self.minus)

    def finish(self):
        self.link.landed(self.h2a1, self.r2a[1])
        self.link.landed(self.h2b0, self.r2b[0])
        self.link.landed(self.h2a0, self.r2a[0])
        self.link.landed(self.h2b1, self.r2b[1])
        for part in (0, 1):
            add_into(self.view(self.me, part), self.r2a[part], self.r2b[part])


class DirectGather:
    def __init__(self, link, view, me, device):
        self.link, self.view, self.me, self.device = link, view, me, device

    def start(self):
        own = self.view(self.me, None)
        self.sent = [(s, self.link.send(own, own, self.device(s))) for s in (1, 3, 2)]

    def finish(self):
        for step, handle in self.sent:
            self.link.landed(handle, self.view(ring(self.me, 4 - step), None))


class DirectScatter:
    def __init__(self, link, view, me, device, landing):
        self.link, self.view, self.me, self.device, self.landing = link, view, me, device, landing

    def start(self):
        self.sent = [
            (s, self.link.send(self.view(ring(self.me, s), None), self.landing.at[s - 1], self.device(s)))
            for s in (1, 3, 2)
        ]

    def finish(self):
        for step, handle in self.sent:
            self.link.landed(handle, self.landing.at[step - 1])
        add_into(self.view(self.me, None), *[self.landing.at[i] for i in range(3)])


LO, HI = pl.ds(0, 64), pl.ds(64, 64)


class CtxGather:
    def __init__(self, link, buf, y, core, plus, minus, other):
        self.link, self.buf, self.y, self.core = link, buf, y, core
        self.plus, self.minus, self.other = plus, minus, other
        self.left, self.far, self.right = ring(y, 3), ring(y, 2), ring(y, 1)
        self.mate = 1 - core

    def half(self, which, part):
        return self.buf.at[which, self.core, (LO, HI)[part]]

    def start(self):
        send = self.link.send
        lo, hi = self.half(self.y, 0), self.half(self.y, 1)
        own = self.buf.at[self.y, self.core]
        self.p0, self.m1 = send(lo, lo, self.plus), send(hi, hi, self.minus)
        self.p1, self.m0 = send(hi, hi, self.plus), send(lo, lo, self.minus)
        self.near = send(own, own, self.other)
        self.late = []

    def pass_on(self, handle, which, part, device):
        half = self.half(which, part)
        self.link.landed(handle, half)
        onward = None if device is None else self.link.send(half, half, device)
        theirs = self.buf.at[which, self.mate, (LO, HI)[part]]
        self.late.append((self.link.send(half, half, self.other), theirs))
        return onward

    def forward(self):
        left, right = self.left, self.right
        self.fp = self.pass_on(self.p0, left, 0, self.plus)
        self.fm = self.pass_on(self.m1, right, 1, self.minus)

    def sides(self):
        self.pass_on(self.p1, self.left, 1, None)
        self.pass_on(self.m0, self.right, 0, None)

    def across(self):
        far = self.far
        self.pass_on(self.fp, far, 0, None)
        self.pass_on(self.fm, far, 1, None)

    def finish_near(self):
        self.link.landed(self.near, self.buf.at[self.y, self.mate])

    def finish_sides(self):
        for handle, ref in self.late[:4]:
            self.link.landed(handle, ref)

    def finish_far(self):
        for handle, ref in self.late[4:]:
            self.link.landed(handle, ref)


class CtxScatter:
    def __init__(self, link, part, rb, r1, r2, y, core, plus, minus, other, own_first):
        self.link, self.part, self.rb, self.r1, self.r2 = link, part, rb, r1, r2
        self.y, self.core, self.own_first = y, core, own_first
        self.plus, self.minus, self.other = plus, minus, other
        self.left, self.far, self.right = ring(y, 3), ring(y, 2), ring(y, 1)
        self.mate = 1 - core
        self.first = link.reserve(4)
        self.at_far, self.at_left, self.at_right, self.at_own = (2, 1, 3, 0) if own_first else (0, 1, 2, 3)

    def group(self, step):
        if self.own_first:
            return lax.rem(self.y + 3 * step, 4)
        return lax.rem(self.y + 2 + step + step // 2 + 2 * (step // 3), 4)

    def cross(self, step):
        g = self.group(step)
        self.link.copy(
            self.part.at[g, self.mate], self.rb.at[g], self.other, self.first + step
        ).start()

    def crossed(self, g, step):
        ref = self.rb.at[g]
        self.link.copy(ref, ref, self.other, self.first + step).wait_recv()

    def block(self, which, rows):
        return self.part.at[which, self.core, rows]

    def start(self):
        far = self.far
        self.crossed(far, self.at_far)
        add_into(self.block(far, LO), self.rb.at[far, LO])
        self.h1a = self.link.send(self.block(far, LO), self.r1.at[0], self.plus)
        add_into(self.block(far, HI), self.rb.at[far, HI])
        self.h1b = self.link.send(self.block(far, HI), self.r1.at[1], self.minus)

    def side_left(self):
        left = self.left
        self.crossed(left, self.at_left)
        add_into(self.block(left, LO), self.rb.at[left, LO])
        self.h2b0 = self.link.send(self.block(left, LO), self.r2.at[1, LO], self.minus)

    def side_right(self):
        right = self.right
        self.crossed(right, self.at_right)
        add_into(self.block(right, HI), self.rb.at[right, HI])
        self.h2a1 = self.link.send(self.block(right, HI), self.r2.at[0, HI], self.plus)

    def middle(self):
        left, right = self.left, self.right
        self.link.landed(self.h1a, self.r1.at[0])
        add_into(self.block(right, LO), self.rb.at[right, LO], self.r1.at[0])
        self.h2a0 = self.link.send(self.block(right, LO), self.r2.at[0, LO], self.plus)
        self.link.landed(self.h1b, self.r1.at[1])
        add_into(self.block(left, HI), self.rb.at[left, HI], self.r1.at[1])
        self.h2b1 = self.link.send(self.block(left, HI), self.r2.at[1, HI], self.minus)

    def finish(self):
        self.crossed(self.y, self.at_own)
        self.link.landed(self.h2b0, self.r2.at[1, LO])
        self.link.landed(self.h2a1, self.r2.at[0, HI])
        self.link.landed(self.h2a0, self.r2.at[0, LO])
        self.link.landed(self.h2b1, self.r2.at[1, HI])
        return (
            self.part[self.y, self.core].astype(f32)
            + self.rb[self.y].astype(f32)
            + self.r2[0].astype(f32)
            + self.r2[1].astype(f32)
        )

    def drain(self):
        for step in range(4):
            g = self.group(step)
            src = self.part.at[g, self.mate]
            self.link.copy(src, src, self.other, self.first + step).wait_send()


def by_channel(blocks, lane, inverse):
    made = []
    for target in range(8):
        total = jnp.zeros((8, 128), f32)
        for source in range(8):
            for h in range(2):
                if inverse:
                    start, lands = 16 * target + 8 * h, 64 * h + 8 * source
                else:
                    start, lands = 64 * h + 8 * target, 16 * source + 8 * h
                moved = pltpu.roll(blocks[source], (lands - start) % 128, 1)
                total = jnp.where((lane >= lands) & (lane < lands + 8), moved, total)
        made.append(total)
    return made


def block_kernel(
    x_hbm,
    cot_hbm,
    mix_hbm,
    in_hbm,
    tap_hbm,
    proj_hbm,
    ffn_hbm,
    gate_hbm,
    up_hbm,
    down_hbm,
    out_hbm,
    gin_hbm,
    gff_hbm,
    gwin_hbm,
    gwout_hbm,
    gpack_hbm,
    x_ref,
    cot_ref,
    mix_ref,
    in_ref,
    tap_ref,
    proj_ref,
    ffn_ref,
    gate_ref,
    up_ref,
    down_ref,
    out_ref,
    gin_ref,
    gff_ref,
    gwin_ref,
    gwout_ref,
    gpack_ref,
    local_sems,
    send_sems,
    recv_sems,
    win_ref,
    pack_ref,
    xg,
    cotg,
    h2g,
    dg,
    wf,
    wi,
    wp,
    wo,
    pre_in,
    wog,
    h1g,
    scale_g,
    proj,
    bx_pad,
    z_buf,
    y_buf,
    y_own,
    dy_buf,
    dy_own,
    hid_buf,
    dgu_buf,
    dz_pad,
    dp_buf,
    mix_acc,
    rs_part,
    rs_rb,
    rs_r1,
    rs_r2,
    gf,
    gi,
    gp,
    go,
    gf_a1,
    gf_a2,
    gf_b1,
    gf_b2,
    gf_a3,
    gf_a4,
    gf_b3,
    gf_b4,
    gi_r1,
    gi_r2,
    gp_r1,
    gp_r2,
    go_r1,
    go_r2,
    post_send,
    post_in,
):
    loads = [
        pltpu.make_async_copy(src, dst, local_sems.at[i])
        for i, (src, dst) in enumerate(
            (
                (x_hbm, x_ref),
                (in_hbm, in_ref),
                (mix_hbm, mix_ref),
                (ffn_hbm, ffn_ref),
                (tap_hbm, tap_ref),
                (proj_hbm, proj_ref),
                (gate_hbm, gate_ref),
                (up_hbm, up_ref),
                (down_hbm, down_ref),
                (cot_hbm, cot_ref),
            )
        )
    ]
    for load in loads:
        load.start()
    f = lax.axis_index("fsdp")
    c = lax.axis_index("ctx")
    z, x = f // 4, lax.rem(f, 4)
    y, core = c // 2, lax.rem(c, 2)
    y_plus, y_minus = (f, ring(y, 1) * 2 + core), (f, ring(y, 3) * 2 + core)
    other = (f, y * 2 + 1 - core)
    x_plus, x_minus = (z * 4 + ring(x, 1), c), (z * 4 + ring(x, 3), c)
    z_plus, z_minus = (ring(z, 1) * 4 + x, c), (ring(z, 3) * 4 + x, c)

    def along_x(step):
        return (z * 4 + ring(x, step), c)

    def along_z(step):
        return (ring(z, step) * 4 + x, c)

    mates = [(f, lax.rem(c + step, 8)) for step in range(1, 8)]

    barrier = pltpu.get_barrier_semaphore()
    rings = [along_x(step) for step in (1, 2, 3)] + [along_z(step) for step in (1, 2, 3)]
    for device in mates + rings:
        pl.semaphore_signal(barrier, inc=1, device_id=device, device_id_type=MESH)

    lane = lax.broadcasted_iota(jnp.int32, (8, 128), 1)
    row = lax.broadcasted_iota(jnp.int32, (8, 128), 0)
    for load in loads[:5]:
        load.wait()
    xg[y, core] = x_ref[0]
    in_rows = in_ref[...].astype(f32)
    for b in range(3):
        blocks = [in_rows[:, 1024 * b + 128 * v : 1024 * b + 128 * v + 128] for v in range(8)]
        for channel, block in enumerate(by_channel(blocks, lane, False)):
            win_ref[channel, :, 128 * b : 128 * b + 128] = block
    pack_ref[...] = jnp.zeros((8, 128), f32)
    pack_ref[0:1, 0:8] = mix_ref[...].astype(f32)
    pack_ref[1:2, 0:8] = ffn_ref[...].astype(f32)
    pack_ref[2:5, 0:8] = tap_ref[...].astype(f32)
    small = pack_ref[...]
    gains = pltpu.roll(small, 64 * lax.rem(f, 2) + 8 * c, 1)
    own_pack = jnp.where(row < 2, gains, pltpu.roll(small, 8 * f, 1))
    for i in range(8):
        win_ref[i, :, 384:512] = own_pack
    pre_in[c] = win_ref[c]
    pl.semaphore_wait(barrier, 13)

    link = Link(send_sems, recv_sems)

    def ctx_gather(buf):
        return CtxGather(link, buf, y, core, y_plus, y_minus, other)

    def ctx_scatter(n, own_first=False):
        return CtxScatter(
            link, rs_part.at[n], rs_rb.at[n], rs_r1.at[n], rs_r2.at[n],
            y, core, y_plus, y_minus, other, own_first,
        )

    def exchange(blocks, landing):
        return [link.send(blocks.at[mate[1]], landing.at[c], mate) for mate in mates]

    def exchanged(handles, landing):
        for step, handle in enumerate(handles):
            link.landed(handle, landing.at[lax.rem(c + 7 - step, 8)])

    def weight_gather(buf, half):
        rest = buf.shape[3] - half
        a, b = pl.ds(0, half), pl.ds(half, rest)

        def pair(part):
            return pl.ds(0, 4) if part is None else pl.ds(2 * part, 2)

        return (
            DirectGather(link, lambda i, p: buf.at[z, i, :, a], x, along_x),
            DirectGather(link, lambda i, p: buf.at[i, x, :, b], z, along_z),
            RingGather(link, lambda i, p: buf.at[i, pair(p), :, a], z, z_plus, z_minus),
            RingGather(link, lambda i, p: buf.at[pair(p), i, :, b], x, x_plus, x_minus),
        )

    low, high = pl.ds(0, 32), pl.ds(32, 32)

    def in_gather():
        return (
            DirectGather(link, lambda i, p: wi.at[z, i, low], x, along_x),
            DirectGather(link, lambda i, p: wi.at[i, x, high], z, along_z),
            DirectGather(link, lambda i, p: wp.at[z, i], x, along_x),
            DirectGather(link, lambda i, p: wi.at[i, :, low], z, along_z),
            DirectGather(link, lambda i, p: wi.at[:, i, high], x, along_x),
            DirectGather(link, lambda i, p: wp.at[i], z, along_z),
        )

    def out_gather():
        return (
            DirectGather(link, lambda i, p: wo.at[i, x], z, along_z),
            DirectGather(link, lambda i, p: wo.at[:, i], x, along_x),
        )

    def in_scatter():
        return (
            DirectScatter(link, lambda i, p: gi.at[i, :, low], z, along_z, gi_r1.at[0]),
            DirectScatter(link, lambda i, p: gi.at[:, i, high], x, along_x, gi_r1.at[1]),
            DirectScatter(link, lambda i, p: gp.at[i], z, along_z, gp_r1),
            DirectScatter(link, lambda i, p: gi.at[z, i, low], x, along_x, gi_r2.at[0]),
            DirectScatter(link, lambda i, p: gi.at[i, x, high], z, along_z, gi_r2.at[1]),
            DirectScatter(link, lambda i, p: gp.at[z, i], x, along_x, gp_r2),
        )

    def out_scatter():
        return (
            DirectScatter(link, lambda i, p: go.at[:, i], x, along_x, go_r1),
            DirectScatter(link, lambda i, p: go.at[i, x], z, along_z, go_r2),
        )

    def weight_scatter(buf, half, low, a1, a2, b1, b2, a3, a4, b3, b4):
        rest = buf.shape[3] - half
        rows = buf.shape[2]
        a, b = pl.ds(0, half), pl.ds(half, rest)

        def rows_of(part):
            return pl.ds(0, rows) if part is None else (pl.ds(0, low), pl.ds(low, rows - low))[part]

        def pair(part):
            return pl.ds(0, 4) if part is None else pl.ds(2 * part, 2)

        return (
            RingScatter(link, lambda i, p: buf.at[i, pair(p), :, a], z, z_plus, z_minus,
                        a1.at[0], a1.at[1], (a2.at[0], a2.at[1]), (a2.at[2], a2.at[3])),
            RingScatter(link, lambda i, p: buf.at[pair(p), i, :, b], x, x_plus, x_minus,
                        b1.at[0], b1.at[1], (b2.at[0], b2.at[1]), (b2.at[2], b2.at[3])),
            RingScatter(link, lambda i, p: buf.at[z, i, rows_of(p), a], x, x_plus, x_minus,
                        a3.at[0], a3.at[1], (a4.at[0], a4.at[1]), (a4.at[2], a4.at[3])),
            RingScatter(link, lambda i, p: buf.at[i, x, rows_of(p), b], z, z_plus, z_minus,
                        b3.at[0], b3.at[1], (b4.at[0], b4.at[1]), (b4.at[2], b4.at[3])),
        )

    pre = exchange(win_ref, pre_in)
    gather_x = ctx_gather(xg)
    gather_x.start()
    for load in loads[5:6]:
        load.wait()
    out_rows = proj_ref[...].astype(f32)
    wo[z, x] = jnp.concatenate(
        [out_rows[:, 128 * w : 128 * w + 128] for w in range(8)], 0
    ).astype(bf16)
    out_w = out_gather()
    out_w[0].start()
    for load in loads[6:]:
        load.wait()
    own = wf.at[z, x]
    own[:, 0:512] = gate_ref[:, 0:512]
    own[:, 512:1024] = up_ref[:, 0:512]
    own[:, 1024:1152] = jnp.concatenate([gate_ref[:, 512:576], up_ref[:, 512:576]], 1)
    own[:, 1152:1792] = jnp.concatenate([down_ref[...], jnp.zeros((64, 64), bf16)], 1)
    ffn_w = weight_gather(wf, 896)
    ffn_w[0].start()
    ffn_w[1].start()
    cotg[y, core] = cot_ref[0]
    out_w[0].finish()
    out_w[1].start()
    exchanged(pre, pre_in)
    wi[z, x] = pre_in[:, :, 0:384].reshape(64, 384).astype(bf16)
    summed = jnp.sum(pre_in[:, :, 384:512], axis=0)
    tile = jnp.where(row < 2, summed, own_pack)
    wp[z, x] = jnp.concatenate([tile, jnp.zeros_like(tile)], 0).astype(bf16)
    in_w = in_gather()
    for part in (in_w[2], in_w[0], in_w[1]):
        part.start()
    gather_x.forward()
    out_w[1].finish()
    slab = wo[...].astype(f32).reshape(16, 8, 8, 128)
    for w in range(8):
        wog[y, core, :, 128 * w : 128 * w + 128] = slab[:, w].reshape(128, 128).astype(bf16)
    gather_out = ctx_gather(wog)
    gather_out.start()
    for part, later in ((in_w[2], in_w[5]), (in_w[0], in_w[3]), (in_w[1], in_w[4])):
        part.finish()
        later.start()
    ffn_w[0].finish()
    ffn_w[2].start()
    ffn_w[1].finish()
    ffn_w[3].start()
    gather_x.sides()
    gather_x.across()
    gather_x.finish_near()
    gather_x.finish_sides()
    gather_x.finish_far()

    def first_scale(g, carry):
        values = xg[g].reshape(256, 1024).astype(f32)
        scale_g[g] = lax.rsqrt(jnp.mean(values * values, axis=-1, keepdims=True) + epsilon)
        return carry

    lax.fori_loop(0, 4, first_scale, 0)
    in_w[5].finish()

    packs = [wp[i // 4, i % 4].astype(f32)[0:8] for i in range(16)]
    gain_one = jnp.concatenate([packs[2 * w][0:1] + packs[2 * w + 1][0:1] for w in range(8)], 1)
    gain_two = jnp.concatenate([packs[2 * w][1:2] + packs[2 * w + 1][1:2] for w in range(8)], 1)
    taps = packs[0]
    for i in range(1, 16):
        taps = taps + packs[i]
    tap = [taps[2 + k : 3 + k] for k in range(3)]

    def lift(g, carry):
        values = xg[g].reshape(256, 1024).astype(f32)
        h1g[g] = (values * scale_g[g] * gain_one).astype(bf16)
        return carry

    def project(g, carry):
        proj[g] = mm(h1g[g], wi[...].reshape(1024, 384))
        return carry

    lax.fori_loop(0, 4, lift, 0)
    gather_out.forward()
    in_w[3].finish()
    in_w[4].finish()
    lax.fori_loop(0, 4, project, 0)
    ffn_w[2].forward()
    ffn_w[3].forward()
    b_part = proj[:, :, 0:128].reshape(1024, 128)
    x_part = proj[:, :, 256:384].reshape(1024, 128)
    bx_pad[0:8] = jnp.zeros((8, 128), f32)
    bx_pad[8:1032] = (b_part * x_part).astype(bf16).astype(f32)
    z_all = tap[0] * bx_pad[6:1030] + tap[1] * bx_pad[7:1031] + tap[2] * bx_pad[8:1032]
    z_buf[...] = z_all
    y_buf[...] = (proj[:, :, 128:256].reshape(1024, 128) * z_all).astype(bf16).reshape(8, 128, 128)
    swap_y = exchange(y_buf, y_own)
    y_own[c] = y_buf[c]
    gather_out.sides()
    gather_out.across()
    gather_cot = ctx_gather(cotg)
    gather_cot.start()
    exchanged(swap_y, y_own)
    gather_out.finish_near()
    gather_out.finish_sides()
    gather_out.finish_far()
    gated = jnp.concatenate([y_own[i] for i in range(8)], 1)
    middle = x_ref[0].astype(f32) + mm(gated, wog[...].reshape(1024, 1024))
    scale_two = lax.rsqrt(jnp.mean(middle * middle, axis=-1, keepdims=True) + epsilon)
    h2g[y, core] = (middle * scale_two * gain_two).astype(bf16)
    gather_h2 = ctx_gather(h2g)
    gather_h2.start()
    gather_h2.forward()
    gather_cot.forward()
    ffn_w[2].finish()
    ffn_w[3].finish()
    gather_h2.finish_near()
    gather_cot.finish_near()

    scatter_dh2 = ctx_scatter(0, own_first=True)
    low_half = lax.broadcasted_iota(jnp.int32, (256, 128), 1) < 64

    def feed_forward(step, carry):
        g = scatter_dh2.group(step)

        @pl.when(step == 1)
        def _():
            gather_h2.sides()
            gather_cot.sides()
            gather_h2.finish_sides()
            gather_cot.finish_sides()

        @pl.when(step == 2)
        def _():
            scatter_dh2.side_left()
            gather_h2.across()
            gather_cot.across()
            gather_h2.finish_far()
            gather_cot.finish_far()

        @pl.when(step == 3)
        def _():
            scatter_dh2.start()

        w_gu = wf[:, :, :, 0:GU].reshape(1024, GU)
        gu = mm(h2g[g].reshape(256, 1024), w_gu)
        mixed = gu[:, 1024:1152]
        gating = jnp.concatenate([gu[:, 0:512], mixed], 1)
        upward = jnp.concatenate([gu[:, 512:1024], pltpu.roll(mixed, 64, 1)], 1)
        sigma = 1.0 / (1.0 + jnp.exp(-gating))
        activated = gating * sigma
        hidden = activated * upward
        hid_buf[g, :, 0:512] = hidden[:, 0:512].astype(bf16)
        hid_buf[g, :, 512:640] = jnp.where(low_half, hidden[:, 512:640], 0.0).astype(bf16)
        w_down = wf[:, :, :, GU:FFL].reshape(1024, HID)
        d_hidden = mm(cotg[g].reshape(256, 1024), w_down)
        d_gating = d_hidden * upward * sigma * (1.0 + gating * (1.0 - sigma))
        d_upward = d_hidden * activated
        d_mixed = jnp.where(low_half, d_gating[:, 512:640], pltpu.roll(d_upward[:, 512:640], 64, 1))
        d_gu = jnp.concatenate([d_gating[:, 0:512], d_upward[:, 0:512], d_mixed], 1).astype(bf16)
        dgu_buf[g] = d_gu
        rs_part[0, g] = mt(d_gu, w_gu).astype(bf16).reshape(2, 128, 1024)
        scatter_dh2.cross(step)
        return carry

    lax.fori_loop(0, 4, feed_forward, 0)
    scatter_dh2.side_right()

    def grad_ffn(i, carry):
        lanes = pl.ds(pl.multiple_of(i * 256, 256), 256)
        lhs = h2g[:, :, :, lanes].reshape(1024, 256)
        gf[i, :, :, 0:GU] = tm(lhs, dgu_buf[...].reshape(1024, GU)).astype(bf16).reshape(4, 64, GU)
        lhs = cotg[:, :, :, lanes].reshape(1024, 256)
        gf[i, :, :, GU:FFL] = (
            tm(lhs, hid_buf[...].reshape(1024, HID)).astype(bf16).reshape(4, 64, HID)
        )

        @pl.when(i == 1)
        def _():
            scatter_dh2.middle()

        return carry

    lax.fori_loop(0, 2, grad_ffn, 0)
    scatter_out = ctx_scatter(1)

    def ffn_out(step, carry):
        g = scatter_out.group(step)
        w_down = wf[:, :, :, GU:FFL].reshape(1024, HID)
        rs_part[1, g] = mt(hid_buf[g], w_down).astype(bf16).reshape(2, 128, 1024)
        scatter_out.cross(step)
        return carry

    lax.fori_loop(0, 4, ffn_out, 0)
    scatter_out.start()
    scatter_out.side_left()
    scatter_out.side_right()
    lax.fori_loop(2, 4, grad_ffn, 0)
    ffn_g = weight_scatter(gf, 896, 32, gf_a1, gf_a2, gf_b1, gf_b2, gf_a3, gf_a4, gf_b3, gf_b4)
    ffn_g[0].start()
    ffn_g[1].start()

    d_second = scatter_dh2.finish()
    normed_two = middle * scale_two
    grad_gain_two = jnp.sum(d_second * normed_two, axis=0, keepdims=True)
    scaled = d_second * gain_two
    d_middle = cot_ref[0].astype(f32) + scale_two * (
        scaled - normed_two * jnp.mean(scaled * normed_two, axis=-1, keepdims=True)
    )
    d_branch = d_middle.astype(bf16)
    dg[y, core] = d_branch
    d_gated = mt(d_branch, wog[...].reshape(1024, 1024)).astype(bf16)
    for i in range(8):
        dy_buf[i] = d_gated[:, 128 * i : 128 * i + 128]
    swap_dy = exchange(dy_buf, dy_own)
    gather_d = ctx_gather(dg)
    dy_own[c] = dy_buf[c]
    gather_d.start()
    ffn_g[0].middle()
    ffn_g[1].middle()
    exchanged(swap_dy, dy_own)
    gather_d.forward()

    d_gated = dy_own[...].reshape(1024, 128).astype(f32)
    dz_pad[0:1024] = d_gated * proj[:, :, 128:256].reshape(1024, 128)
    dp_buf[:, :, 128:256] = (d_gated * z_buf[...]).astype(bf16).reshape(4, 256, 128)
    dz_pad[1024:1032] = jnp.zeros((8, 128), f32)
    d_bx = tap[2] * dz_pad[0:1024] + tap[1] * dz_pad[1:1025] + tap[0] * dz_pad[2:1026]
    d_bx = d_bx.reshape(4, 256, 128)
    dp_buf[:, :, 0:128] = (d_bx * proj[:, :, 256:384]).astype(bf16)
    dp_buf[:, :, 256:384] = (d_bx * proj[:, :, 0:128]).astype(bf16)
    grad_tap = [
        jnp.sum(dz_pad[0:1024] * bx_pad[6 + k : 1030 + k], axis=0, keepdims=True) for k in range(3)
    ]
    def grad_in(i, carry):
        lanes = pl.ds(pl.multiple_of(i * 256, 256), 256)
        lhs = h1g[:, :, lanes].reshape(1024, 256)
        gi[i] = tm(lhs, dp_buf[...].reshape(1024, 384)).astype(bf16).reshape(4, 64, 384)
        return carry

    lax.fori_loop(0, 4, grad_in, 0)
    in_g = in_scatter()
    in_g[0].start()
    in_g[1].start()
    scatter_dh1 = ctx_scatter(2)
    mix_acc[...] = jnp.zeros((8, 1024), f32)

    def branch_back(step, carry):
        g = scatter_dh1.group(step)
        d_lifted = mt(dp_buf[g], wi[...].reshape(1024, 384))
        rs_part[2, g] = d_lifted.astype(bf16).reshape(2, 128, 1024)
        scatter_dh1.cross(step)
        normed = xg[g].reshape(256, 1024).astype(f32) * scale_g[g]
        mix_acc[...] += jnp.sum((d_lifted * normed).reshape(32, 8, 1024), axis=0)
        return carry

    lax.fori_loop(0, 4, branch_back, 0)
    scatter_dh1.start()
    scatter_dh1.side_left()
    scatter_dh1.side_right()
    grad_mix = jnp.sum(mix_acc[...], axis=0, keepdims=True)
    for i in range(16):
        lanes = slice(128 * (i // 2), 128 * (i // 2) + 128)
        rows = [grad_mix[:, lanes], grad_gain_two[:, lanes], *grad_tap, jnp.zeros((11, 128), f32)]
        gp[i // 4, i % 4] = jnp.concatenate(rows, 0).astype(bf16)
    in_g[2].start()
    for part, later in ((in_g[0], in_g[3]), (in_g[1], in_g[4]), (in_g[2], in_g[5])):
        part.finish()
        later.start()
    scatter_dh1.middle()
    gather_d.sides()
    gather_d.across()
    gather_d.finish_near()
    gather_d.finish_sides()
    gather_d.finish_far()
    g_out = tm(y_buf[...].reshape(1024, 128), dg[...].reshape(1024, 1024))
    pieces = [g_out[:, 128 * w : 128 * w + 128].reshape(16, 1, 8, 128) for w in range(8)]
    go[...] = jnp.concatenate(pieces, 1).reshape(4, 4, 64, 128).astype(bf16)
    out_g = out_scatter()
    out_g[0].start()
    scatter_out.middle()
    ffn_g[0].finish()
    ffn_g[2].start()
    ffn_g[1].finish()
    ffn_g[3].start()
    out_g[0].finish()
    out_g[1].start()
    for part in in_g[3:6]:
        part.finish()

    post_send[:, :, 0:384] = gi[z, x].astype(f32).reshape(8, 8, 384)
    own_pack = gp[z, x].astype(f32)[0:8]
    for i in range(8):
        post_send[i, :, 384:512] = own_pack
    post = exchange(post_send, post_in)
    ffn_g[2].middle()
    ffn_g[3].middle()

    d_lifted = scatter_dh1.finish()
    local = x_ref[0].astype(f32)
    scale_one = lax.rsqrt(jnp.mean(local * local, axis=-1, keepdims=True) + epsilon)
    normed_one = local * scale_one
    scaled = d_lifted * gain_one
    gin_ref[...] = d_middle + scale_one * (
        scaled - normed_one * jnp.mean(scaled * normed_one, axis=-1, keepdims=True)
    )
    stores = [
        pltpu.make_async_copy(src, dst, local_sems.at[10 + i])
        for i, (src, dst) in enumerate(
            (
                (gin_ref, gin_hbm),
                (gff_ref, gff_hbm),
                (out_ref, out_hbm),
                (gwout_ref, gwout_hbm),
                (gwin_ref, gwin_hbm),
                (gpack_ref, gpack_hbm),
            )
        )
    ]
    stores[0].start()
    ffn_g[2].finish()
    ffn_g[3].finish()
    gff_ref[...] = gf[z, x].astype(f32)
    stores[1].start()
    out_ref[...] = (middle + scatter_out.finish()).astype(bf16)
    stores[2].start()
    out_g[1].finish()
    gwout_ref[...] = go[z, x].astype(f32)
    stores[3].start()
    post_in[c] = post_send[c]
    exchanged(post, post_in)
    gwin_ref[...] = post_in[:, :, 0:384]
    summed = jnp.sum(post_in[:, :, 384:512], axis=0)
    gpack_ref[...] = jnp.where(row < 2, summed, own_pack)
    stores[4].start()
    stores[5].start()
    for store in stores:
        store.wait()

    link.drain()
    for scatter in (scatter_dh2, scatter_out, scatter_dh1):
        scatter.drain()


def spread_kernel(
    block_ref,
    gin_ref,
    gff_ref,
    gwin_ref,
    gwout_ref,
    gpack_ref,
    o_block,
    o_gin,
    o_mix,
    o_in,
    o_tap,
    o_proj,
    o_ffn,
    o_gate,
    o_up,
    o_down,
):
    f = lax.axis_index("fsdp")
    c = lax.axis_index("ctx")
    lane = lax.broadcasted_iota(jnp.int32, (8, 128), 1)
    o_block[0] = block_ref[...]
    o_gin[0] = gin_ref[...]
    for b in range(3):
        blocks = [gwin_ref[i, :, 128 * b : 128 * b + 128] for i in range(8)]
        for v, block in enumerate(by_channel(blocks, lane, True)):
            o_in[:, 1024 * b + 128 * v : 1024 * b + 128 * v + 128] = block
    for w in range(8):
        o_proj[:, 128 * w : 128 * w + 128] = gwout_ref[8 * w : 8 * w + 8]
    small = gpack_ref[...]
    gains = pltpu.roll(small, lax.rem(256 - 64 * lax.rem(f, 2) - 8 * c, 128), 1)
    o_mix[...] = gains[0:1, 0:8]
    o_ffn[...] = gains[1:2, 0:8]
    o_tap[...] = pltpu.roll(small, lax.rem(128 - 8 * f, 128), 1)[2:5, 0:8]
    mixed = gff_ref[:, 1024:1152]
    o_gate[:, 0:512] = gff_ref[:, 0:512]
    o_gate[:, 512:576] = mixed[:, 0:64]
    o_up[:, 0:512] = gff_ref[:, 512:1024]
    o_up[:, 512:576] = pltpu.roll(mixed, 64, 1)[:, 0:64]
    o_down[...] = gff_ref[:, 1152:1728]


def per_device(
    inputs,
    mix_gain,
    in_proj,
    conv_kernel,
    out_proj,
    ffn_gain,
    gate_proj,
    up_proj,
    down_proj,
    cotangent,
):
    v = pltpu.VMEM
    anywhere = pl.BlockSpec(memory_space=pl.ANY)
    sems = 256
    out_shape = (
        jax.ShapeDtypeStruct((128, 1024), bf16),
        jax.ShapeDtypeStruct((128, 1024), f32),
        jax.ShapeDtypeStruct((64, FFL), f32),
        jax.ShapeDtypeStruct((8, 8, 384), f32),
        jax.ShapeDtypeStruct((64, 128), f32),
        jax.ShapeDtypeStruct((8, 128), f32),
    )
    scratch = [
        v(inputs.shape, bf16),
        v(cotangent.shape, bf16),
        v((1, 8), bf16),
        v(in_proj.shape, bf16),
        v(conv_kernel.shape, bf16),
        v(out_proj.shape, bf16),
        v((1, 8), bf16),
        v(gate_proj.shape, bf16),
        v(up_proj.shape, bf16),
        v(down_proj.shape[::-1], bf16),
        *[v(shape.shape, shape.dtype) for shape in out_shape],
        pltpu.SemaphoreType.DMA((16,)),
        pltpu.SemaphoreType.DMA((sems,)),
        pltpu.SemaphoreType.DMA((sems,)),
        v((8, 8, 512), f32),
        v((8, 128), f32),
        v((4, 2, 128, 1024), bf16),
        v((4, 2, 128, 1024), bf16),
        v((4, 2, 128, 1024), bf16),
        v((4, 2, 128, 1024), bf16),
        v((4, 4, 64, FFL), bf16),
        v((4, 4, 64, 384), bf16),
        v((4, 4, 16, 128), bf16),
        v((4, 4, 64, 128), bf16),
        v((8, 8, 512), f32),
        v((4, 2, 128, 1024), bf16),
        v((4, 256, 1024), bf16),
        v((4, 256, 1), f32),
        v((4, 256, 384), f32),
        v((1032, 128), f32),
        v((1024, 128), f32),
        v((8, 128, 128), bf16),
        v((8, 128, 128), bf16),
        v((8, 128, 128), bf16),
        v((8, 128, 128), bf16),
        v((4, 256, HID), bf16),
        v((4, 256, GU), bf16),
        v((1032, 128), f32),
        v((4, 256, 384), bf16),
        v((8, 1024), f32),
        v((3, 4, 2, 128, 1024), bf16),
        v((3, 4, 128, 1024), bf16),
        v((3, 2, 64, 1024), bf16),
        v((3, 2, 128, 1024), bf16),
        v((4, 4, 64, FFL), bf16),
        v((4, 4, 64, 384), bf16),
        v((4, 4, 16, 128), bf16),
        v((4, 4, 64, 128), bf16),
        v((2, 2, 64, 896), bf16),
        v((4, 2, 64, 896), bf16),
        v((2, 2, 64, 896), bf16),
        v((4, 2, 64, 896), bf16),
        v((2, 32, 896), bf16),
        v((4, 32, 896), bf16),
        v((2, 32, 896), bf16),
        v((4, 32, 896), bf16),
        v((2, 3, 4, 32, 384), bf16),
        v((2, 3, 32, 384), bf16),
        v((3, 4, 16, 128), bf16),
        v((3, 16, 128), bf16),
        v((3, 4, 64, 128), bf16),
        v((3, 64, 128), bf16),
        v((8, 8, 512), f32),
        v((8, 8, 512), f32),
    ]
    raw = pl.pallas_call(
        block_kernel,
        out_shape=out_shape,
        in_specs=[anywhere] * 10,
        out_specs=(anywhere,) * 6,
        scratch_shapes=scratch,
        compiler_params=pltpu.CompilerParams(
            collective_id=0, has_side_effects=True, vmem_limit_bytes=62 * 1024 * 1024
        ),
    )(
        inputs,
        cotangent,
        mix_gain.reshape(1, 8),
        in_proj,
        conv_kernel,
        out_proj,
        ffn_gain.reshape(1, 8),
        gate_proj,
        up_proj,
        down_proj.T,
    )
    made = pl.pallas_call(
        spread_kernel,
        out_shape=(
            jax.ShapeDtypeStruct(inputs.shape, bf16),
            jax.ShapeDtypeStruct(inputs.shape, f32),
            jax.ShapeDtypeStruct((1, 8), f32),
            jax.ShapeDtypeStruct(in_proj.shape, f32),
            jax.ShapeDtypeStruct(conv_kernel.shape, f32),
            jax.ShapeDtypeStruct(out_proj.shape, f32),
            jax.ShapeDtypeStruct((1, 8), f32),
            jax.ShapeDtypeStruct(gate_proj.shape, f32),
            jax.ShapeDtypeStruct(up_proj.shape, f32),
            jax.ShapeDtypeStruct(down_proj.shape[::-1], f32),
        ),
        grid=(1,),
        compiler_params=pltpu.CompilerParams(vmem_limit_bytes=62 * 1024 * 1024),
    )(*raw)
    return (*made[:2], made[2].reshape(8), *made[3:6], made[6].reshape(8), *made[7:9], made[9].T)


def solution(mesh):
    in_specs = (
        P("fsdp", "ctx", None),
        P(("fsdp", "ctx")),
        P(("fsdp", "ctx"), None),
        P(None, ("fsdp", "ctx")),
        P(("fsdp", "ctx"), None),
        P(("fsdp", "ctx")),
        P("fsdp", "ctx"),
        P("fsdp", "ctx"),
        P("ctx", "fsdp"),
        P("fsdp", "ctx", None),
    )
    out_specs = (
        P("fsdp", "ctx", None),
        P("fsdp", "ctx", None),
        P(("fsdp", "ctx")),
        P(("fsdp", "ctx"), None),
        P(None, ("fsdp", "ctx")),
        P(("fsdp", "ctx"), None),
        P(("fsdp", "ctx")),
        P("fsdp", "ctx"),
        P("fsdp", "ctx"),
        P("ctx", "fsdp"),
    )
    return jax.shard_map(
        per_device, mesh=mesh, in_specs=in_specs, out_specs=out_specs, check_vma=False
    )
```

```python
import jax
import jax.numpy as jnp
from jax import lax
from jax.experimental import pallas as pl
from jax.experimental.pallas import tpu as pltpu
from jax.sharding import PartitionSpec as P

epsilon = 1e-05
f32 = jnp.float32
bf16 = jnp.bfloat16
MESH = pl.DeviceIdType.MESH

GU = 1152
FFL = 1792
HID = 640


def mm(a, b):
    return lax.dot_general(a, b, (((1,), (0,)), ((), ())), preferred_element_type=f32)


def mt(a, b):
    return lax.dot_general(a, b, (((1,), (1,)), ((), ())), preferred_element_type=f32)


def tm(a, b):
    return lax.dot_general(a, b, (((0,), (0,)), ((), ())), preferred_element_type=f32)


def add_into(ref, *others):
    total = ref[...].astype(f32)
    for other in others:
        total = total + other[...].astype(f32)
    ref[...] = total.astype(ref.dtype)


class Link:
    def __init__(self, send_sems, recv_sems):
        self.send_sems, self.recv_sems = send_sems, recv_sems
        self.used = 0
        self.started = []

    def reserve(self, count):
        first = self.used
        self.used += count
        return first

    def copy(self, src, dst, device, slot):
        return pltpu.make_async_remote_copy(
            src_ref=src,
            dst_ref=dst,
            send_sem=self.send_sems.at[slot],
            recv_sem=self.recv_sems.at[slot],
            device_id=device,
            device_id_type=MESH,
        )

    def send(self, src, dst, device):
        slot = self.reserve(1)
        self.copy(src, dst, device, slot).start()
        self.started.append((src, device, slot))
        return (device, slot)

    def landed(self, handle, ref):
        device, slot = handle
        self.copy(ref, ref, device, slot).wait_recv()

    def drain(self):
        for src, device, slot in self.started:
            self.copy(src, src, device, slot).wait_send()


def ring(value, step):
    return lax.rem(value + step, 4)


class RingGather:
    def __init__(self, link, view, me, plus, minus):
        self.link, self.view, self.me, self.plus, self.minus = link, view, me, plus, minus
        self.left, self.far, self.right = ring(me, 3), ring(me, 2), ring(me, 1)

    def start(self):
        send = self.link.send
        lo, hi = self.view(self.me, 0), self.view(self.me, 1)
        self.p0, self.m1 = send(lo, lo, self.plus), send(hi, hi, self.minus)
        self.p1, self.m0 = send(hi, hi, self.plus), send(lo, lo, self.minus)

    def forward(self):
        part = self.view(self.left, 0)
        self.link.landed(self.p0, part)
        self.fp = self.link.send(part, part, self.plus)
        part = self.view(self.right, 1)
        self.link.landed(self.m1, part)
        self.fm = self.link.send(part, part, self.minus)

    def finish(self):
        self.link.landed(self.p1, self.view(self.left, 1))
        self.link.landed(self.m0, self.view(self.right, 0))
        self.link.landed(self.fp, self.view(self.far, 0))
        self.link.landed(self.fm, self.view(self.far, 1))


class RingScatter:
    def __init__(self, link, view, me, plus, minus, r1a, r1b, r2a, r2b):
        self.link, self.view, self.me, self.plus, self.minus = link, view, me, plus, minus
        self.r1a, self.r1b, self.r2a, self.r2b = r1a, r1b, r2a, r2b
        self.left, self.far, self.right = ring(me, 3), ring(me, 2), ring(me, 1)

    def start(self):
        send = self.link.send
        self.h1a = send(self.view(self.far, 0), self.r1a, self.plus)
        self.h1b = send(self.view(self.far, 1), self.r1b, self.minus)
        self.h2a1 = send(self.view(self.right, 1), self.r2a[1], self.plus)
        self.h2b0 = send(self.view(self.left, 0), self.r2b[0], self.minus)

    def middle(self):
        self.link.landed(self.h1a, self.r1a)
        add_into(self.view(self.right, 0), self.r1a)
        self.h2a0 = self.link.send(self.view(self.right, 0), self.r2a[0], self.plus)
        self.link.landed(self.h1b, self.r1b)
        add_into(self.view(self.left, 1), self.r1b)
        self.h2b1 = self.link.send(self.view(self.left, 1), self.r2b[1], self.minus)

    def finish(self):
        self.link.landed(self.h2a1, self.r2a[1])
        self.link.landed(self.h2b0, self.r2b[0])
        self.link.landed(self.h2a0, self.r2a[0])
        self.link.landed(self.h2b1, self.r2b[1])
        for part in (0, 1):
            add_into(self.view(self.me, part), self.r2a[part], self.r2b[part])


class DirectGather:
    def __init__(self, link, view, me, device):
        self.link, self.view, self.me, self.device = link, view, me, device

    def start(self):
        own = self.view(self.me, None)
        self.sent = [(s, self.link.send(own, own, self.device(s))) for s in (1, 3, 2)]

    def finish(self):
        for step, handle in self.sent:
            self.link.landed(handle, self.view(ring(self.me, 4 - step), None))


class DirectScatter:
    def __init__(self, link, view, me, device, landing):
        self.link, self.view, self.me, self.device, self.landing = link, view, me, device, landing

    def start(self):
        self.sent = [
            (s, self.link.send(self.view(ring(self.me, s), None), self.landing.at[s - 1], self.device(s)))
            for s in (1, 3, 2)
        ]

    def finish(self):
        for step, handle in self.sent:
            self.link.landed(handle, self.landing.at[step - 1])
        add_into(self.view(self.me, None), *[self.landing.at[i] for i in range(3)])


LO, HI = pl.ds(0, 64), pl.ds(64, 64)


class CtxGather:
    def __init__(self, link, buf, y, core, plus, minus, other):
        self.link, self.buf, self.y, self.core = link, buf, y, core
        self.plus, self.minus, self.other = plus, minus, other
        self.left, self.far, self.right = ring(y, 3), ring(y, 2), ring(y, 1)
        self.mate = 1 - core

    def half(self, which, part):
        return self.buf.at[which, self.core, (LO, HI)[part]]

    def start(self):
        send = self.link.send
        lo, hi = self.half(self.y, 0), self.half(self.y, 1)
        own = self.buf.at[self.y, self.core]
        self.p0, self.m1 = send(lo, lo, self.plus), send(hi, hi, self.minus)
        self.p1, self.m0 = send(hi, hi, self.plus), send(lo, lo, self.minus)
        self.near = send(own, own, self.other)
        self.late = []

    def pass_on(self, handle, which, part, device):
        half = self.half(which, part)
        self.link.landed(handle, half)
        onward = None if device is None else self.link.send(half, half, device)
        theirs = self.buf.at[which, self.mate, (LO, HI)[part]]
        self.late.append((self.link.send(half, half, self.other), theirs))
        return onward

    def forward(self):
        left, right = self.left, self.right
        self.fp = self.pass_on(self.p0, left, 0, self.plus)
        self.fm = self.pass_on(self.m1, right, 1, self.minus)

    def sides(self):
        self.pass_on(self.p1, self.left, 1, None)
        self.pass_on(self.m0, self.right, 0, None)

    def across(self):
        far = self.far
        self.pass_on(self.fp, far, 0, None)
        self.pass_on(self.fm, far, 1, None)

    def finish_near(self):
        self.link.landed(self.near, self.buf.at[self.y, self.mate])

    def finish_sides(self):
        for handle, ref in self.late[:4]:
            self.link.landed(handle, ref)

    def finish_far(self):
        for handle, ref in self.late[4:]:
            self.link.landed(handle, ref)


class CtxScatter:
    def __init__(self, link, part, rb, r1, r2, y, core, plus, minus, other, own_first):
        self.link, self.part, self.rb, self.r1, self.r2 = link, part, rb, r1, r2
        self.y, self.core, self.own_first = y, core, own_first
        self.plus, self.minus, self.other = plus, minus, other
        self.left, self.far, self.right = ring(y, 3), ring(y, 2), ring(y, 1)
        self.mate = 1 - core
        self.first = link.reserve(4)
        self.at_far, self.at_left, self.at_right, self.at_own = (2, 1, 3, 0) if own_first else (0, 1, 2, 3)

    def group(self, step):
        if self.own_first:
            return lax.rem(self.y + 3 * step, 4)
        return lax.rem(self.y + 2 + step + step // 2 + 2 * (step // 3), 4)

    def cross(self, step):
        g = self.group(step)
        self.link.copy(
            self.part.at[g, self.mate], self.rb.at[g], self.other, self.first + step
        ).start()

    def crossed(self, g, step):
        ref = self.rb.at[g]
        self.link.copy(ref, ref, self.other, self.first + step).wait_recv()

    def block(self, which, rows):
        return self.part.at[which, self.core, rows]

    def start(self):
        far = self.far
        self.crossed(far, self.at_far)
        add_into(self.block(far, LO), self.rb.at[far, LO])
        self.h1a = self.link.send(self.block(far, LO), self.r1.at[0], self.plus)
        add_into(self.block(far, HI), self.rb.at[far, HI])
        self.h1b = self.link.send(self.block(far, HI), self.r1.at[1], self.minus)

    def side_left(self):
        left = self.left
        self.crossed(left, self.at_left)
        add_into(self.block(left, LO), self.rb.at[left, LO])
        self.h2b0 = self.link.send(self.block(left, LO), self.r2.at[1, LO], self.minus)

    def side_right(self):
        right = self.right
        self.crossed(right, self.at_right)
        add_into(self.block(right, HI), self.rb.at[right, HI])
        self.h2a1 = self.link.send(self.block(right, HI), self.r2.at[0, HI], self.plus)

    def middle(self):
        left, right = self.left, self.right
        self.link.landed(self.h1a, self.r1.at[0])
        add_into(self.block(right, LO), self.rb.at[right, LO], self.r1.at[0])
        self.h2a0 = self.link.send(self.block(right, LO), self.r2.at[0, LO], self.plus)
        self.link.landed(self.h1b, self.r1.at[1])
        add_into(self.block(left, HI), self.rb.at[left, HI], self.r1.at[1])
        self.h2b1 = self.link.send(self.block(left, HI), self.r2.at[1, HI], self.minus)

    def finish(self):
        self.crossed(self.y, self.at_own)
        self.link.landed(self.h2b0, self.r2.at[1, LO])
        self.link.landed(self.h2a1, self.r2.at[0, HI])
        self.link.landed(self.h2a0, self.r2.at[0, LO])
        self.link.landed(self.h2b1, self.r2.at[1, HI])
        return (
            self.part[self.y, self.core].astype(f32)
            + self.rb[self.y].astype(f32)
            + self.r2[0].astype(f32)
            + self.r2[1].astype(f32)
        )

    def drain(self):
        for step in range(4):
            g = self.group(step)
            src = self.part.at[g, self.mate]
            self.link.copy(src, src, self.other, self.first + step).wait_send()


def by_channel(blocks, lane, inverse):
    made = []
    for target in range(8):
        total = jnp.zeros((8, 128), f32)
        for source in range(8):
            for h in range(2):
                if inverse:
                    start, lands = 16 * target + 8 * h, 64 * h + 8 * source
                else:
                    start, lands = 64 * h + 8 * target, 16 * source + 8 * h
                moved = pltpu.roll(blocks[source], (lands - start) % 128, 1)
                total = jnp.where((lane >= lands) & (lane < lands + 8), moved, total)
        made.append(total)
    return made


def block_kernel(
    x_hbm,
    cot_hbm,
    mix_hbm,
    in_hbm,
    tap_hbm,
    proj_hbm,
    ffn_hbm,
    gate_hbm,
    up_hbm,
    down_hbm,
    out_hbm,
    gin_hbm,
    gff_hbm,
    gwin_hbm,
    gwout_hbm,
    gpack_hbm,
    x_ref,
    cot_ref,
    mix_ref,
    in_ref,
    tap_ref,
    proj_ref,
    ffn_ref,
    gate_ref,
    up_ref,
    down_ref,
    out_ref,
    gin_ref,
    gff_ref,
    gwin_ref,
    gwout_ref,
    gpack_ref,
    local_sems,
    send_sems,
    recv_sems,
    win_ref,
    pack_ref,
    xg,
    cotg,
    h2g,
    dg,
    wf,
    wi,
    wp,
    wo,
    pre_in,
    wog,
    h1g,
    scale_g,
    proj,
    bx_pad,
    z_buf,
    y_buf,
    y_own,
    dy_buf,
    dy_own,
    hid_buf,
    dgu_buf,
    dz_pad,
    dp_buf,
    mix_acc,
    rs_part,
    rs_rb,
    rs_r1,
    rs_r2,
    gf,
    gi,
    gp,
    go,
    gf_a1,
    gf_a2,
    gf_b1,
    gf_b2,
    gf_a3,
    gf_a4,
    gf_b3,
    gf_b4,
    gi_r1,
    gi_r2,
    gp_r1,
    gp_r2,
    go_r1,
    go_r2,
    post_send,
    post_in,
):
    loads = [
        pltpu.make_async_copy(src, dst, local_sems.at[i])
        for i, (src, dst) in enumerate(
            (
                (x_hbm, x_ref),
                (in_hbm, in_ref),
                (mix_hbm, mix_ref),
                (ffn_hbm, ffn_ref),
                (tap_hbm, tap_ref),
                (proj_hbm, proj_ref),
                (gate_hbm, gate_ref),
                (up_hbm, up_ref),
                (down_hbm, down_ref),
                (cot_hbm, cot_ref),
            )
        )
    ]
    for load in loads:
        load.start()
    f = lax.axis_index("fsdp")
    c = lax.axis_index("ctx")
    z, x = f // 4, lax.rem(f, 4)
    y, core = c // 2, lax.rem(c, 2)
    y_plus, y_minus = (f, ring(y, 1) * 2 + core), (f, ring(y, 3) * 2 + core)
    other = (f, y * 2 + 1 - core)
    x_plus, x_minus = (z * 4 + ring(x, 1), c), (z * 4 + ring(x, 3), c)
    z_plus, z_minus = (ring(z, 1) * 4 + x, c), (ring(z, 3) * 4 + x, c)

    def along_x(step):
        return (z * 4 + ring(x, step), c)

    def along_z(step):
        return (ring(z, step) * 4 + x, c)

    mates = [(f, lax.rem(c + step, 8)) for step in range(1, 8)]

    barrier = pltpu.get_barrier_semaphore()
    rings = [along_x(step) for step in (1, 2, 3)] + [along_z(step) for step in (1, 2, 3)]
    for device in mates + rings:
        pl.semaphore_signal(barrier, inc=1, device_id=device, device_id_type=MESH)

    lane = lax.broadcasted_iota(jnp.int32, (8, 128), 1)
    row = lax.broadcasted_iota(jnp.int32, (8, 128), 0)
    for load in loads[:5]:
        load.wait()
    xg[y, core] = x_ref[0]
    in_rows = in_ref[...].astype(f32)
    for b in range(3):
        blocks = [in_rows[:, 1024 * b + 128 * v : 1024 * b + 128 * v + 128] for v in range(8)]
        for channel, block in enumerate(by_channel(blocks, lane, False)):
            win_ref[channel, :, 128 * b : 128 * b + 128] = block
    pack_ref[...] = jnp.zeros((8, 128), f32)
    pack_ref[0:1, 0:8] = mix_ref[...].astype(f32)
    pack_ref[1:2, 0:8] = ffn_ref[...].astype(f32)
    pack_ref[2:5, 0:8] = tap_ref[...].astype(f32)
    small = pack_ref[...]
    gains = pltpu.roll(small, 64 * lax.rem(f, 2) + 8 * c, 1)
    own_pack = jnp.where(row < 2, gains, pltpu.roll(small, 8 * f, 1))
    for i in range(8):
        win_ref[i, :, 384:512] = own_pack
    pre_in[c] = win_ref[c]
    pl.semaphore_wait(barrier, 13)

    link = Link(send_sems, recv_sems)

    def ctx_gather(buf):
        return CtxGather(link, buf, y, core, y_plus, y_minus, other)

    def ctx_scatter(n, own_first=False):
        return CtxScatter(
            link, rs_part.at[n], rs_rb.at[n], rs_r1.at[n], rs_r2.at[n],
            y, core, y_plus, y_minus, other, own_first,
        )

    def exchange(blocks, landing):
        return [link.send(blocks.at[mate[1]], landing.at[c], mate) for mate in mates]

    def exchanged(handles, landing):
        for step, handle in enumerate(handles):
            link.landed(handle, landing.at[lax.rem(c + 7 - step, 8)])

    def weight_gather(buf, half):
        rest = buf.shape[3] - half
        a, b = pl.ds(0, half), pl.ds(half, rest)

        def pair(part):
            return pl.ds(0, 4) if part is None else pl.ds(2 * part, 2)

        return (
            DirectGather(link, lambda i, p: buf.at[z, i, :, a], x, along_x),
            DirectGather(link, lambda i, p: buf.at[i, x, :, b], z, along_z),
            RingGather(link, lambda i, p: buf.at[i, pair(p), :, a], z, z_plus, z_minus),
            RingGather(link, lambda i, p: buf.at[pair(p), i, :, b], x, x_plus, x_minus),
        )

    low, high = pl.ds(0, 32), pl.ds(32, 32)

    def in_gather():
        return (
            DirectGather(link, lambda i, p: wi.at[z, i, low], x, along_x),
            DirectGather(link, lambda i, p: wi.at[i, x, high], z, along_z),
            DirectGather(link, lambda i, p: wp.at[z, i], x, along_x),
            DirectGather(link, lambda i, p: wi.at[i, :, low], z, along_z),
            DirectGather(link, lambda i, p: wi.at[:, i, high], x, along_x),
            DirectGather(link, lambda i, p: wp.at[i], z, along_z),
        )

    def out_gather():
        return (
            DirectGather(link, lambda i, p: wo.at[i, x], z, along_z),
            DirectGather(link, lambda i, p: wo.at[:, i], x, along_x),
        )

    def in_scatter():
        return (
            DirectScatter(link, lambda i, p: gi.at[i, :, low], z, along_z, gi_r1.at[0]),
            DirectScatter(link, lambda i, p: gi.at[:, i, high], x, along_x, gi_r1.at[1]),
            DirectScatter(link, lambda i, p: gp.at[i], z, along_z, gp_r1),
            DirectScatter(link, lambda i, p: gi.at[z, i, low], x, along_x, gi_r2.at[0]),
            DirectScatter(link, lambda i, p: gi.at[i, x, high], z, along_z, gi_r2.at[1]),
            DirectScatter(link, lambda i, p: gp.at[z, i], x, along_x, gp_r2),
        )

    def out_scatter():
        return (
            DirectScatter(link, lambda i, p: go.at[:, i], x, along_x, go_r1),
            DirectScatter(link, lambda i, p: go.at[i, x], z, along_z, go_r2),
        )

    def weight_scatter(buf, half, low, a1, a2, b1, b2, a3, a4, b3, b4):
        rest = buf.shape[3] - half
        rows = buf.shape[2]
        a, b = pl.ds(0, half), pl.ds(half, rest)

        def rows_of(part):
            return pl.ds(0, rows) if part is None else (pl.ds(0, low), pl.ds(low, rows - low))[part]

        def pair(part):
            return pl.ds(0, 4) if part is None else pl.ds(2 * part, 2)

        return (
            RingScatter(link, lambda i, p: buf.at[i, pair(p), :, a], z, z_plus, z_minus,
                        a1.at[0], a1.at[1], (a2.at[0], a2.at[1]), (a2.at[2], a2.at[3])),
            RingScatter(link, lambda i, p: buf.at[pair(p), i, :, b], x, x_plus, x_minus,
                        b1.at[0], b1.at[1], (b2.at[0], b2.at[1]), (b2.at[2], b2.at[3])),
            RingScatter(link, lambda i, p: buf.at[z, i, rows_of(p), a], x, x_plus, x_minus,
                        a3.at[0], a3.at[1], (a4.at[0], a4.at[1]), (a4.at[2], a4.at[3])),
            RingScatter(link, lambda i, p: buf.at[i, x, rows_of(p), b], z, z_plus, z_minus,
                        b3.at[0], b3.at[1], (b4.at[0], b4.at[1]), (b4.at[2], b4.at[3])),
        )

    pre = exchange(win_ref, pre_in)
    gather_x = ctx_gather(xg)
    for load in loads[5:6]:
        load.wait()
    out_rows = proj_ref[...].astype(f32)
    wo[z, x] = jnp.concatenate(
        [out_rows[:, 128 * w : 128 * w + 128] for w in range(8)], 0
    ).astype(bf16)
    out_w = out_gather()
    out_w[0].start()
    for load in loads[6:]:
        load.wait()
    own = wf.at[z, x]
    own[:, 0:512] = gate_ref[:, 0:512]
    own[:, 512:1024] = up_ref[:, 0:512]
    own[:, 1024:1152] = jnp.concatenate([gate_ref[:, 512:576], up_ref[:, 512:576]], 1)
    own[:, 1152:1792] = jnp.concatenate([down_ref[...], jnp.zeros((64, 64), bf16)], 1)
    ffn_w = weight_gather(wf, 896)
    ffn_w[0].start()
    ffn_w[1].start()
    cotg[y, core] = cot_ref[0]
    out_w[0].finish()
    out_w[1].start()
    exchanged(pre, pre_in)
    gather_x.start()
    wi[z, x] = pre_in[:, :, 0:384].reshape(64, 384).astype(bf16)
    summed = jnp.sum(pre_in[:, :, 384:512], axis=0)
    tile = jnp.where(row < 2, summed, own_pack)
    wp[z, x] = jnp.concatenate([tile, jnp.zeros_like(tile)], 0).astype(bf16)
    in_w = in_gather()
    for part in (in_w[2], in_w[0], in_w[1]):
        part.start()
    gather_x.forward()
    out_w[1].finish()
    slab = wo[...].astype(f32).reshape(16, 8, 8, 128)
    for w in range(8):
        wog[y, core, :, 128 * w : 128 * w + 128] = slab[:, w].reshape(128, 128).astype(bf16)
    gather_out = ctx_gather(wog)
    gather_out.start()
    for part, later in ((in_w[2], in_w[5]), (in_w[0], in_w[3]), (in_w[1], in_w[4])):
        part.finish()
        later.start()
    ffn_w[0].finish()
    ffn_w[2].start()
    ffn_w[1].finish()
    ffn_w[3].start()
    gather_x.sides()
    gather_x.across()
    gather_x.finish_near()
    gather_x.finish_sides()
    gather_x.finish_far()

    def first_scale(g, carry):
        values = xg[g].reshape(256, 1024).astype(f32)
        scale_g[g] = lax.rsqrt(jnp.mean(values * values, axis=-1, keepdims=True) + epsilon)
        return carry

    lax.fori_loop(0, 4, first_scale, 0)
    in_w[5].finish()

    packs = [wp[i // 4, i % 4].astype(f32)[0:8] for i in range(16)]
    gain_one = jnp.concatenate([packs[2 * w][0:1] + packs[2 * w + 1][0:1] for w in range(8)], 1)
    gain_two = jnp.concatenate([packs[2 * w][1:2] + packs[2 * w + 1][1:2] for w in range(8)], 1)
    taps = packs[0]
    for i in range(1, 16):
        taps = taps + packs[i]
    tap = [taps[2 + k : 3 + k] for k in range(3)]

    def lift(g, carry):
        values = xg[g].reshape(256, 1024).astype(f32)
        h1g[g] = (values * scale_g[g] * gain_one).astype(bf16)
        return carry

    def project(g, carry):
        proj[g] = mm(h1g[g], wi[...].reshape(1024, 384))
        return carry

    lax.fori_loop(0, 4, lift, 0)
    gather_out.forward()
    in_w[3].finish()
    in_w[4].finish()
    lax.fori_loop(0, 4, project, 0)
    ffn_w[2].forward()
    ffn_w[3].forward()
    b_part = proj[:, :, 0:128].reshape(1024, 128)
    x_part = proj[:, :, 256:384].reshape(1024, 128)
    bx_pad[0:8] = jnp.zeros((8, 128), f32)
    bx_pad[8:1032] = (b_part * x_part).astype(bf16).astype(f32)
    z_all = tap[0] * bx_pad[6:1030] + tap[1] * bx_pad[7:1031] + tap[2] * bx_pad[8:1032]
    z_buf[...] = z_all
    y_buf[...] = (proj[:, :, 128:256].reshape(1024, 128) * z_all).astype(bf16).reshape(8, 128, 128)
    swap_y = exchange(y_buf, y_own)
    y_own[c] = y_buf[c]
    gather_out.sides()
    gather_out.across()
    gather_cot = ctx_gather(cotg)
    gather_cot.start()
    exchanged(swap_y, y_own)
    gather_out.finish_near()
    gather_out.finish_sides()
    gather_out.finish_far()
    gated = jnp.concatenate([y_own[i] for i in range(8)], 1)
    middle = x_ref[0].astype(f32) + mm(gated, wog[...].reshape(1024, 1024))
    scale_two = lax.rsqrt(jnp.mean(middle * middle, axis=-1, keepdims=True) + epsilon)
    h2g[y, core] = (middle * scale_two * gain_two).astype(bf16)
    gather_h2 = ctx_gather(h2g)
    gather_h2.start()
    gather_h2.forward()
    gather_cot.forward()
    ffn_w[2].finish()
    ffn_w[3].finish()
    gather_h2.finish_near()
    gather_cot.finish_near()

    scatter_dh2 = ctx_scatter(0, own_first=True)
    low_half = lax.broadcasted_iota(jnp.int32, (256, 128), 1) < 64

    def feed_forward(step, carry):
        g = scatter_dh2.group(step)

        @pl.when(step == 1)
        def _():
            gather_h2.sides()
            gather_cot.sides()
            gather_h2.finish_sides()
            gather_cot.finish_sides()

        @pl.when(step == 2)
        def _():
            scatter_dh2.side_left()
            gather_h2.across()
            gather_cot.across()
            gather_h2.finish_far()
            gather_cot.finish_far()

        @pl.when(step == 3)
        def _():
            scatter_dh2.start()

        w_gu = wf[:, :, :, 0:GU].reshape(1024, GU)
        gu = mm(h2g[g].reshape(256, 1024), w_gu)
        mixed = gu[:, 1024:1152]
        gating = jnp.concatenate([gu[:, 0:512], mixed], 1)
        upward = jnp.concatenate([gu[:, 512:1024], pltpu.roll(mixed, 64, 1)], 1)
        sigma = 1.0 / (1.0 + jnp.exp(-gating))
        activated = gating * sigma
        hidden = activated * upward
        hid_buf[g, :, 0:512] = hidden[:, 0:512].astype(bf16)
        hid_buf[g, :, 512:640] = jnp.where(low_half, hidden[:, 512:640], 0.0).astype(bf16)
        w_down = wf[:, :, :, GU:FFL].reshape(1024, HID)
        d_hidden = mm(cotg[g].reshape(256, 1024), w_down)
        d_gating = d_hidden * upward * sigma * (1.0 + gating * (1.0 - sigma))
        d_upward = d_hidden * activated
        d_mixed = jnp.where(low_half, d_gating[:, 512:640], pltpu.roll(d_upward[:, 512:640], 64, 1))
        d_gu = jnp.concatenate([d_gating[:, 0:512], d_upward[:, 0:512], d_mixed], 1).astype(bf16)
        dgu_buf[g] = d_gu
        rs_part[0, g] = mt(d_gu, w_gu).astype(bf16).reshape(2, 128, 1024)
        scatter_dh2.cross(step)
        return carry

    lax.fori_loop(0, 4, feed_forward, 0)
    scatter_dh2.side_right()

    def grad_ffn(i, carry):
        lanes = pl.ds(pl.multiple_of(i * 256, 256), 256)
        lhs = h2g[:, :, :, lanes].reshape(1024, 256)
        gf[i, :, :, 0:GU] = tm(lhs, dgu_buf[...].reshape(1024, GU)).astype(bf16).reshape(4, 64, GU)
        lhs = cotg[:, :, :, lanes].reshape(1024, 256)
        gf[i, :, :, GU:FFL] = (
            tm(lhs, hid_buf[...].reshape(1024, HID)).astype(bf16).reshape(4, 64, HID)
        )

        @pl.when(i == 1)
        def _():
            scatter_dh2.middle()

        return carry

    lax.fori_loop(0, 2, grad_ffn, 0)
    scatter_out = ctx_scatter(1)

    def ffn_out(step, carry):
        g = scatter_out.group(step)
        w_down = wf[:, :, :, GU:FFL].reshape(1024, HID)
        rs_part[1, g] = mt(hid_buf[g], w_down).astype(bf16).reshape(2, 128, 1024)
        scatter_out.cross(step)
        return carry

    lax.fori_loop(0, 4, ffn_out, 0)
    scatter_out.start()
    scatter_out.side_left()
    scatter_out.side_right()
    lax.fori_loop(2, 4, grad_ffn, 0)
    ffn_g = weight_scatter(gf, 896, 32, gf_a1, gf_a2, gf_b1, gf_b2, gf_a3, gf_a4, gf_b3, gf_b4)
    ffn_g[0].start()
    ffn_g[1].start()

    d_second = scatter_dh2.finish()
    normed_two = middle * scale_two
    grad_gain_two = jnp.sum(d_second * normed_two, axis=0, keepdims=True)
    scaled = d_second * gain_two
    d_middle = cot_ref[0].astype(f32) + scale_two * (
        scaled - normed_two * jnp.mean(scaled * normed_two, axis=-1, keepdims=True)
    )
    d_branch = d_middle.astype(bf16)
    dg[y, core] = d_branch
    d_gated = mt(d_branch, wog[...].reshape(1024, 1024)).astype(bf16)
    for i in range(8):
        dy_buf[i] = d_gated[:, 128 * i : 128 * i + 128]
    swap_dy = exchange(dy_buf, dy_own)
    gather_d = ctx_gather(dg)
    dy_own[c] = dy_buf[c]
    gather_d.start()
    ffn_g[0].middle()
    ffn_g[1].middle()
    exchanged(swap_dy, dy_own)
    gather_d.forward()

    d_gated = dy_own[...].reshape(1024, 128).astype(f32)
    dz_pad[0:1024] = d_gated * proj[:, :, 128:256].reshape(1024, 128)
    dp_buf[:, :, 128:256] = (d_gated * z_buf[...]).astype(bf16).reshape(4, 256, 128)
    dz_pad[1024:1032] = jnp.zeros((8, 128), f32)
    d_bx = tap[2] * dz_pad[0:1024] + tap[1] * dz_pad[1:1025] + tap[0] * dz_pad[2:1026]
    d_bx = d_bx.reshape(4, 256, 128)
    dp_buf[:, :, 0:128] = (d_bx * proj[:, :, 256:384]).astype(bf16)
    dp_buf[:, :, 256:384] = (d_bx * proj[:, :, 0:128]).astype(bf16)
    grad_tap = [
        jnp.sum(dz_pad[0:1024] * bx_pad[6 + k : 1030 + k], axis=0, keepdims=True) for k in range(3)
    ]
    def grad_in(i, carry):
        lanes = pl.ds(pl.multiple_of(i * 256, 256), 256)
        lhs = h1g[:, :, lanes].reshape(1024, 256)
        gi[i] = tm(lhs, dp_buf[...].reshape(1024, 384)).astype(bf16).reshape(4, 64, 384)
        return carry

    lax.fori_loop(0, 4, grad_in, 0)
    in_g = in_scatter()
    in_g[0].start()
    in_g[1].start()
    scatter_dh1 = ctx_scatter(2)
    mix_acc[...] = jnp.zeros((8, 1024), f32)

    def branch_back(step, carry):
        g = scatter_dh1.group(step)
        d_lifted = mt(dp_buf[g], wi[...].reshape(1024, 384))
        rs_part[2, g] = d_lifted.astype(bf16).reshape(2, 128, 1024)
        scatter_dh1.cross(step)
        normed = xg[g].reshape(256, 1024).astype(f32) * scale_g[g]
        mix_acc[...] += jnp.sum((d_lifted * normed).reshape(32, 8, 1024), axis=0)
        return carry

    lax.fori_loop(0, 4, branch_back, 0)
    scatter_dh1.start()
    scatter_dh1.side_left()
    scatter_dh1.side_right()
    grad_mix = jnp.sum(mix_acc[...], axis=0, keepdims=True)
    for i in range(16):
        lanes = slice(128 * (i // 2), 128 * (i // 2) + 128)
        rows = [grad_mix[:, lanes], grad_gain_two[:, lanes], *grad_tap, jnp.zeros((11, 128), f32)]
        gp[i // 4, i % 4] = jnp.concatenate(rows, 0).astype(bf16)
    in_g[2].start()
    for part, later in ((in_g[0], in_g[3]), (in_g[1], in_g[4]), (in_g[2], in_g[5])):
        part.finish()
        later.start()
    scatter_dh1.middle()
    gather_d.sides()
    gather_d.across()
    gather_d.finish_near()
    gather_d.finish_sides()
    gather_d.finish_far()
    g_out = tm(y_buf[...].reshape(1024, 128), dg[...].reshape(1024, 1024))
    pieces = [g_out[:, 128 * w : 128 * w + 128].reshape(16, 1, 8, 128) for w in range(8)]
    go[...] = jnp.concatenate(pieces, 1).reshape(4, 4, 64, 128).astype(bf16)
    out_g = out_scatter()
    out_g[0].start()
    scatter_out.middle()
    ffn_g[0].finish()
    ffn_g[2].start()
    ffn_g[1].finish()
    ffn_g[3].start()
    out_g[0].finish()
    out_g[1].start()
    for part in in_g[3:6]:
        part.finish()

    post_send[:, :, 0:384] = gi[z, x].astype(f32).reshape(8, 8, 384)
    own_pack = gp[z, x].astype(f32)[0:8]
    for i in range(8):
        post_send[i, :, 384:512] = own_pack
    post = exchange(post_send, post_in)
    ffn_g[2].middle()
    ffn_g[3].middle()

    d_lifted = scatter_dh1.finish()
    local = x_ref[0].astype(f32)
    scale_one = lax.rsqrt(jnp.mean(local * local, axis=-1, keepdims=True) + epsilon)
    normed_one = local * scale_one
    scaled = d_lifted * gain_one
    gin_ref[...] = d_middle + scale_one * (
        scaled - normed_one * jnp.mean(scaled * normed_one, axis=-1, keepdims=True)
    )
    stores = [
        pltpu.make_async_copy(src, dst, local_sems.at[10 + i])
        for i, (src, dst) in enumerate(
            (
                (gin_ref, gin_hbm),
                (gff_ref, gff_hbm),
                (out_ref, out_hbm),
                (gwout_ref, gwout_hbm),
                (gwin_ref, gwin_hbm),
                (gpack_ref, gpack_hbm),
            )
        )
    ]
    stores[0].start()
    ffn_g[2].finish()
    ffn_g[3].finish()
    gff_ref[...] = gf[z, x].astype(f32)
    stores[1].start()
    out_ref[...] = (middle + scatter_out.finish()).astype(bf16)
    stores[2].start()
    out_g[1].finish()
    gwout_ref[...] = go[z, x].astype(f32)
    stores[3].start()
    post_in[c] = post_send[c]
    exchanged(post, post_in)
    gwin_ref[...] = post_in[:, :, 0:384]
    summed = jnp.sum(post_in[:, :, 384:512], axis=0)
    gpack_ref[...] = jnp.where(row < 2, summed, own_pack)
    stores[4].start()
    stores[5].start()
    for store in stores:
        store.wait()

    link.drain()
    for scatter in (scatter_dh2, scatter_out, scatter_dh1):
        scatter.drain()


def spread_kernel(
    block_ref,
    gin_ref,
    gff_ref,
    gwin_ref,
    gwout_ref,
    gpack_ref,
    o_block,
    o_gin,
    o_mix,
    o_in,
    o_tap,
    o_proj,
    o_ffn,
    o_gate,
    o_up,
    o_down,
):
    f = lax.axis_index("fsdp")
    c = lax.axis_index("ctx")
    lane = lax.broadcasted_iota(jnp.int32, (8, 128), 1)
    o_block[0] = block_ref[...]
    o_gin[0] = gin_ref[...]
    for b in range(3):
        blocks = [gwin_ref[i, :, 128 * b : 128 * b + 128] for i in range(8)]
        for v, block in enumerate(by_channel(blocks, lane, True)):
            o_in[:, 1024 * b + 128 * v : 1024 * b + 128 * v + 128] = block
    for w in range(8):
        o_proj[:, 128 * w : 128 * w + 128] = gwout_ref[8 * w : 8 * w + 8]
    small = gpack_ref[...]
    gains = pltpu.roll(small, lax.rem(256 - 64 * lax.rem(f, 2) - 8 * c, 128), 1)
    o_mix[...] = gains[0:1, 0:8]
    o_ffn[...] = gains[1:2, 0:8]
    o_tap[...] = pltpu.roll(small, lax.rem(128 - 8 * f, 128), 1)[2:5, 0:8]
    mixed = gff_ref[:, 1024:1152]
    o_gate[:, 0:512] = gff_ref[:, 0:512]
    o_gate[:, 512:576] = mixed[:, 0:64]
    o_up[:, 0:512] = gff_ref[:, 512:1024]
    o_up[:, 512:576] = pltpu.roll(mixed, 64, 1)[:, 0:64]
    o_down[...] = gff_ref[:, 1152:1728]


def per_device(
    inputs,
    mix_gain,
    in_proj,
    conv_kernel,
    out_proj,
    ffn_gain,
    gate_proj,
    up_proj,
    down_proj,
    cotangent,
):
    v = pltpu.VMEM
    anywhere = pl.BlockSpec(memory_space=pl.ANY)
    sems = 256
    out_shape = (
        jax.ShapeDtypeStruct((128, 1024), bf16),
        jax.ShapeDtypeStruct((128, 1024), f32),
        jax.ShapeDtypeStruct((64, FFL), f32),
        jax.ShapeDtypeStruct((8, 8, 384), f32),
        jax.ShapeDtypeStruct((64, 128), f32),
        jax.ShapeDtypeStruct((8, 128), f32),
    )
    scratch = [
        v(inputs.shape, bf16),
        v(cotangent.shape, bf16),
        v((1, 8), bf16),
        v(in_proj.shape, bf16),
        v(conv_kernel.shape, bf16),
        v(out_proj.shape, bf16),
        v((1, 8), bf16),
        v(gate_proj.shape, bf16),
        v(up_proj.shape, bf16),
        v(down_proj.shape[::-1], bf16),
        *[v(shape.shape, shape.dtype) for shape in out_shape],
        pltpu.SemaphoreType.DMA((16,)),
        pltpu.SemaphoreType.DMA((sems,)),
        pltpu.SemaphoreType.DMA((sems,)),
        v((8, 8, 512), f32),
        v((8, 128), f32),
        v((4, 2, 128, 1024), bf16),
        v((4, 2, 128, 1024), bf16),
        v((4, 2, 128, 1024), bf16),
        v((4, 2, 128, 1024), bf16),
        v((4, 4, 64, FFL), bf16),
        v((4, 4, 64, 384), bf16),
        v((4, 4, 16, 128), bf16),
        v((4, 4, 64, 128), bf16),
        v((8, 8, 512), f32),
        v((4, 2, 128, 1024), bf16),
        v((4, 256, 1024), bf16),
        v((4, 256, 1), f32),
        v((4, 256, 384), f32),
        v((1032, 128), f32),
        v((1024, 128), f32),
        v((8, 128, 128), bf16),
        v((8, 128, 128), bf16),
        v((8, 128, 128), bf16),
        v((8, 128, 128), bf16),
        v((4, 256, HID), bf16),
        v((4, 256, GU), bf16),
        v((1032, 128), f32),
        v((4, 256, 384), bf16),
        v((8, 1024), f32),
        v((3, 4, 2, 128, 1024), bf16),
        v((3, 4, 128, 1024), bf16),
        v((3, 2, 64, 1024), bf16),
        v((3, 2, 128, 1024), bf16),
        v((4, 4, 64, FFL), bf16),
        v((4, 4, 64, 384), bf16),
        v((4, 4, 16, 128), bf16),
        v((4, 4, 64, 128), bf16),
        v((2, 2, 64, 896), bf16),
        v((4, 2, 64, 896), bf16),
        v((2, 2, 64, 896), bf16),
        v((4, 2, 64, 896), bf16),
        v((2, 32, 896), bf16),
        v((4, 32, 896), bf16),
        v((2, 32, 896), bf16),
        v((4, 32, 896), bf16),
        v((2, 3, 4, 32, 384), bf16),
        v((2, 3, 32, 384), bf16),
        v((3, 4, 16, 128), bf16),
        v((3, 16, 128), bf16),
        v((3, 4, 64, 128), bf16),
        v((3, 64, 128), bf16),
        v((8, 8, 512), f32),
        v((8, 8, 512), f32),
    ]
    raw = pl.pallas_call(
        block_kernel,
        out_shape=out_shape,
        in_specs=[anywhere] * 10,
        out_specs=(anywhere,) * 6,
        scratch_shapes=scratch,
        compiler_params=pltpu.CompilerParams(
            collective_id=0, has_side_effects=True, vmem_limit_bytes=62 * 1024 * 1024
        ),
    )(
        inputs,
        cotangent,
        mix_gain.reshape(1, 8),
        in_proj,
        conv_kernel,
        out_proj,
        ffn_gain.reshape(1, 8),
        gate_proj,
        up_proj,
        down_proj.T,
    )
    made = pl.pallas_call(
        spread_kernel,
        out_shape=(
            jax.ShapeDtypeStruct(inputs.shape, bf16),
            jax.ShapeDtypeStruct(inputs.shape, f32),
            jax.ShapeDtypeStruct((1, 8), f32),
            jax.ShapeDtypeStruct(in_proj.shape, f32),
            jax.ShapeDtypeStruct(conv_kernel.shape, f32),
            jax.ShapeDtypeStruct(out_proj.shape, f32),
            jax.ShapeDtypeStruct((1, 8), f32),
            jax.ShapeDtypeStruct(gate_proj.shape, f32),
            jax.ShapeDtypeStruct(up_proj.shape, f32),
            jax.ShapeDtypeStruct(down_proj.shape[::-1], f32),
        ),
        grid=(1,),
        compiler_params=pltpu.CompilerParams(vmem_limit_bytes=62 * 1024 * 1024),
    )(*raw)
    return (*made[:2], made[2].reshape(8), *made[3:6], made[6].reshape(8), *made[7:9], made[9].T)


def solution(mesh):
    in_specs = (
        P("fsdp", "ctx", None),
        P(("fsdp", "ctx")),
        P(("fsdp", "ctx"), None),
        P(None, ("fsdp", "ctx")),
        P(("fsdp", "ctx"), None),
        P(("fsdp", "ctx")),
        P("fsdp", "ctx"),
        P("fsdp", "ctx"),
        P("ctx", "fsdp"),
        P("fsdp", "ctx", None),
    )
    out_specs = (
        P("fsdp", "ctx", None),
        P("fsdp", "ctx", None),
        P(("fsdp", "ctx")),
        P(("fsdp", "ctx"), None),
        P(None, ("fsdp", "ctx")),
        P(("fsdp", "ctx"), None),
        P(("fsdp", "ctx")),
        P("fsdp", "ctx"),
        P("fsdp", "ctx"),
        P("ctx", "fsdp"),
    )
    return jax.shard_map(
        per_device, mesh=mesh, in_specs=in_specs, out_specs=out_specs, check_vma=False
    )
```
